32 devices in a mesh: shard: 2 (over x), context: 4 (over z), tensor: 4 (over y, core).
Axes of the slice: x: 2, y: 2, z: 4, core: 2. Of those that a mesh axis runs over, the one named last changes fastest.
Arguments:
- tokens: bfloat16 [10240, 1088], P(('shard', 'context', 'tensor')), may hold values from -6 to 6
- cotangent: bfloat16 [10240, 1088], P(('shard', 'context', 'tensor')), may hold values from -6 to 6
- segment_of: int32 [10240], P('shard'), may hold values from 0 to 51, as said below
- position_of: int32 [10240], P('shard'), may hold values from 0 to 1279, as said below
- parent: int32 [52], replicated, may hold values from -1 to 51, as said below
- ln1_gain: bfloat16 [1088], P('shard'), may hold values from 0.099609375 to 1.8984375
- ln1_bias: bfloat16 [1088], P('shard'), may hold values from -4 to 4
- w_qkv: bfloat16 [1088, 3264], P('shard'), may hold values from -0.25 to 0.25
- b_query: bfloat16 [1088], P('shard'), may hold values from -4 to 4
- b_value: bfloat16 [1088], P('shard'), may hold values from -4 to 4
- w_out: bfloat16 [1088, 1088], P('shard'), may hold values from -3 to 3
- b_out: bfloat16 [1088], P('shard'), may hold values from -4 to 4
- ln2_gain: bfloat16 [1088], P('shard'), may hold values from 0.099609375 to 1.8984375
- ln2_bias: bfloat16 [1088], P('shard'), may hold values from -4 to 4
- w_fc: bfloat16 [1088, 4352], P('shard', 'tensor'), may hold values from -0.1875 to 0.1875
- b_fc: bfloat16 [4352], P('tensor'), may hold values from -4 to 4
- w_proj: bfloat16 [4352, 1088], P('tensor', 'shard'), may hold values from -0.09375 to 0.09375
- b_proj: bfloat16 [1088], P('shard'), may hold values from -4 to 4
Outputs:
- out: bfloat16 [10240, 1088], P(('shard', 'context', 'tensor'))
- d_tokens: float32 [10240, 1088], P(('shard', 'context', 'tensor'))
- grad_ln1_gain: float32 [1088], P('shard')
- grad_ln1_bias: float32 [1088], P('shard')
- grad_w_qkv: float32 [1088, 3264], P('shard')
- grad_b_query: float32 [1088], P('shard')
- grad_b_value: float32 [1088], P('shard')
- grad_w_out: float32 [1088, 1088], P('shard')
- grad_b_out: float32 [1088], P('shard')
- grad_ln2_gain: float32 [1088], P('shard')
- grad_ln2_bias: float32 [1088], P('shard')
- grad_w_fc: float32 [1088, 4352], P('shard', 'tensor')
- grad_b_fc: float32 [4352], P('tensor')
- grad_w_proj: float32 [4352, 1088], P('tensor', 'shard')
- grad_b_proj: float32 [1088], P('shard')
The draws below stay inside these ranges and needn't reach their ends.
Inputs may be any that keep to these rules, and one draw needn't show every extreme that they name: Tree i holds rows i * 2560 to (i + 1) * 2560 - 1 and segments of its own: a trunk of 1024 tokens (parent -1), 4 branches whose parent is the trunk, and 2 leaves on each branch; branches and leaves have 128 tokens. Segment numbers are a permutation within each tree's block of 13 consecutive numbers, and the trunk has the block's last number. `segment_of`: A tree's rows are its 20 pieces of 128 aligned rows (the trunk's 8 pieces and one piece for every other segment) in any order. `position_of`: trunk tokens have positions 0 to 1023, a branch's continue from 1024, a leaf's from (9) * 128; within a piece positions rise by one.
All inputs are finite; a program needn't handle non-finite values.
Results may differ from the reference program's by a relative error of at most 0.012.
The reference program's roundings to bfloat16 on the way count: a program that leaves them out, or rounds other values in their place, can miss the bound.
Values may be sent and summed in bfloat16 or wider, within the bound.
A program may use at most 192 MiB of HBM per device.

```python
import jax
import jax.numpy as jnp
from jax import lax

D = 1088
HEADS = 17
HEAD_DIM = 64
FF = 4352
SEG = 128
TRUNK_SEGS = 8
BRANCHES = 4
LEAVES = 2
TREE_SEGS = 13
PIECES = 20
TREE = 2560
TREES = 4
TOKENS = 10240


def tree_layout(key):
    base_key = jax.random.fold_in(key, 11)
    tree_keys = jax.random.split(base_key, TREES)
    leaf_count = BRANCHES * LEAVES

    def one_tree(tree_key, tree_id):
        relabel_key, branch_key, order_key = jax.random.split(tree_key, 3)
        others = jax.random.permutation(relabel_key, TREE_SEGS - 1).astype(jnp.int32)
        relabel = jnp.concatenate([jnp.full((1,), TREE_SEGS - 1, jnp.int32), others])
        leaf_branch = (jax.random.permutation(branch_key, leaf_count) // LEAVES).astype(jnp.int32)
        placing = jax.random.permutation(order_key, PIECES).astype(jnp.int32)
        local_parent = jnp.concatenate([jnp.full((1,), -1, jnp.int32), jnp.zeros((BRANCHES,), jnp.int32), 1 + leaf_branch])
        base_id = tree_id * TREE_SEGS
        parent_ids = jnp.where(local_parent < 0, -1, base_id + relabel[jnp.maximum(local_parent, 0)])
        parent_table = jnp.zeros((TREE_SEGS,), jnp.int32).at[relabel].set(parent_ids)
        piece_local = jnp.concatenate([jnp.zeros((TRUNK_SEGS,), jnp.int32), 1 + jnp.arange(BRANCHES, dtype=jnp.int32), 1 + BRANCHES + jnp.arange(leaf_count, dtype=jnp.int32)])
        piece_first = jnp.concatenate([jnp.arange(TRUNK_SEGS, dtype=jnp.int32) * SEG, jnp.full((BRANCHES,), TRUNK_SEGS * SEG, jnp.int32), jnp.full((leaf_count,), (TRUNK_SEGS + 1) * SEG, jnp.int32)])
        slot_segment = base_id + relabel[piece_local[placing]]
        slot_first = piece_first[placing]
        segments = jnp.repeat(slot_segment, SEG)
        places = (slot_first[:, None] + jnp.arange(SEG, dtype=jnp.int32)[None, :]).reshape(-1)
        return (parent_table, segments, places)
    tables, segments, places = jax.vmap(one_tree)(tree_keys, jnp.arange(TREES, dtype=jnp.int32))
    return (tables.reshape(-1), segments.reshape(-1), places.reshape(-1))


def draw_parent(key, part):
    return tree_layout(key)[0]


def draw_segment_of(key, part):
    return tree_layout(key)[1]


def draw_position_of(key, part):
    return tree_layout(key)[2]


def shard_levels(rng, dims, pieces, smallest, high):
    factor_of, own = 1.0, jax.random.fold_in(rng, 6)
    for position, shards_of in pieces:
        steps = jnp.exp(jax.random.uniform(jax.random.fold_in(own, position), (shards_of,), jnp.float32, smallest / len(pieces), high / len(pieces)))
        factor_of = factor_of * jnp.repeat(steps, dims[position] // shards_of).reshape([-1 if axis == position else 1 for axis in range(len(dims))])
    return factor_of


def noise(own_key, extent, scale, bound, shards=(), held_as=jnp.bfloat16):
    level = shard_levels(own_key, extent, shards, -0.22, 0.18) if shards else 1.0
    array = jax.random.normal(own_key, extent, jnp.float32) * scale * level
    return jnp.minimum(jnp.maximum(array, -bound), bound).astype(held_as)


def setup_inputs(seed: int = 0) -> dict:
    key_of = jax.random.split(jax.random.key(seed), 19)
    return {
        "tokens": noise(key_of[0], (TOKENS, D), 1.0, 6.0, ((0, 32),)),
        "cotangent": noise(key_of[1], (TOKENS, D), 1.0, 6.0, ((0, 32),)),
        "segment_of": draw_segment_of(jax.random.fold_in(key_of[18], 71), 0),
        "position_of": draw_position_of(jax.random.fold_in(key_of[18], 71), 0),
        "parent": draw_parent(jax.random.fold_in(key_of[18], 71), 0),
        "ln1_gain": jnp.clip(1.0 + 0.18 * jax.random.normal(key_of[5], (D,), jnp.float32), 0.099609375, 1.8984375).astype(jnp.bfloat16),
        "ln1_bias": noise(key_of[6], (D,), 0.3, 4.0, ((0, 2),)),
        "w_qkv": noise(key_of[7], (D, 3 * D), (D // 2) ** -0.5, 0.25, ((0, 2),)),
        "b_query": noise(key_of[8], (D,), 0.3, 4.0, ((0, 2),)),
        "b_value": noise(key_of[9], (D,), 0.3, 4.0, ((0, 2),)),
        "w_out": noise(key_of[10], (D, D), (max(1, D // (2 * SEG))) ** -0.5, 3.0, ((0, 2),)),
        "b_out": noise(key_of[11], (D,), 0.3, 4.0, ((0, 2),)),
        "ln2_gain": jnp.clip(1.0 + 0.18 * jax.random.normal(key_of[12], (D,), jnp.float32), 0.099609375, 1.8984375).astype(jnp.bfloat16),
        "ln2_bias": noise(key_of[13], (D,), 0.3, 4.0, ((0, 2),)),
        "w_fc": noise(key_of[14], (D, FF), D ** -0.5, 0.1875, ((0, 2), (1, 4))),
        "b_fc": noise(key_of[15], (FF,), 0.3, 4.0, ((0, 4),)),
        "w_proj": noise(key_of[16], (FF, D), FF ** -0.5, 0.09375, ((0, 4), (1, 2))),
        "b_proj": noise(key_of[17], (D,), 0.3, 4.0, ((0, 2),)),
    }


@jax.custom_vjp
def low(v):
    return lax.optimization_barrier(v.astype(jnp.bfloat16)).astype(jnp.float32)

@jax.custom_vjp
def low_back(v):
    return v

def low_keep(v):
    return (low(v), None)

def low_pass(kept, grad):
    return (grad,)

def back_keep(v):
    return (v, None)

def back_low(kept, grad):
    return (low(grad),)
low.defvjp(low_keep, low_pass)
low_back.defvjp(back_keep, back_low)
NEGATIVE = -1e+30
EPSILON = 1e-05

def product(left, right):
    return jnp.dot(left, right, precision=lax.Precision.HIGHEST, preferred_element_type=jnp.float32)

def layer_norm(inputs, gain, shift):
    average = lax.optimization_barrier(jnp.mean(inputs, axis=-1, keepdims=True))
    centered = inputs - average
    spread = lax.optimization_barrier(jnp.mean(centered * centered, axis=-1, keepdims=True))
    return centered * lax.rsqrt(spread + EPSILON) * gain + shift

def tree_layer(inputs, params, allowed):
    ln1_gain, ln1_bias, w_qkv, b_query, b_value, w_out, b_out, ln2_gain, ln2_bias, w_fc, b_fc, w_proj, b_proj = params
    row_count = inputs.shape[0]
    score_scale = HEAD_DIM ** (-0.5)
    normed = low(layer_norm(inputs, ln1_gain, ln1_bias))
    mixed = product(normed, w_qkv)
    query = low(low_back((mixed[:, :D] + b_query) * score_scale))
    keys = low(low_back(mixed[:, D:2 * D]))
    values = low(low_back(mixed[:, 2 * D:] + b_value))
    query_heads = query.reshape(row_count, HEADS, HEAD_DIM).transpose(1, 0, 2)
    key_heads = keys.reshape(row_count, HEADS, HEAD_DIM).transpose(1, 0, 2)
    value_heads = values.reshape(row_count, HEADS, HEAD_DIM).transpose(1, 0, 2)

    def one_head(operands):
        head_query, head_keys, head_values = operands
        scores = low_back(product(head_query, head_keys.T))
        scores = jnp.where(allowed, scores, NEGATIVE)
        largest = lax.optimization_barrier(jnp.max(scores, axis=1, keepdims=True))
        raised = jnp.exp(scores - largest)
        probs = raised / lax.optimization_barrier(jnp.sum(raised, axis=1, keepdims=True))
        return product(low(probs), head_values)
    attended = lax.map(jax.checkpoint(one_head), (query_heads, key_heads, value_heads))
    attended = low(low_back(attended.transpose(1, 0, 2).reshape(row_count, D)))
    middle = inputs + low_back(product(attended, w_out) + b_out)
    normed_two = low(layer_norm(middle, ln2_gain, ln2_bias))
    before = low_back(product(normed_two, w_fc) + b_fc)
    hidden = low(jax.nn.gelu(before, approximate=False))
    return middle + product(hidden, w_proj) + b_proj

def ancestor(table, identities):
    return jnp.where(identities >= 0, table[jnp.maximum(identities, 0)], -1)

def reference(tokens, cotangent, segment_of, position_of, parent, ln1_gain, ln1_bias, w_qkv, b_query, b_value, w_out, b_out, ln2_gain, ln2_bias, w_fc, b_fc, w_proj, b_proj):
    params = tuple((item.astype(jnp.float32) for item in (ln1_gain, ln1_bias, w_qkv, b_query, b_value, w_out, b_out, ln2_gain, ln2_bias, w_fc, b_fc, w_proj, b_proj)))
    inputs_all = tokens.astype(jnp.float32).reshape(TREES, TREE, D)
    pulled_all = cotangent.astype(jnp.float32).reshape(TREES, TREE, D)
    segments_all = segment_of.reshape(TREES, TREE)
    places_all = position_of.reshape(TREES, TREE)

    def one_tree(totals, operands):
        inputs, pulled, segments, places = operands
        first_up = ancestor(parent, segments)
        second_up = ancestor(parent, first_up)
        related = (segments[None, :] == segments[:, None]) | (segments[None, :] == first_up[:, None]) | (segments[None, :] == second_up[:, None])
        allowed = related & (places[None, :] <= places[:, None])
        result, pullback = jax.vjp(lambda rows_in, weights_in: tree_layer(rows_in, weights_in, allowed), inputs, params)
        d_inputs, d_params = pullback(pulled)
        totals = jax.tree.map(lambda left, right: left + right, totals, d_params)
        return (totals, (result.astype(jnp.bfloat16), d_inputs))
    zero_grads = jax.tree.map(jnp.zeros_like, params)
    totals, (outputs, d_inputs_all) = lax.scan(one_tree, zero_grads, (inputs_all, pulled_all, segments_all, places_all))
    g_ln1_gain, g_ln1_bias, g_w_qkv, g_b_query, g_b_value, g_w_out, g_b_out, g_ln2_gain, g_ln2_bias, g_w_fc, g_b_fc, g_w_proj, g_b_proj = totals
    return (outputs.reshape(TOKENS, D), d_inputs_all.reshape(TOKENS, D), g_ln1_gain, g_ln1_bias, g_w_qkv, g_b_query, g_b_value, g_w_out, g_b_out, g_ln2_gain, g_ln2_bias, g_w_fc, g_b_fc, g_w_proj, g_b_proj)
```

```python
import functools

import jax
import jax.numpy as jnp
from jax import lax
from jax.experimental import pallas as pl
from jax.experimental.pallas import tpu as pltpu
from jax.sharding import PartitionSpec as P

HEAD_DIM = 64
PAIR = 2 * HEAD_DIM
PIECE = 128
TRUNK = 8 * PIECE
BRANCH = 3 * PIECE
EPSILON = 1e-05
NEGATIVE = -1e30
F32 = jnp.float32
BF16 = jnp.bfloat16
VMEM = pl.BlockSpec(memory_space=pltpu.VMEM)
SMEM = pl.BlockSpec(memory_space=pltpu.SMEM)
ANY = pl.BlockSpec(memory_space=pl.ANY)
MESH = pl.DeviceIdType.MESH


def contract(left, right, left_dim, right_dim):
    return lax.dot_general(
        left, right, (((left_dim,), (right_dim,)), ((), ())), preferred_element_type=F32
    )


def layer_norm(inputs, gain, shift):
    average = jnp.mean(inputs, axis=-1, keepdims=True)
    centered = inputs - average
    spread = jnp.mean(centered * centered, axis=-1, keepdims=True)
    return centered * lax.rsqrt(spread + EPSILON) * gain + shift


def gelu_exact(inputs):
    return jax.nn.gelu(inputs, approximate=False)


def flip(value, bit):
    low = 1 << bit
    return value + low - 2 * low * lax.rem(lax.div(value, low), 2)


def place():
    tensor, context = lax.axis_index("tensor"), lax.axis_index("context")
    return tensor, context, lax.rem(context, 2) * lax.axis_size("tensor") + tensor


def member(mask):
    tensor, context, _ = place()
    size = lax.axis_size("tensor")
    bits = size.bit_length() - 1
    for bit in range(bits):
        if mask >> bit & 1:
            tensor = flip(tensor, bit)
    if mask >> bits & 1:
        context = flip(context, 0)
    return {"context": context, "tensor": tensor}, lax.rem(context, 2) * size + tensor


def greet(masks):
    barrier = pltpu.get_barrier_semaphore()
    for mask in masks:
        pl.semaphore_signal(barrier, inc=1, device_id=member(mask)[0], device_id_type=MESH)
    pl.semaphore_wait(barrier, len(masks))


def swap(value, axis, bit):
    size = lax.axis_size(axis)
    return lax.ppermute(value, axis, [(i, i ^ 1 << bit) for i in range(size)])


def group_gather_kernel(masks, natural, x, out, own_sem, send, recv):
    rows = x.shape[0]
    far = [m for m in masks if m & 1 == 0]
    greet(far + [1])

    def copy(source, target, owner):
        seen = owner ^ target
        index = member(owner)[1] if natural else seen
        return pltpu.make_async_remote_copy(
            src_ref=source,
            dst_ref=out.at[pl.ds(pl.multiple_of(index * rows, rows), rows)],
            send_sem=send.at[seen],
            recv_sem=recv.at[seen],
            device_id=member(target)[0],
            device_id_type=MESH,
        )

    def held(owner):
        index = member(owner)[1] if natural else owner
        return out.at[pl.ds(pl.multiple_of(index * rows, rows), rows)]

    first = [copy(x, m, 0) for m in far]
    for c in first:
        c.start()
    near = copy(x, 1, 0)
    near.start()
    own = pltpu.make_async_copy(x, held(0), own_sem)
    own.start()
    passed = []
    for m, c in zip(far, first):
        c.wait_recv()
        on = copy(held(m), 1, m)
        on.start()
        passed.append(on)
    own.wait()
    near.wait_recv()
    for on in passed:
        on.wait_recv()
    for c in first + [near] + passed:
        c.wait_send()


def semaphores(size):
    return [
        pltpu.SemaphoreType.DMA,
        pltpu.SemaphoreType.DMA((size,)),
        pltpu.SemaphoreType.DMA((size,)),
    ]


def group_gather(x, whole_tree, natural, collective_id, name):
    size = lax.axis_size("tensor") * (2 if whole_tree else 1)
    return pl.pallas_call(
        functools.partial(group_gather_kernel, list(range(1, size)), natural),
        in_specs=[ANY],
        out_specs=ANY,
        out_shape=jax.ShapeDtypeStruct((size * x.shape[0], x.shape[1]), x.dtype),
        scratch_shapes=semaphores(size),
        compiler_params=pltpu.CompilerParams(collective_id=collective_id, has_side_effects=True),
        name=name,
    )(x)


def exchange_kernel(masks, to_rows, x, out, own_sem, send, recv):
    greet(masks)
    tall, wide = (x, out) if to_rows else (out, x)
    rows, columns = wide.shape[0], tall.shape[1]

    def below(ref, index):
        return ref.at[pl.ds(pl.multiple_of(index * rows, rows), rows), :]

    def beside(ref, index):
        return ref.at[:, pl.ds(pl.multiple_of(index * columns, columns), columns)]

    source, target = (below, beside) if to_rows else (beside, below)
    me = member(0)[1]
    copies = []
    for mask in masks:
        device, index = member(mask)
        copies.append(
            pltpu.make_async_remote_copy(
                src_ref=source(x, index),
                dst_ref=target(out, me),
                send_sem=send.at[mask],
                recv_sem=recv.at[mask],
                device_id=device,
                device_id_type=MESH,
            )
        )
        copies[-1].start()
    own = pltpu.make_async_copy(source(x, me), target(out, me), own_sem)
    own.start()
    own.wait()
    for copy in copies:
        copy.wait_recv()
    for copy in copies:
        copy.wait_send()


def exchange(x, to_rows, collective_id, name):
    size = 2 * lax.axis_size("tensor")
    rows, columns = x.shape
    shape = (rows // size, columns * size) if to_rows else (rows * size, columns // size)
    return pl.pallas_call(
        functools.partial(exchange_kernel, list(range(1, size)), to_rows),
        in_specs=[ANY],
        out_specs=ANY,
        out_shape=jax.ShapeDtypeStruct(shape, x.dtype),
        scratch_shapes=semaphores(size),
        compiler_params=pltpu.CompilerParams(collective_id=collective_id, has_side_effects=True),
        name=name,
    )(x)


def sum_scatter_kernel(x, out, near, far, send, recv):
    rows = out.shape[0]
    greet([1, 2])

    def block(mask):
        return x.at[mask * rows : (mask + 1) * rows, :]

    def copy(source, target, mask, index):
        return pltpu.make_async_remote_copy(
            src_ref=source,
            dst_ref=target,
            send_sem=send.at[index],
            recv_sem=recv.at[index],
            device_id=member(mask)[0],
            device_id_type=MESH,
        )

    onward = copy(block(3), near.at[1], 1, 0)
    onward.start()
    mine = copy(block(1), near.at[0], 1, 1)
    mine.start()
    onward.wait_recv()
    far[0] = (block(2)[...].astype(F32) + near[1].astype(F32)).astype(BF16)
    across = copy(far.at[0], far.at[1], 2, 2)
    across.start()
    mine.wait_recv()
    out[...] = block(0)[...].astype(F32) + near[0].astype(F32)
    across.wait_recv()
    out[...] += far[1].astype(F32)
    for c in (onward, mine, across):
        c.wait_send()


def sum_scatter(x, collective_id, name):
    rows, columns = x.shape[0] // lax.axis_size("tensor"), x.shape[1]
    return pl.pallas_call(
        sum_scatter_kernel,
        in_specs=[VMEM],
        out_specs=VMEM,
        out_shape=jax.ShapeDtypeStruct((rows, columns), F32),
        scratch_shapes=[
            pltpu.VMEM((2, rows, columns), BF16),
            pltpu.VMEM((2, rows, columns), BF16),
            pltpu.SemaphoreType.DMA((3,)),
            pltpu.SemaphoreType.DMA((3,)),
        ],
        compiler_params=pltpu.CompilerParams(
            collective_id=collective_id, has_side_effects=True, vmem_limit_bytes=24 << 20
        ),
        name=name,
    )(x)


def tri(n):
    r=lax.broadcasted_iota(jnp.int32,(n,n),0); c=lax.broadcasted_iota(jnp.int32,(n,n),1)
    return c<=r

def branch_mask():
    r=lax.broadcasted_iota(jnp.int32,(BRANCH,BRANCH),0); c=lax.broadcasted_iota(jnp.int32,(BRANCH,BRANCH),1)
    return (c<=r)&((c<PIECE)|(c//PIECE==r//PIECE))

def split_heads(x):
    lane=lax.broadcasted_iota(jnp.int32,(1,2*64),1)<64
    z=jnp.zeros_like(x)
    return jnp.concatenate([jnp.where(lane,x,z),jnp.where(lane,z,x)],axis=0)

def join_heads(x):
    n=x.shape[0]//2
    lane=lax.broadcasted_iota(jnp.int32,(1,2*64),1)<64
    return jnp.where(lane,x[:n],x[n:])

def fwd_kernel(order, qkv, q16, qinfo, kinfo, att, att16, canon, of, lse, of16, lse16):
    n_p=qkv.shape[0]//PIECE
    for i in range(n_p):
        src=pl.ds(pl.multiple_of(order[i]*PIECE,PIECE),PIECE)
        canon[i*PIECE:(i+1)*PIECE,:]=qkv[src,0:384]
    def rows(start,size,parts):
        qh=split_heads(canon[pl.ds(start,size),0:128])
        ss=[]
        for ks,kn,mask in parts:
            s=contract(qh,canon[pl.ds(ks,kn),128:256],1,1)
            if mask is not None:
                m2=jnp.concatenate([mask,mask],axis=0)
                s=jnp.where(m2,s,NEGATIVE)
            ss.append(s)
        top=functools.reduce(jnp.maximum,[jnp.max(s,axis=1,keepdims=True) for s in ss])
        tot=0.; o=0.
        for (ks,kn,_),s in zip(parts,ss):
            e=jnp.exp(s-top)
            tot=tot+jnp.sum(e,axis=1,keepdims=True)
            o=o+contract(e.astype(BF16),canon[pl.ds(ks,kn),256:384],1,0)
        o=join_heads(o*(1.0/tot))
        of[pl.ds(start,size),:]=o
        l=top+jnp.log(tot)
        lse[pl.ds(start,size),:]=join_heads(jnp.broadcast_to(l,(2*size,128)))
    t=tri(256)
    for b in range(4):
        parts=[(b*256,256,t)]
        if b: parts.insert(0,(0,b*256,None))
        rows(b*256,256,parts)
    bm=branch_mask()
    def branch(b,_):
        st=pl.multiple_of(TRUNK+b*BRANCH,PIECE)
        rows(st,BRANCH,[(0,TRUNK,None),(st,BRANCH,bm)])
        return 0
    lax.fori_loop(0,4,branch,0)
    for i in range(n_p):
        dst=pl.ds(pl.multiple_of(order[i]*PIECE,PIECE),PIECE)
        att[dst,:]=of[i*PIECE:(i+1)*PIECE,:].astype(BF16)
    s=contract(q16[...],qkv[:,384:512],1,1)
    s=jnp.where(allowed_mask(qinfo,kinfo),s,NEGATIVE)
    top=jnp.max(s,axis=1,keepdims=True)
    e=jnp.exp(s-top)
    tot=jnp.sum(e,axis=1,keepdims=True)
    o=contract(e.astype(BF16),qkv[:,384:512],1,0)*(1.0/tot)
    of16[...]=o
    att16[...]=o.astype(BF16)
    lse16[...]=jnp.broadcast_to(top+jnp.log(tot),o.shape)

def allowed_mask(qinfo,kinfo):
    ks=kinfo[0:1,:]; kp=kinfo[1:2,:]
    return ((ks==qinfo[:,0:1])|(ks==qinfo[:,1:2])|(ks==qinfo[:,2:3]))&(kp<=qinfo[:,3:4])

def attention_forward(order,qkv,q16,qinfo,kinfo):
    n=qkv.shape[0]; r=q16.shape[0]
    sd=jax.ShapeDtypeStruct
    V=pl.BlockSpec(memory_space=pltpu.VMEM)
    return pl.pallas_call(fwd_kernel,
        in_specs=[pl.BlockSpec(memory_space=pltpu.SMEM)]+[V]*4,
        out_specs=[V]*7,
        out_shape=[sd((n,128),BF16),sd((r,128),BF16),sd((n,384),BF16),sd((n,128),F32),sd((n,128),F32),sd((r,128),F32),sd((r,128),F32)],
        compiler_params=pltpu.CompilerParams(vmem_limit_bytes=50<<20),
        cost_estimate=pl.CostEstimate(flops=20_000_000_000,bytes_accessed=8_000_000,transcendentals=7_000_000),
        name="tree_attention_forward",
    )(order,qkv,q16,qinfo,kinfo)

def bwd_kernel(order, canon, of, lse, datt, kv16, q16, of16, lse16, datt16, qinfo, kinfo, dqkv, dq16, dc, dacc):
    n_p=canon.shape[0]//PIECE
    for i in range(n_p):
        src=pl.ds(pl.multiple_of(order[i]*PIECE,PIECE),PIECE)
        dc[i*PIECE:(i+1)*PIECE,:]=datt[src,:]
    def rows(start,size,parts):
        r=pl.ds(start,size)
        qh=split_heads(canon[r,0:128])
        d=dc[r,:]
        dh=split_heads(d)
        prod=d.astype(F32)*of[r,:]
        delta=jnp.concatenate([jnp.sum(prod[:,0:64],axis=1,keepdims=True),jnp.sum(prod[:,64:128],axis=1,keepdims=True)],axis=0)
        l=jnp.concatenate([lse[r,0:1],lse[r,64:65]],axis=0)
        dq=0.
        for ks,kn,mask,first in parts:
            kk=canon[pl.ds(ks,kn),128:256]
            s=contract(qh,kk,1,1)
            if mask is not None:
                s=jnp.where(jnp.concatenate([mask,mask],axis=0),s,NEGATIVE)
            p=jnp.exp(s-l)
            dp=contract(dh,canon[pl.ds(ks,kn),256:384],1,1)
            ds=(p*(dp-delta)).astype(BF16)
            dv=contract(p.astype(BF16),dh,0,0)
            dk=contract(ds,qh,0,0)
            dq=dq+contract(ds,kk,1,0)
            if first:
                dacc[pl.ds(ks,kn),128:256]=dk
                dacc[pl.ds(ks,kn),256:384]=dv
            else:
                dacc[pl.ds(ks,kn),128:256]+=dk
                dacc[pl.ds(ks,kn),256:384]+=dv
        dacc[r,0:128]=join_heads(dq)
    t=tri(256)
    for b in range(4):
        parts=[(b*256,256,t,True)]
        if b: parts.insert(0,(0,b*256,None,False))
        rows(b*256,256,parts)
    bm=branch_mask()
    def branch(b,_):
        st=pl.multiple_of(TRUNK+b*BRANCH,PIECE)
        rows(st,BRANCH,[(0,TRUNK,None,False),(st,BRANCH,bm,True)])
        return 0
    lax.fori_loop(0,4,branch,0)
    for i in range(n_p):
        dst=pl.ds(pl.multiple_of(order[i]*PIECE,PIECE),PIECE)
        x=dacc[i*PIECE:(i+1)*PIECE,:]
        dqkv[dst,0:128]=(x[:,0:128]*0.125).astype(BF16)
        dqkv[dst,128:384]=x[:,128:384].astype(BF16)
    k16=kv16[:,384:512]
    s=contract(q16[...],k16,1,1)
    s=jnp.where(allowed_mask(qinfo,kinfo),s,NEGATIVE)
    p=jnp.exp(s-lse16[:,0:1])
    dp=contract(datt16[...],k16,1,1)
    delta=jnp.sum(datt16[...].astype(F32)*of16[...],axis=1,keepdims=True)
    ds=(p*(dp-delta)).astype(BF16)
    dqkv[:,384:512]=(contract(ds,q16[...],0,0)+contract(p.astype(BF16),datt16[...],0,0)).astype(BF16)
    dq16[...]=(contract(ds,k16,1,0)*0.125).astype(BF16)

def attention_backward(order,canon,of,lse,datt,qkv,q16,of16,lse16,datt16,qinfo,kinfo):
    n=canon.shape[0]; r=q16.shape[0]
    sd=jax.ShapeDtypeStruct
    V=pl.BlockSpec(memory_space=pltpu.VMEM)
    return pl.pallas_call(bwd_kernel,
        in_specs=[pl.BlockSpec(memory_space=pltpu.SMEM)]+[V]*11,
        out_specs=[V]*2,
        out_shape=[sd((n,512),BF16),sd((r,128),BF16)],
        scratch_shapes=[pltpu.VMEM((n,128),BF16),pltpu.VMEM((n,384),F32)],
        compiler_params=pltpu.CompilerParams(vmem_limit_bytes=60<<20),
        cost_estimate=pl.CostEstimate(flops=50_000_000_000,bytes_accessed=15_000_000,transcendentals=7_000_000),
        name="tree_attention_backward",
    )(order,canon,of,lse,datt,qkv,q16,of16,lse16,datt16,qinfo,kinfo)


def parent_lookup(identities, shifted_table):
    labels = jnp.arange(shifted_table.shape[0], dtype=jnp.int32)
    matches = identities[:, None] == labels[None, :]
    return jnp.sum(jnp.where(matches, shifted_table[None, :], 0), axis=1) - 1


def tree_order(segments, places, parent):
    own = segments.reshape(-1, PIECE)[:, 0]
    start = places.reshape(-1, PIECE)[:, 0]
    table = parent + 1
    first_up = parent_lookup(own, table)
    second_up = parent_lookup(first_up, table)
    is_branch = (first_up >= 0) & (second_up < 0)
    is_leaf = second_up >= 0
    branch = jnp.where(is_leaf, first_up, own)
    rank = jnp.sum((is_branch[None, :] & (own[None, :] < branch[:, None])).astype(jnp.int32), axis=1)
    twin = is_leaf[None, :] & (first_up[None, :] == first_up[:, None]) & (own[None, :] < own[:, None])
    leaf = 1 + jnp.sum(twin.astype(jnp.int32), axis=1)
    target = jnp.where(
        first_up < 0, start // PIECE, TRUNK // PIECE + 3 * rank + jnp.where(is_leaf, leaf, 0)
    )
    pieces = jnp.arange(own.shape[0], dtype=jnp.int32)
    order = jnp.sum(jnp.where(target[None, :] == pieces[:, None], pieces[None, :], 0), axis=1)
    return order, first_up, second_up


def local(
    tokens,
    cotangent,
    segment_of,
    position_of,
    parent,
    ln1_gain,
    ln1_bias,
    w_qkv,
    b_query,
    b_value,
    w_out,
    b_out,
    ln2_gain,
    ln2_bias,
    w_fc,
    b_fc,
    w_proj,
    b_proj,
):
    rows, width = tokens.shape
    half = w_qkv.shape[0]
    shard = lax.axis_index("shard")
    tensor, context, me = place()
    members = 2 * lax.axis_size("tensor")
    tree_rows = members * rows
    low = shard == 0
    shared = width - HEAD_DIM
    scale = HEAD_DIM ** (-0.5)

    def both(mine, other, axis=0):
        return jnp.concatenate([jnp.where(low, mine, other), jnp.where(low, other, mine)], axis=axis)

    vectors = jnp.stack(
        [ln1_gain, ln1_bias, b_query, b_value, b_out, ln2_gain, ln2_bias, b_proj]
    )
    vectors = both(vectors, swap(vectors, "shard", 0), 1).astype(F32)
    gain_one, shift_one, bias_query, bias_value, bias_out, gain_two, shift_two, bias_proj = vectors

    def pair_columns(array, axis):
        return lax.dynamic_slice_in_dim(array, me * PAIR, PAIR, axis)

    mixer = jnp.concatenate(
        [pair_columns(w_qkv[:, i * width : (i + 1) * width], 1) for i in range(3)]
        + [w_qkv[:, i * width + shared : (i + 1) * width] for i in (1, 2, 0)],
        axis=1,
    )
    mixer = both(mixer, swap(mixer, "shard", 0))
    everyone = group_gather(tokens, True, True, 0, "gather_tokens")
    out_other = swap(w_out, "shard", 0)
    out_weight = both(w_out, out_other)
    fc_weight = both(w_fc, swap(w_fc, "shard", 0))
    proj_other = swap(w_proj, "shard", 0)
    proj_weight = both(w_proj, proj_other, 1)
    quarter = half // 2
    near = lax.rem(tensor, 2)
    mixer_part = lax.dynamic_slice_in_dim(w_qkv, near * quarter, quarter, 0)
    mixer_part, _ = lax.optimization_barrier((mixer_part, proj_other))
    mixer_part = swap(mixer_part, "shard", 0)
    mixer_rest = swap(mixer_part, "tensor", 0)
    mixer_other = jnp.concatenate(
        [
            jnp.where(near == 0, mixer_part, mixer_rest),
            jnp.where(near == 0, mixer_rest, mixer_part),
        ],
        axis=0,
    )

    tree_start = lax.div(context, 2) * tree_rows
    segments = lax.dynamic_slice_in_dim(segment_of, tree_start, tree_rows)
    places = lax.dynamic_slice_in_dim(position_of, tree_start, tree_rows)
    order, first_up, second_up = tree_order(segments, places, parent)
    key_info = jnp.stack([segments, places])
    query_info = jnp.stack(
        [segments, jnp.repeat(first_up, PIECE), jnp.repeat(second_up, PIECE), places], axis=1
    )
    query_info = lax.dynamic_slice_in_dim(query_info, me * rows, rows, 0)

    normed_all = layer_norm(everyone.astype(F32), gain_one, shift_one).astype(BF16)
    inputs = tokens.astype(F32)
    normed_f, norm_one_pull = jax.vjp(layer_norm, inputs, gain_one, shift_one)
    normed = normed_f.astype(BF16)
    zero = jnp.zeros((PAIR,), F32)
    mixed_bias = jnp.concatenate(
        [pair_columns(bias_query, 0), zero, pair_columns(bias_value, 0), zero[:HEAD_DIM], bias_value[shared:]]
    )
    mixed_scale = jnp.concatenate([jnp.full((PAIR,), scale, F32), jnp.ones((3 * PAIR,), F32)])
    mixed = (
        (jnp.dot(normed_all, mixer[:, : 4 * PAIR], preferred_element_type=F32) + mixed_bias) * mixed_scale
    ).astype(BF16)
    query_last = (
        (jnp.dot(normed, mixer[:, 4 * PAIR :], preferred_element_type=F32) + bias_query[shared:]) * scale
    ).astype(BF16)
    query_last = jnp.pad(query_last, ((0, 0), (0, HEAD_DIM)))
    attended_pair, attended_last, sorted_qkv, exact, level, exact_last, level_last = attention_forward(
        order, mixed, query_last, query_info, key_info
    )
    attended = jnp.concatenate(
        [exchange(attended_pair, True, 1, "attended_to_rows"), attended_last[:, HEAD_DIM:]], axis=1
    )
    middle = inputs + jnp.dot(attended, out_weight, preferred_element_type=F32) + bias_out

    normed_two_f, norm_two_pull = jax.vjp(layer_norm, middle, gain_two, shift_two)
    group_rows = group_gather(normed_two_f.astype(BF16), False, False, 2, "gather_normed")
    grads = [cotangent]
    for mask in range(1, lax.axis_size("tensor")):
        grads.append(
            lax.ppermute(cotangent, "tensor", [(i, i ^ mask) for i in range(lax.axis_size("tensor"))])
        )
    group_grads = jnp.concatenate(grads, axis=0)
    before = jnp.dot(group_rows, fc_weight, preferred_element_type=F32) + b_fc.astype(F32)
    hidden_f, gelu_pull = jax.vjp(gelu_exact, before)
    hidden = hidden_f.astype(BF16)
    d_hidden = contract(group_grads, proj_weight, 1, 1)
    d_before = gelu_pull(d_hidden)[0].astype(BF16)
    d_normed_two = sum_scatter(contract(d_before, fc_weight, 1, 1).astype(BF16), 3, "sum_d_normed")
    mlp_out = sum_scatter(
        jnp.dot(hidden, proj_weight, preferred_element_type=F32).astype(BF16), 4, "sum_mlp"
    )
    output = (middle + mlp_out + bias_proj).astype(BF16)
    grad_proj = contract(group_grads, hidden, 0, 0)
    grad_fc = contract(group_rows, d_before, 0, 0)
    grad_bias_fc = jnp.sum(d_before, axis=0, dtype=F32)

    def halves(array, axis=0):
        first, second = jnp.split(array, 2, axis)
        return jnp.where(low, first, second), jnp.where(low, second, first)

    def low_half(array, is_low, axis=0):
        first, second = jnp.split(array, 2, axis)
        return jnp.where(is_low, first, second), jnp.where(is_low, second, first)

    keep_fc, give_fc = halves(grad_fc)
    keep_proj, give_proj = halves(grad_proj)
    got = swap(jnp.stack([give_fc, give_proj]).astype(BF16), "shard", 0).astype(F32)
    partial = jnp.stack([keep_fc + got[0], keep_proj + got[1]])
    contexts = lax.axis_size("context")
    chunk = half // 4
    low_bits = lax.rem(context, 4)

    def context_swap(value, mask):
        return lax.ppermute(value, "context", [(i, i ^ mask) for i in range(contexts)])

    def relative(mask):
        index = low_bits
        for bit in range(2):
            if mask >> bit & 1:
                index = flip(index, bit)
        return index * chunk

    total = lax.dynamic_slice_in_dim(partial, relative(0), chunk, 1)
    for mask in range(1, 4):
        part = lax.dynamic_slice_in_dim(partial, relative(mask), chunk, 1).astype(BF16)
        total = total + context_swap(part, mask).astype(F32)
    mask = 4
    while mask < contexts:
        total = total + context_swap(total.astype(BF16), mask).astype(F32)
        mask *= 2
    total = total.astype(BF16)
    whole = jnp.zeros((2, half, grad_fc.shape[1]), F32)
    whole = lax.dynamic_update_slice_in_dim(whole, total.astype(F32), relative(0), 1)
    for mask in range(1, 4):
        whole = lax.dynamic_update_slice_in_dim(
            whole, context_swap(total, mask).astype(F32), relative(mask), 1
        )
    own_fc, own_proj = whole[0], whole[1].T

    d_middle, grad_gain_two, grad_shift_two = norm_two_pull(d_normed_two)
    d_middle = d_middle + cotangent.astype(F32)
    d_attn = d_middle.astype(BF16)
    d_attended = contract(d_attn, out_weight, 1, 1).astype(BF16)
    d_pair = exchange(d_attended[:, :shared], False, 5, "d_attended_to_heads")
    d_last = jnp.pad(d_attended[:, shared:], ((0, 0), (HEAD_DIM, 0)))
    d_mixed, d_query_last = attention_backward(
        order, sorted_qkv, exact, level, d_pair, mixed, query_last, exact_last, level_last, d_last,
        query_info, key_info,
    )
    d_rows = exchange(d_mixed, True, 6, "d_mixed_to_rows").reshape(rows, members, 4, PAIR)
    d_key_value_last = jnp.sum(d_rows[:, :, 3].astype(F32), axis=1).astype(BF16)
    d_last_rows = jnp.concatenate([d_query_last[:, :HEAD_DIM], d_key_value_last], axis=1)
    d_own = jnp.concatenate(
        [
            part
            for i in range(3)
            for part in (
                d_rows[:, :, i].reshape(rows, shared),
                d_last_rows[:, i * HEAD_DIM : (i + 1) * HEAD_DIM],
            )
        ],
        axis=1,
    )
    d_normed = both(contract(d_own, w_qkv, 1, 1), contract(d_own, mixer_other, 1, 1), 1)
    d_inputs, grad_gain_one, grad_shift_one = norm_one_pull(d_normed)
    d_inputs = d_inputs + d_middle

    grad_pair = contract(normed_all, d_mixed[:, : 3 * PAIR], 0, 0)
    keep, give = halves(grad_pair)
    keep = keep + swap(give.astype(BF16), "shard", 0).astype(F32)
    mask = 2
    while mask < contexts:
        keep = keep + context_swap(keep.astype(BF16), mask).astype(F32)
        mask *= 2
    pairs = group_gather(keep.astype(BF16), True, True, 7, "gather_pair_gradients")
    pairs = pairs.reshape(members, half, 3, PAIR)

    grad_out = contract(attended, d_attn, 0, 0)
    grad_last = contract(normed, d_last_rows, 0, 0)
    joint = jnp.concatenate([grad_out, jnp.pad(grad_last, ((0, 0), (0, HEAD_DIM)))], axis=1)
    is_near = near == 0
    keep, give = low_half(joint, is_near, 1)
    keep = keep + swap(give.astype(BF16), "tensor", 0).astype(F32)
    keep, give = halves(keep)
    keep = keep + swap(give.astype(BF16), "shard", 0).astype(F32)
    is_second = lax.rem(lax.div(tensor, 2), 2) == 0
    keep, give = low_half(keep, is_second)
    keep = keep + swap(give.astype(BF16), "tensor", 1).astype(F32)
    is_context = lax.rem(context, 2) == 0
    keep, give = low_half(keep, is_context)
    keep = keep + context_swap(give.astype(BF16), 1).astype(F32)
    mask = 2
    while mask < contexts:
        keep = keep + context_swap(keep.astype(BF16), mask).astype(F32)
        mask *= 2
    keep = keep.astype(BF16)

    def rejoin(mine, other, is_low, axis=0):
        return jnp.concatenate(
            [jnp.where(is_low, mine, other), jnp.where(is_low, other, mine)], axis=axis
        )

    keep = rejoin(keep, context_swap(keep, 1), is_context)
    keep = rejoin(keep, swap(keep, "tensor", 1), is_second)
    keep = rejoin(keep, swap(keep, "tensor", 0), is_near, 1).astype(F32)
    own_out = keep[:, :width]
    own_mixer = jnp.concatenate(
        [
            part
            for i in range(3)
            for part in (
                pairs[:, :, i].transpose(1, 0, 2).reshape(half, shared).astype(F32),
                keep[:, width + i * HEAD_DIM : width + (i + 1) * HEAD_DIM],
            )
        ],
        axis=1,
    )

    sums = [
        grad_gain_one,
        grad_shift_one,
        jnp.sum(d_own[:, :width], axis=0, dtype=F32),
        jnp.sum(d_own[:, 2 * width :], axis=0, dtype=F32),
        jnp.sum(d_attn, axis=0, dtype=F32),
        grad_gain_two,
        grad_shift_two,
        jnp.sum(cotangent, axis=0, dtype=F32),
    ]
    sums += [jnp.where(tensor == i, grad_bias_fc, 0.0) for i in range(lax.axis_size("tensor"))]
    sums = lax.psum(jnp.stack(sums), ("shard", "context", "tensor"))
    mine = lax.dynamic_slice_in_dim(sums[:8], shard * half, half, 1)
    own_bias_fc = lax.dynamic_slice_in_dim(sums, 8 + tensor, 1, 0)[0]
    return (
        output,
        d_inputs,
        mine[0],
        mine[1],
        own_mixer,
        mine[2],
        mine[3],
        own_out,
        mine[4],
        mine[5],
        mine[6],
        own_fc,
        own_bias_fc,
        own_proj,
        mine[7],
    )


def solution(mesh):
    return jax.shard_map(
        local,
        mesh=mesh,
        in_specs=(
            P(("shard", "context", "tensor"), None),
            P(("shard", "context", "tensor"), None),
            P("shard"),
            P("shard"),
            P(),
            P("shard"),
            P("shard"),
            P("shard", None),
            P("shard"),
            P("shard"),
            P("shard", None),
            P("shard"),
            P("shard"),
            P("shard"),
            P("shard", "tensor"),
            P("tensor"),
            P("tensor", "shard"),
            P("shard"),
        ),
        out_specs=(
            P(("shard", "context", "tensor"), None),
            P(("shard", "context", "tensor"), None),
            P("shard"),
            P("shard"),
            P("shard", None),
            P("shard"),
            P("shard"),
            P("shard", None),
            P("shard"),
            P("shard"),
            P("shard"),
            P("shard", "tensor"),
            P("tensor"),
            P("tensor", "shard"),
            P("shard"),
        ),
        check_vma=False,
    )
```

```python
import functools

import jax
import jax.numpy as jnp
from jax import lax
from jax.experimental import pallas as pl
from jax.experimental.pallas import tpu as pltpu
from jax.sharding import PartitionSpec as P

HEAD_DIM = 64
PAIR = 2 * HEAD_DIM
PIECE = 128
TRUNK = 8 * PIECE
BRANCH = 3 * PIECE
EPSILON = 1e-05
NEGATIVE = -1e30
F32 = jnp.float32
BF16 = jnp.bfloat16
VMEM = pl.BlockSpec(memory_space=pltpu.VMEM)
SMEM = pl.BlockSpec(memory_space=pltpu.SMEM)
ANY = pl.BlockSpec(memory_space=pl.ANY)
MESH = pl.DeviceIdType.MESH


def contract(left, right, left_dim, right_dim):
    return lax.dot_general(
        left, right, (((left_dim,), (right_dim,)), ((), ())), preferred_element_type=F32
    )


def flip(value, bit):
    low = 1 << bit
    return value + low - 2 * low * lax.rem(lax.div(value, low), 2)


def place():
    tensor, context = lax.axis_index("tensor"), lax.axis_index("context")
    return tensor, context, lax.rem(context, 2) * lax.axis_size("tensor") + tensor


def member(mask):
    tensor, context, _ = place()
    size = lax.axis_size("tensor")
    bits = size.bit_length() - 1
    for bit in range(bits):
        if mask >> bit & 1:
            tensor = flip(tensor, bit)
    if mask >> bits & 1:
        context = flip(context, 0)
    return {"context": context, "tensor": tensor}, lax.rem(context, 2) * size + tensor


def swap(value, axis, bit):
    size = lax.axis_size(axis)
    return lax.ppermute(value, axis, [(i, i ^ 1 << bit) for i in range(size)])


class Wires:
    def __init__(self, send, recv):
        self.send, self.recv, self.used = send, recv, 0

    def start(self, source, target, device):
        copy = pltpu.make_async_remote_copy(
            src_ref=source,
            dst_ref=target,
            send_sem=self.send.at[self.used],
            recv_sem=self.recv.at[self.used],
            device_id=device,
            device_id_type=MESH,
        )
        self.used += 1
        copy.start()
        return copy


def by_rows(rows, step, body, first=0):
    def run(i, carry):
        body(pl.ds(pl.multiple_of(first + i * step, step), step))
        return carry

    lax.fori_loop(0, rows // step, run, 0)


def norm_backward(values, grad, gain):
    average = jnp.mean(values, axis=1, keepdims=True)
    centered = values - average
    inverse = lax.rsqrt(jnp.mean(centered * centered, axis=1, keepdims=True) + EPSILON)
    normal = centered * inverse
    scaled = grad * gain
    result = inverse * (
        scaled
        - jnp.mean(scaled, axis=1, keepdims=True)
        - normal * jnp.mean(scaled * normal, axis=1, keepdims=True)
    )
    return result, jnp.sum(grad * normal, axis=0, keepdims=True), jnp.sum(grad, axis=0, keepdims=True)


def norm_forward(values, gain, shift):
    average = jnp.mean(values, axis=1, keepdims=True)
    centered = values - average
    spread = jnp.mean(centered * centered, axis=1, keepdims=True)
    return centered * lax.rsqrt(spread + EPSILON) * gain + shift


def project_kernel(
    tokens, w_qkv, half_vectors, w_fc, normed, mixed, query_last, vectors, weight, fc_other, everyone, seen, local_sem, send, recv
):
    tensor, context, me = place()
    shard = lax.axis_index("shard")
    members = 2 * lax.axis_size("tensor")
    rows, width = tokens.shape
    half = width // 2
    cut = rows // 2
    shared = width - HEAD_DIM
    across = {"shard": 1 - shard}
    wires = Wires(send, recv)
    turn = members // 2

    barrier = pltpu.get_barrier_semaphore()
    peers = [member(mask)[0] for mask in (1, 2, turn)] + [across]
    rest = [m for m in range(4, members) if m & 1 == 0 and m not in (turn, turn + 2)]
    for peer in peers:
        pl.semaphore_signal(barrier, inc=1, device_id=peer, device_id_type=MESH)
    pl.semaphore_wait(barrier, len(peers))
    assert not rest

    def slot(owner, first=0, size=rows):
        index = member(owner)[1] * rows + first
        return everyone.at[pl.ds(pl.multiple_of(index, 16), size)]

    def hand(source, target):
        return wires.start(source, source, member(target)[0])

    own = pltpu.make_async_copy(tokens, slot(0), local_sem.at[0])
    own.start()
    far = {m: wires.start(tokens, slot(0), member(m)[0]) for m in (2, turn)}
    vector_wire = wires.start(half_vectors, seen, across)
    close = {0: wires.start(tokens, slot(0), member(1)[0])}
    lane = lax.broadcasted_iota(jnp.int32, (1, PAIR), 1) < HEAD_DIM

    def choose(i, carry):
        r = pl.ds(pl.multiple_of(i * 32, 32), 32)
        to = pl.ds(pl.multiple_of(shard * half + i * 32, 32), 32)

        def window(start, size=PAIR):
            return w_qkv[r, pl.ds(pl.multiple_of(start, PAIR), size)]

        def turned(value):
            return pltpu.roll(value.astype(F32), HEAD_DIM, 1)

        weight[to, 0:PAIR] = window(me * PAIR)
        left, right = window(shared + me * PAIR), window(shared + (me + 1) * PAIR)
        weight[to, PAIR : 2 * PAIR] = jnp.where(lane, turned(left), turned(right)).astype(BF16)
        weight[to, 2 * PAIR : 3 * PAIR] = window(2 * width + me * PAIR)
        value = w_qkv[r, 2 * width + shared :]
        value = jnp.concatenate([value, value], axis=1)
        key = turned(w_qkv[r, 2 * width - PAIR : 2 * width])
        weight[to, 3 * PAIR : 4 * PAIR] = jnp.where(lane, key, value.astype(F32)).astype(BF16)
        query = w_qkv[r, shared : shared + PAIR]
        weight[to, 4 * PAIR :] = jnp.where(lane, query, jnp.zeros_like(query))
        return carry

    lax.fori_loop(0, half // 32, choose, 0)
    chosen = weight.at[pl.ds(pl.multiple_of(shard * half, half), half)]
    weight_wire = wires.start(chosen, chosen, across)

    vector_wire.wait_recv()
    vectors[...] = half_vectors[...] + seen[...]
    gain, shift = vectors[0:1, :], vectors[1:2, :]
    scale = HEAD_DIM ** (-0.5)
    pair_lanes = pl.ds(pl.multiple_of(me * PAIR, PAIR), PAIR)
    bias_query, bias_value = vectors[2:3, pair_lanes], vectors[3:4, pair_lanes]
    value_tail = vectors[3:4, shared:]
    bias_last = jnp.where(lane, 0.0, jnp.concatenate([value_tail, value_tail], axis=1))
    query_tail = vectors[2:3, shared:]
    query_tail = jnp.where(lane, jnp.concatenate([query_tail, query_tail], axis=1), 0.0)

    def normalise(owner, first=0, size=rows):
        index = member(owner)[1] * rows + first

        def run(i, carry):
            r = pl.ds(pl.multiple_of(index + i * 32, 32), 32)
            normed[r, :] = norm_forward(everyone[r, :].astype(F32), gain, shift).astype(BF16)
            return carry

        lax.fori_loop(0, size // 32, run, 0)

    def multiply(owner, first=0, size=rows):
        r = pl.ds(pl.multiple_of(member(owner)[1] * rows + first, 32), size)
        result = jnp.dot(normed[r, :], weight[:, 0 : 4 * PAIR], preferred_element_type=F32)
        mixed[r, 0:PAIR] = ((result[:, 0:PAIR] + bias_query) * scale).astype(BF16)
        mixed[r, PAIR : 2 * PAIR] = result[:, PAIR : 2 * PAIR].astype(BF16)
        mixed[r, 2 * PAIR : 3 * PAIR] = (result[:, 2 * PAIR : 3 * PAIR] + bias_value).astype(BF16)
        mixed[r, 3 * PAIR :] = (result[:, 3 * PAIR :] + bias_last).astype(BF16)

    own.wait()
    normalise(0)
    close[0].wait_recv()
    normalise(1)
    pieces = {}
    for m, other, first in ((2, turn, 0), (turn, 2, cut)):
        far[m].wait_recv()
        close[m] = hand(slot(m), 1)
        pieces[other] = hand(slot(m, first, cut), other)
    weight_wire.wait_recv()
    fc_wire = wires.start(w_fc, fc_other, across)
    multiply(0)
    last = jnp.dot(
        normed[pl.ds(pl.multiple_of(me * rows, 32), rows), :], weight[:, 4 * PAIR :], preferred_element_type=F32
    )
    query_last[...] = ((last + query_tail) * scale).astype(BF16)
    multiply(1)
    for m in (2, turn):
        normalise(m)
        multiply(m)
    for m in (2, turn):
        close[m].wait_recv()
        normalise(m ^ 1)
        multiply(m ^ 1)
    opposite = 2 ^ turn
    passed = []
    for m, first in ((turn, 0), (2, cut)):
        pieces[m].wait_recv()
        passed.append(hand(slot(opposite, first, cut), 1))
    normalise(opposite)
    multiply(opposite)
    for wire in passed:
        wire.wait_recv()
    normalise(opposite ^ 1)
    multiply(opposite ^ 1)
    fc_wire.wait_recv()
    for wire in list(far.values()) + list(close.values()) + list(pieces.values()) + passed + [vector_wire, weight_wire, fc_wire]:
        wire.wait_send()


def project(tokens, w_qkv, half_vectors, w_fc):
    rows, width = tokens.shape
    tree = 2 * lax.axis_size("tensor") * rows
    shape = jax.ShapeDtypeStruct
    return pl.pallas_call(
        project_kernel,
        in_specs=[VMEM] * 3 + [ANY],
        out_specs=[VMEM] * 5 + [ANY],
        out_shape=[
            shape((tree, width), BF16),
            shape((tree, 4 * PAIR), BF16),
            shape((rows, PAIR), BF16),
            shape(half_vectors.shape, F32),
            shape((width, 5 * PAIR), BF16),
            shape(w_fc.shape, BF16),
        ],
        scratch_shapes=[
            pltpu.VMEM((tree, width), BF16),
            pltpu.VMEM(half_vectors.shape, F32),
            pltpu.SemaphoreType.DMA((1,)),
            pltpu.SemaphoreType.DMA((16,)),
            pltpu.SemaphoreType.DMA((16,)),
        ],
        compiler_params=pltpu.CompilerParams(
            collective_id=0, has_side_effects=True, vmem_limit_bytes=32 << 20
        ),
        name="project",
    )(tokens, w_qkv, half_vectors, w_fc)


def feed_forward_kernel(
    pair,
    last,
    tokens,
    cotangent,
    cotangent_far,
    out_mine,
    fc_mine,
    fc_other,
    proj_mine,
    proj_other,
    vectors,
    bias_fc,
    residual,
    fed_give,
    d_middle,
    d_pair,
    d_last,
    joint_keep,
    joint_give,
    fc_keep,
    fc_give,
    proj_sum,
    sums,
    w_out,
    w_fc,
    w_proj,
    attended,
    middle,
    normed,
    hidden,
    d_before,
    d_hidden,
    part,
    near,
    passing,
    far,
    d_attn,
    d_attended,
    grads,
    proj_keep,
    proj_give,
    proj_got,
    joint,
    joint_near,
    local_sem,
    send,
    recv,
):
    tensor, context, me = place()
    shard = lax.axis_index("shard")
    near_bit = lax.rem(tensor, 2)
    members = 2 * lax.axis_size("tensor")
    rows, width = tokens.shape
    half = width // 2
    shared = width - HEAD_DIM
    group = range(1, members)
    wires = Wires(send, recv)
    bias_out, gain, shift, bias_proj = (vectors[i : i + 1, :] for i in (4, 5, 6, 7))
    across = {"shard": 1 - shard}

    barrier = pltpu.get_barrier_semaphore()
    peers = [member(mask)[0] for mask in group] + [across]
    for peer in peers:
        pl.semaphore_signal(barrier, inc=1, device_id=peer, device_id_type=MESH)
    pl.semaphore_wait(barrier, len(peers))

    def slab(ref, index, size):
        return ref.at[pl.ds(pl.multiple_of(index * size, size), size)]

    def beside(ref, index):
        return ref.at[:, pl.ds(pl.multiple_of(index * PAIR, PAIR), PAIR)]

    moved = []
    for mask in group:
        device, index = member(mask)
        moved.append(wires.start(slab(pair, index, rows), beside(attended, me), device))
    quarter = half // 2
    out_wire = wires.start(
        slab(out_mine, near_bit, quarter), slab(w_out, 2 * shard + near_bit, quarter), across
    )
    local = [
        pltpu.make_async_copy(source, target, local_sem.at[i])
        for i, (source, target) in enumerate(
            (
                (slab(pair, me, rows), beside(attended, me)),
                (out_mine, slab(w_out, shard, half)),
                (fc_mine, slab(w_fc, shard, half)),
                (fc_other, slab(w_fc, 1 - shard, half)),
                (proj_mine, slab(w_proj, shard, half)),
                (proj_other, slab(w_proj, 1 - shard, half)),
                (cotangent, slab(grads, 0, rows)),
                (cotangent_far, slab(grads, 2, rows)),
            )
        )
    ]
    pulled_wires = [
        wires.start(source, slab(grads, index, rows), member(1)[0])
        for index, source in ((1, cotangent), (3, cotangent_far))
    ]
    for copy in local:
        copy.start()
    attended[:, shared:] = last[:, 0:HEAD_DIM]
    out_wire.wait_recv()
    out_part = slab(w_out, 2 * (1 - shard) + near_bit, quarter)
    out_near = wires.start(out_part, out_part, member(1)[0])
    for copy in local:
        copy.wait()
    for wire in moved + [out_near]:
        wire.wait_recv()

    start = 0
    while start < width:
        stop = min(start + 2 * PAIR, width)
        middle[:, start:stop] = (
            tokens[:, start:stop].astype(F32)
            + jnp.dot(attended[...], w_out[:, start:stop], preferred_element_type=F32)
            + bias_out[:, start:stop]
        )
        start = stop

    def second_norm(r):
        normed[r, :] = norm_forward(middle[r, :], gain, shift).astype(BF16)

    cut = rows // 2

    def piece(mask, i):
        return slice(mask * rows + i * cut, mask * rows + (i + 1) * cut)

    cross = []
    for i in range(2):
        by_rows(cut, 32, second_norm, i * cut)
        cross.append(wires.start(normed.at[piece(0, i)], normed.at[piece(2, i)], member(2)[0]))

    def block(ref, mask):
        return ref.at[mask * rows : (mask + 1) * rows, :]

    close = wires.start(block(normed, 0), block(normed, 1), member(1)[0])
    for wire in pulled_wires:
        wire.wait_recv()
    for mask in range(4):
        block(d_hidden, mask)[...] = jnp.dot(
            block(grads, mask)[...], w_proj[...], preferred_element_type=F32
        )

    def feed(r):
        start = 0
        while start < width:
            stop = min(start + 2 * PAIR, width)
            c = slice(start, stop)
            before = jnp.dot(normed[r, :], w_fc[:, c], preferred_element_type=F32) + bias_fc[0:1, c]
            cumulative = 0.5 + 0.5 * lax.erf(before * (0.5**0.5))
            hidden[r, c] = (before * cumulative).astype(BF16)
            slope = cumulative + before * jnp.exp(-0.5 * before * before) * ((2 * jnp.pi) ** -0.5)
            d_before[r, c] = (d_hidden[r, c] * slope).astype(BF16)
            start = stop

    def back(r):
        return contract(d_before[r, :], w_fc[...], 1, 1)

    def ahead(mask):
        return contract(hidden[mask * rows : (mask + 1) * rows, :], w_proj[...], 1, 1)

    feed(slice(0, rows))
    close.wait_recv()
    feed(slice(rows, 2 * rows))
    part[0] = back(slice(rows, 2 * rows)).astype(BF16)
    to_near = wires.start(part.at[0], near.at[0], member(1)[0])
    relay, to_pass, to_far = [], [], []
    for i in range(2):
        h = slice(i * cut, (i + 1) * cut)
        cross[i].wait_recv()
        relay.append(wires.start(normed.at[piece(2, i)], normed.at[piece(3, i)], member(1)[0]))
        feed(piece(2, i))
        relay[i].wait_recv()
        feed(piece(3, i))
        part[1, h] = back(piece(3, i)).astype(BF16)
        to_pass.append(wires.start(part.at[1, h], near.at[1, h], member(1)[0]))
        mine = back(piece(2, i))
        to_pass[i].wait_recv()
        passing[h] = (mine + near[1, h].astype(F32)).astype(BF16)
        to_far.append(wires.start(passing.at[h], far.at[h], member(2)[0]))

    other_part = pl.ds(pl.multiple_of(2 * rows + (1 - shard) * half, 8), half)
    own_part = pl.ds(pl.multiple_of(2 * rows + shard * half, 8), half)
    proj_wires = []
    start = 0
    while start < width:
        stop = min(start + 2 * PAIR, width)
        c = slice(start, stop)
        d_hidden_part = d_hidden.at[2 * rows : 2 * rows + width, 0 : stop - start]
        d_hidden_part[...] = contract(grads[...], hidden[:, c], 0, 0)
        proj_give[:, c] = d_hidden[other_part, 0 : stop - start].astype(BF16)
        proj_wires.append(wires.start(proj_give.at[:, c], proj_got.at[:, c], across))
        proj_keep[:, c] = d_hidden[own_part, 0 : stop - start]
        start = stop
    start = 0
    while start < width:
        stop = min(start + 2 * PAIR, width)
        c = slice(start, stop)
        d_hidden_part = d_hidden.at[2 * rows : 2 * rows + width, 0 : stop - start]
        d_hidden_part[...] = contract(normed[...], d_before[:, c], 0, 0)
        fc_give[:, c] = d_hidden[other_part, 0 : stop - start].astype(BF16)
        fc_keep[:, c] = d_hidden[own_part, 0 : stop - start].astype(BF16)
        start = stop
    d_hidden[0:rows, :] = back(slice(0, rows))
    to_near.wait_recv()
    for wire in to_far:
        wire.wait_recv()

    sums[...] = jnp.zeros_like(sums)

    def second_back(r):
        grad = d_hidden[r, :] + near[0, r, :].astype(F32) + far[r, :].astype(F32)
        result, by_gain, by_shift = norm_backward(middle[r, :], grad, gain)
        pulled = cotangent[r, :].astype(F32)
        result = result + pulled
        d_middle[r, :] = result
        low = result.astype(BF16)
        d_attn[r, 0:width] = low
        d_attn[r, width:] = jnp.zeros((r.size, d_attn.shape[1] - width), BF16)
        sums[4:5, :] += jnp.sum(low.astype(F32), axis=0, keepdims=True)
        sums[5:6, :] += by_gain
        sums[6:7, :] += by_shift
        sums[7:8, :] += jnp.sum(pulled, axis=0, keepdims=True)

    by_rows(rows, 64, second_back)
    start = 0
    while start < width:
        stop = min(start + 2 * PAIR, width)
        d_attended[:, start:stop] = contract(d_attn[:, 0:width], w_out[start:stop, :], 1, 1).astype(BF16)
        start = stop
    returned = []
    for mask in group:
        device, index = member(mask)
        returned.append(wires.start(beside(d_attended, index), slab(d_pair, me, rows), device))
    own_copy = pltpu.make_async_copy(beside(d_attended, me), slab(d_pair, me, rows), local_sem.at[0])
    own_copy.start()
    lane = lax.broadcasted_iota(jnp.int32, (1, PAIR), 1) >= HEAD_DIM
    tail = jnp.concatenate([d_attended[:, shared:]] * 2, axis=1)
    d_last[...] = jnp.where(lane, tail, jnp.zeros_like(tail))
    joint[:, shared : shared + PAIR] = jnp.zeros((width, PAIR), BF16)
    start = 0
    while start < d_attn.shape[1]:
        stop = min(start + 2 * PAIR, d_attn.shape[1])
        to = start if start < shared else start + PAIR
        joint[:, to : to + stop - start] = contract(attended[...], d_attn[:, start:stop], 0, 0).astype(BF16)
        start = stop
    side = joint.shape[1] // 2
    kept = pl.ds(pl.multiple_of(near_bit * side, side), side)
    given = pl.ds(pl.multiple_of((1 - near_bit) * side, side), side)
    joint_wire = wires.start(joint.at[:, given], joint_near, member(1)[0])
    part[2] = ahead(3).astype(BF16)
    to_pass_out = wires.start(part.at[2], near.at[3], member(1)[0])
    part[3] = ahead(1).astype(BF16)
    to_near_out = wires.start(part.at[3], near.at[2], member(1)[0])
    d_hidden[2 * rows : 3 * rows, :] = ahead(2)
    d_hidden[rows : 2 * rows, :] = ahead(0)
    bias = jnp.zeros((1, width), F32)

    def add_bias(i, total):
        r = pl.ds(pl.multiple_of(i * 64, 64), 64)
        return total + jnp.sum(d_before[r, :].astype(F32), axis=0, keepdims=True)

    bias = lax.fori_loop(0, 4 * rows // 64, add_bias, bias)
    for i in range(lax.axis_size("tensor")):
        sums[8 + i : 9 + i, :] = jnp.where(tensor == i, bias, 0.0)
    to_near_out.wait_recv()
    to_pass_out.wait_recv()

    def finish_output(r):
        third = pl.ds(pl.multiple_of(2 * rows + r.start, 64), r.size)
        again = pl.ds(pl.multiple_of(rows + r.start, 64), r.size)
        fed_give[r, :] = (d_hidden[third, :] + near[3, r, :].astype(F32)).astype(BF16)
        residual[r, :] = middle[r, :] + d_hidden[again, :] + near[2, r, :].astype(F32) + bias_proj

    by_rows(rows, 64, finish_output)
    joint_wire.wait_recv()
    second = lax.rem(lax.div(tensor, 2), 2)

    def add_joint(target, which):
        for i in range(2):

            def run(r):
                source = pl.ds(pl.multiple_of((2 * i + which) * quarter - i * quarter + r.start, 16), r.size)
                total = joint[source, kept].astype(F32) + joint_near[source, :].astype(F32)
                target[r, :] = total.astype(BF16)

            by_rows(quarter, 16, run, i * quarter)

    add_joint(joint_keep, second)
    add_joint(joint_give, 1 - second)
    for wire in proj_wires:
        wire.wait_recv()

    def add_proj(r):
        proj_sum[r, :] = (proj_keep[r, :] + proj_got[r, :].astype(F32)).astype(BF16)

    by_rows(half, 32, add_proj)
    own_copy.wait()
    for wire in returned:
        wire.wait_recv()
    for wire in (
        moved + returned + [out_wire, out_near] + pulled_wires + proj_wires
        + cross + relay + to_pass + to_far + [joint_wire, close, to_near, to_near_out, to_pass_out]
    ):
        wire.wait_send()


def feed_forward(pair, last, tokens, cotangent, cotangent_far, out_mine, fc_mine, fc_other, proj_mine, proj_other, vectors, bias_fc):
    rows, width = tokens.shape
    members = 2 * lax.axis_size("tensor")
    hidden = fc_mine.shape[1]
    tall = 4 * rows
    shape = jax.ShapeDtypeStruct
    return pl.pallas_call(
        feed_forward_kernel,
        in_specs=[ANY] + [VMEM] * 4 + [ANY] * 5 + [VMEM] * 2,
        out_specs=[VMEM] * 3 + [ANY] + [VMEM] * 7,
        out_shape=[
            shape((rows, width), F32),
            shape((rows, width), BF16),
            shape((rows, width), F32),
            shape((members * rows, PAIR), BF16),
            shape((rows, PAIR), BF16),
            shape((width // 2, 5 * PAIR), BF16),
            shape((width // 2, 5 * PAIR), BF16),
            shape((width // 2, hidden), BF16),
            shape((width // 2, hidden), BF16),
            shape((width // 2, hidden), BF16),
            shape((16, width), F32),
        ],
        scratch_shapes=[
            pltpu.VMEM((width, width), BF16),
            pltpu.VMEM((width, hidden), BF16),
            pltpu.VMEM((width, hidden), BF16),
            pltpu.VMEM((rows, width), BF16),
            pltpu.VMEM((rows, width), F32),
            pltpu.VMEM((tall, width), BF16),
            pltpu.VMEM((tall, hidden), BF16),
            pltpu.VMEM((tall, hidden), BF16),
            pltpu.VMEM((2 * rows + max(2 * rows, width), hidden), F32),
            pltpu.VMEM((4, rows, width), BF16),
            pltpu.VMEM((4, rows, width), BF16),
            pltpu.VMEM((rows, width), BF16),
            pltpu.VMEM((rows, width), BF16),
            pltpu.VMEM((rows, 9 * PAIR), BF16),
            pltpu.VMEM((rows, width), BF16),
            pltpu.VMEM((tall, width), BF16),
            pltpu.VMEM((width // 2, hidden), F32),
            pltpu.VMEM((width // 2, hidden), BF16),
            pltpu.VMEM((width // 2, hidden), BF16),
            pltpu.VMEM((width, 10 * PAIR), BF16),
            pltpu.VMEM((width, 5 * PAIR), BF16),
            pltpu.SemaphoreType.DMA((8,)),
            pltpu.SemaphoreType.DMA((2 * members + 20,)),
            pltpu.SemaphoreType.DMA((2 * members + 20,)),
        ],
        compiler_params=pltpu.CompilerParams(
            collective_id=3, has_side_effects=True, vmem_limit_bytes=62 << 20
        ),
        name="feed_forward",
    )(pair, last, tokens, cotangent, cotangent_far, out_mine, fc_mine, fc_other, proj_mine, proj_other, vectors, bias_fc)


def finish_kernel(
    d_mixed,
    d_query_last,
    normed,
    weight,
    tokens,
    d_middle,
    gain,
    joint_keep,
    joint_other,
    vectors,
    residual,
    fed_give,
    output,
    d_tokens,
    own_mixer,
    own_out,
    sums,
    near_give,
    near_got,
    row_sum,
    second_got,
    turn_got,
    second_last,
    turn_last,
    last_low,
    fed_got,
    pair_t,
    pair,
    pair_give,
    pair_got,
    pair_low,
    pair_seen,
    pairs,
    tail,
    tail_near,
    tail_sum,
    tail_give,
    tail_got,
    joint_give,
    joint_got,
    half_low,
    half_seen,
    joint_all,
    pair_sum,
    half_sum,
    vec,
    vec_give,
    vec_got,
    mixer_rows,
    mixer_sem,
    send,
    recv,
):
    tensor, context, me = place()
    shard = lax.axis_index("shard")
    near = lax.rem(tensor, 2)
    second = lax.rem(lax.div(tensor, 2), 2)
    contexts = lax.axis_size("context")
    members = 2 * lax.axis_size("tensor")
    turn = members // 2
    rows, width = tokens.shape
    half = width // 2
    quarter = half // 2
    cut = rows // 2
    side = joint_keep.shape[1]
    shared = width - HEAD_DIM
    block = 4 * PAIR
    across = {"shard": 1 - shard}
    higher = [
        {"context": flip(context, bit)} for bit in range(1, contexts.bit_length() - 1)
    ]
    group = range(1, members)
    wires = Wires(send, recv)
    lane = lax.broadcasted_iota(jnp.int32, (1, PAIR), 1) < HEAD_DIM

    barrier = pltpu.get_barrier_semaphore()
    peers = [member(mask)[0] for mask in group] + [across] + higher
    for peer in peers:
        pl.semaphore_signal(barrier, inc=1, device_id=peer, device_id_type=MESH)
    pl.semaphore_wait(barrier, len(peers))

    def part(ref, index, size):
        return ref.at[pl.ds(pl.multiple_of(index * size, size), size)]

    def term(mask):
        r = pl.ds(pl.multiple_of(member(mask)[1] * rows, rows), rows)
        return contract(d_mixed[r, :], weight[:, 0:block], 1, 1)

    steps = d_mixed.shape[0] // (2 * rows)
    pair_t[...] = jnp.zeros_like(pair_t)

    def accumulate(i, carry):
        r = pl.ds(pl.multiple_of(i * 2 * rows, 2 * rows), 2 * rows)
        pair_t[...] += contract(d_mixed[r, :], normed[r, :], 0, 0)
        return carry

    lax.fori_loop(0, steps, accumulate, 0)
    pair[...] = pair_t[...].T
    other = pl.ds(pl.multiple_of((1 - shard) * half, half), half)
    own = pl.ds(pl.multiple_of(shard * half, half), half)
    pair_give[...] = pair[other, 0 : 3 * PAIR].astype(BF16)
    pair_wire = wires.start(pair_give, pair_got, across)
    mine = pl.ds(pl.multiple_of(me * rows, rows), rows)
    tail[:, 0:PAIR] = pair[:, 3 * PAIR :].astype(BF16)
    tail[:, PAIR:] = contract(d_query_last[...], normed[mine, :], 0, 0).T.astype(BF16)
    tail_near_wire = wires.start(tail, tail_near, member(1)[0])

    order = [6, 2, 4, 0]
    near_wires = {}
    for i, mask in enumerate(order):
        near_give[i] = term(mask ^ 1).astype(BF16)
        near_wires[mask] = wires.start(near_give.at[i], near_got.at[i], member(1)[0])

    tail_near_wire.wait_recv()

    def add_tail_near(r):
        tail_sum[r, :] = tail[r, :].astype(F32) + tail_near[r, :].astype(F32)

    by_rows(width, 64, add_tail_near)
    to_second, to_turn = member(2)[0], member(turn)[0]
    for i in range(2):
        source = pl.ds(pl.multiple_of(i * half + (1 - second) * quarter, 16), quarter)
        tail_give[i * quarter : (i + 1) * quarter, :] = tail_sum[source, :].astype(BF16)
    tail_wire = wires.start(tail_give, tail_got, to_second)

    first = slice(0, cut)
    rest = slice(cut, rows)
    second_wires, turn_wires = [], []
    for i, mask in enumerate(order):
        total = term(mask)
        if mask == 0:
            query = pltpu.roll(d_query_last[...].astype(F32), HEAD_DIM, 1).astype(BF16)
            total = total + contract(query, weight[:, block:], 1, 1)
        near_wires[mask].wait_recv()
        total = total + near_got[i].astype(F32)
        if i:
            row_sum[i - 1] = total
        if mask:
            near_got[i] = total.astype(BF16)
        if mask & 2:
            second_wires.append(
                wires.start(near_got.at[i, first], second_got.at[len(second_wires)], to_second)
            )
        if mask & turn:
            turn_wires.append(wires.start(near_got.at[i, rest], turn_got.at[len(turn_wires)], to_turn))

    pair_wire.wait_recv()
    pair_own = pair[own, 0 : 3 * PAIR] + pair_got[...].astype(F32)
    pair_wires = []
    for i, device in enumerate(higher):
        pair_low[i] = pair_own.astype(BF16)
        wire = wires.start(pair_low.at[i], pair_seen.at[i], device)
        pair_wires.append(wire)
        if i < len(higher) - 1:
            wire.wait_recv()
            pair_own = pair_own + pair_seen[i].astype(F32)
    pair_sum[...] = pair_own

    tail_wire.wait_recv()
    wide = joint_keep.shape[1] - 2 * PAIR

    def joint_term(which):
        r = pl.ds(pl.multiple_of(which * quarter, quarter), quarter)
        s = pl.ds(pl.multiple_of(which * half + second * quarter, quarter), quarter)
        total = joint_keep[r, :].astype(F32) + joint_other[r, :].astype(F32)
        last = jnp.where(near == 1, tail_sum[s, :] + tail_got[r, :].astype(F32), 0.0)
        return jnp.concatenate([total[:, :wide], total[:, wide:] + last], axis=1)

    joint_give[...] = joint_term(1 - shard).astype(BF16)
    joint_wire = wires.start(joint_give, joint_got, across)

    vec[...] = vectors[...]

    def add_columns(i, total):
        r = pl.ds(pl.multiple_of(i * 64, 64), 64)
        return total + jnp.sum(d_mixed[r, :].astype(F32), axis=0, keepdims=True)

    columns = lax.fori_loop(0, d_mixed.shape[0] // 64, add_columns, jnp.zeros((1, block), F32))
    pair_lanes = pl.ds(pl.multiple_of(me * PAIR, PAIR), PAIR)
    vec[2:3, pair_lanes] = columns[:, 0:PAIR]
    vec[3:4, pair_lanes] = columns[:, 2 * PAIR : 3 * PAIR]
    query = jnp.sum(d_query_last[...].astype(F32), axis=0, keepdims=True)
    vec[2:3, shared:] = pltpu.roll(query, HEAD_DIM, 1)[:, :HEAD_DIM]
    vec[3:4, shared:] = pltpu.roll(columns[:, 3 * PAIR :], HEAD_DIM, 1)[:, :HEAD_DIM]

    joint_wire.wait_recv()
    half_sum[...] = joint_term(shard) + joint_got[...].astype(F32)
    hops = [to_turn] + higher
    joint_wires = []

    def joint_hop(i):
        if i:
            joint_wires[-1].wait_recv()
            half_sum[...] += half_seen[i - 1].astype(F32)
        if i < len(hops):
            half_low[i] = half_sum[...].astype(BF16)
            joint_wires.append(wires.start(half_low.at[i], half_seen.at[i], hops[i]))

    joint_hop(0)

    second_wires[0].wait_recv()
    last_low[0] = (row_sum[1, first] + second_got[0].astype(F32)).astype(BF16)
    turn_wires.append(wires.start(last_low.at[0], turn_last, to_turn))
    turn_wires[0].wait_recv()
    last_low[1] = (row_sum[0, rest] + turn_got[0].astype(F32)).astype(BF16)
    second_wires.append(wires.start(last_low.at[1], second_last, to_second))

    for i in range(1, len(hops)):
        joint_hop(i)

    if pair_wires:
        pair_wires[-1].wait_recv()
        pair_sum[...] += pair_seen[len(higher) - 1].astype(F32)

    def slot(owner, start=0, size=half):
        return pairs.at[pl.ds(pl.multiple_of(member(owner)[1] * half + start, 16), size)]

    def hand(source, target):
        return wires.start(source, source, member(target)[0])

    pairs[pl.ds(pl.multiple_of(me * half, half), half), :] = pair_sum[...].astype(BF16)
    far = {mask: hand(slot(0), mask) for mask in (2, turn)}
    close = {0: hand(slot(0), 1)}

    second_wires[1].wait_recv()
    second_wires[2].wait_recv()
    turn_wires[1].wait_recv()
    turn_wires[2].wait_recv()
    row_sum[2, first] = row_sum[2, first] + second_got[1].astype(F32) + turn_last[...].astype(F32)
    row_sum[2, rest] = row_sum[2, rest] + turn_got[1].astype(F32) + second_last[...].astype(F32)

    def first_norm(r):
        result, by_gain, by_shift = norm_backward(tokens[r, :].astype(F32), row_sum[2, r, :], gain[0:1, :])
        d_tokens[r, :] = result + d_middle[r, :]
        vec[0:1, :] += by_gain
        vec[1:2, :] += by_shift

    by_rows(rows, 64, first_norm)
    vec_wires = []

    def vec_send(i, device):
        vec_give[i] = vec[...]
        vec_wires.append(wires.start(vec_give.at[i], vec_got.at[i], device))

    def vec_add():
        i = len(vec_wires) - 1
        vec_wires[i].wait_recv()
        vec[...] += vec_got[i]

    vec_stops = [member(1)[0], to_second, to_turn, across] + higher
    vec_send(0, vec_stops[0])

    pieces = {}
    for mask, onward, start in ((2, turn, 0), (turn, 2, quarter)):
        far[mask].wait_recv()
        close[mask] = hand(slot(mask), 1)
        pieces[onward] = hand(slot(mask, start, quarter), onward)
    vec_add()
    vec_send(1, vec_stops[1])

    joint_hop(len(hops))
    keep = pl.ds(pl.multiple_of(second * quarter, quarter), quarter)
    kept = pl.ds(pl.multiple_of(near * side, side), side)
    joint_all[keep, kept] = half_sum[...].astype(BF16)
    joint_mine = joint_all.at[keep, kept]
    back = wires.start(joint_mine, joint_mine, to_second)
    vec_add()
    vec_send(2, vec_stops[2])
    fed_wire = wires.start(fed_give, fed_got, to_second)
    opposite = 2 ^ turn
    passed = []
    for mask, start in ((turn, 0), (2, quarter)):
        pieces[mask].wait_recv()
        passed.append(hand(slot(opposite, start, quarter), 1))
    vec_add()
    vec_send(3, vec_stops[3])
    back.wait_recv()
    joint_side = joint_all.at[:, kept]
    back_near = wires.start(joint_side, joint_side, member(1)[0])
    vec_add()
    for i in range(4, len(vec_stops)):
        vec_send(i, vec_stops[i])
        vec_add()
    sums[...] = vec[...]
    fed_wire.wait_recv()

    def add_fed(r):
        output[r, :] = (residual[r, :] + fed_got[r, :].astype(F32)).astype(BF16)

    by_rows(rows, 64, add_fed)
    for wire in list(close.values()) + passed:
        wire.wait_recv()
    back_near.wait_recv()

    tall = mixer_rows.shape[1]

    def mixer_copy(i, j):
        r = pl.ds(pl.multiple_of((2 * i + j) * tall, tall), tall)
        return pltpu.make_async_copy(mixer_rows.at[j], own_mixer.at[r], mixer_sem.at[j])

    def write(i, carry):
        for j in range(2):

            @pl.when(i > 0)
            def _():
                mixer_copy(i - 1, j).wait()

            start = (2 * i + j) * tall
            r = pl.ds(pl.multiple_of(start, tall), tall)
            own_out[r, 0:shared] = joint_all[r, 0:shared].astype(F32)
            eighth = joint_all[r, shared : shared + PAIR].astype(F32)
            ninth = joint_all[r, shared + PAIR :].astype(F32)
            own_out[r, shared:] = ninth[:, :HEAD_DIM]
            keys = []
            for k in range(members):
                value = pairs[pl.ds(pl.multiple_of(k * half + start, tall), tall), :].astype(F32)
                mixer_rows[j, :, k * PAIR : (k + 1) * PAIR] = value[:, 0:PAIR]
                mixer_rows[j, :, 2 * width + k * PAIR : 2 * width + (k + 1) * PAIR] = value[:, 2 * PAIR :]
                keys.append(value[:, PAIR : 2 * PAIR])
            keys = jnp.concatenate(keys + [jnp.where(lane, eighth, ninth)], axis=1)
            mixer_rows[j, :, shared : 2 * width] = pltpu.roll(keys, HEAD_DIM, 1)
            mixer_rows[j, :, 2 * width + shared :] = pltpu.roll(eighth, HEAD_DIM, 1)[:, :HEAD_DIM]
            mixer_copy(i, j).start()
        return carry

    trips = half // (2 * tall)
    lax.fori_loop(0, trips, write, 0)
    for j in range(2):
        mixer_copy(trips - 1, j).wait()
    for wire in (
        [pair_wire, tail_near_wire, tail_wire, joint_wire, back, back_near, fed_wire]
        + list(near_wires.values()) + second_wires + turn_wires + pair_wires + list(far.values())
        + list(close.values()) + list(pieces.values()) + passed + joint_wires + vec_wires
    ):
        wire.wait_send()


def finish(d_mixed, d_query_last, normed, weight, tokens, d_middle, gain, joint_keep, joint_other, vectors, residual, fed_give):
    rows, width = tokens.shape
    half = width // 2
    members = 2 * lax.axis_size("tensor")
    higher = lax.axis_size("context").bit_length() - 2
    side = joint_keep.shape[1]
    tall = vectors.shape[0]
    scratch = [
        pltpu.VMEM((4, rows, width), BF16),
        pltpu.VMEM((4, rows, width), BF16),
        pltpu.VMEM((3, rows, width), F32),
        pltpu.VMEM((2, rows // 2, width), BF16),
        pltpu.VMEM((2, rows // 2, width), BF16),
        pltpu.VMEM((rows // 2, width), BF16),
        pltpu.VMEM((rows // 2, width), BF16),
        pltpu.VMEM((2, rows // 2, width), BF16),
        pltpu.VMEM((rows, width), BF16),
        pltpu.VMEM((4 * PAIR, width), F32),
        pltpu.VMEM((width, 4 * PAIR), F32),
        pltpu.VMEM((half, 3 * PAIR), BF16),
        pltpu.VMEM((half, 3 * PAIR), BF16),
        pltpu.VMEM((max(higher, 1), half, 3 * PAIR), BF16),
        pltpu.VMEM((max(higher, 1), half, 3 * PAIR), BF16),
        pltpu.VMEM((members * half, 3 * PAIR), BF16),
        pltpu.VMEM((width, 2 * PAIR), BF16),
        pltpu.VMEM((width, 2 * PAIR), BF16),
        pltpu.VMEM((width, 2 * PAIR), F32),
        pltpu.VMEM((half, 2 * PAIR), BF16),
        pltpu.VMEM((half, 2 * PAIR), BF16),
        pltpu.VMEM((half // 2, side), BF16),
        pltpu.VMEM((half // 2, side), BF16),
        pltpu.VMEM((higher + 1, half // 2, side), BF16),
        pltpu.VMEM((higher + 1, half // 2, side), BF16),
        pltpu.VMEM((half, 2 * side), BF16),
        pltpu.VMEM((half, 3 * PAIR), F32),
        pltpu.VMEM((half // 2, side), F32),
        pltpu.VMEM((tall, width), F32),
        pltpu.VMEM((higher + 4, tall, width), F32),
        pltpu.VMEM((higher + 4, tall, width), F32),
        pltpu.VMEM((2, 16, 3 * width), F32),
        pltpu.SemaphoreType.DMA((2,)),
        pltpu.SemaphoreType.DMA((3 * members + 3 * higher + 20,)),
        pltpu.SemaphoreType.DMA((3 * members + 3 * higher + 20,)),
    ]
    return pl.pallas_call(
        finish_kernel,
        in_specs=[VMEM] * 12,
        out_specs=[VMEM] * 2 + [ANY] + [VMEM] * 2,
        out_shape=[
            jax.ShapeDtypeStruct((rows, width), BF16),
            jax.ShapeDtypeStruct((rows, width), F32),
            jax.ShapeDtypeStruct((half, 3 * width), F32),
            jax.ShapeDtypeStruct((half, width), F32),
            jax.ShapeDtypeStruct((tall, width), F32),
        ],
        scratch_shapes=scratch,
        compiler_params=pltpu.CompilerParams(
            collective_id=6, has_side_effects=True, vmem_limit_bytes=63 << 20
        ),
        name="finish",
    )(d_mixed, d_query_last, normed, weight, tokens, d_middle, gain, joint_keep, joint_other, vectors, residual, fed_give)


def tri(n):
    r=lax.broadcasted_iota(jnp.int32,(n,n),0); c=lax.broadcasted_iota(jnp.int32,(n,n),1)
    return c<=r

def branch_mask():
    r=lax.broadcasted_iota(jnp.int32,(BRANCH,BRANCH),0); c=lax.broadcasted_iota(jnp.int32,(BRANCH,BRANCH),1)
    return (c<=r)&((c<PIECE)|(c//PIECE==r//PIECE))

def split_heads(x):
    lane=lax.broadcasted_iota(jnp.int32,(1,2*64),1)<64
    z=jnp.zeros_like(x)
    return jnp.concatenate([jnp.where(lane,x,z),jnp.where(lane,z,x)],axis=0)

def join_heads(x):
    n=x.shape[0]//2
    lane=lax.broadcasted_iota(jnp.int32,(1,2*64),1)<64
    return jnp.where(lane,x[:n],x[n:])

def fwd_kernel(order, qkv, q16, qinfo, kinfo, att, att16, canon, of, lse, of16, lse16):
    n_p=qkv.shape[0]//PIECE
    for i in range(n_p):
        src=pl.ds(pl.multiple_of(order[i]*PIECE,PIECE),PIECE)
        canon[i*PIECE:(i+1)*PIECE,:]=qkv[src,0:384]
    def rows(start,size,parts):
        qh=split_heads(canon[pl.ds(start,size),0:128])
        ss=[]
        for ks,kn,mask in parts:
            s=contract(qh,canon[pl.ds(ks,kn),128:256],1,1)
            if mask is not None:
                m2=jnp.concatenate([mask,mask],axis=0)
                s=jnp.where(m2,s,NEGATIVE)
            ss.append(s)
        top=functools.reduce(jnp.maximum,[jnp.max(s,axis=1,keepdims=True) for s in ss])
        tot=0.; o=0.
        for (ks,kn,_),s in zip(parts,ss):
            e=jnp.exp(s-top)
            tot=tot+jnp.sum(e,axis=1,keepdims=True)
            o=o+contract(e.astype(BF16),canon[pl.ds(ks,kn),256:384],1,0)
        o=join_heads(o*(1.0/tot))
        of[pl.ds(start,size),:]=o
        l=top+jnp.log(tot)
        lse[pl.ds(start,size),:]=join_heads(jnp.broadcast_to(l,(2*size,128)))
    t=tri(256)
    for b in range(4):
        parts=[(b*256,256,t)]
        if b: parts.insert(0,(0,b*256,None))
        rows(b*256,256,parts)
    bm=branch_mask()
    def branch(b,_):
        st=pl.multiple_of(TRUNK+b*BRANCH,PIECE)
        rows(st,BRANCH,[(0,TRUNK,None),(st,BRANCH,bm)])
        return 0
    lax.fori_loop(0,4,branch,0)
    for i in range(n_p):
        dst=pl.ds(pl.multiple_of(order[i]*PIECE,PIECE),PIECE)
        att[dst,:]=of[i*PIECE:(i+1)*PIECE,:].astype(BF16)
    s=contract(q16[...],qkv[:,384:512],1,1)
    s=jnp.where(allowed_mask(qinfo,kinfo),s,NEGATIVE)
    top=jnp.max(s,axis=1,keepdims=True)
    e=jnp.exp(s-top)
    tot=jnp.sum(e,axis=1,keepdims=True)
    o=contract(e.astype(BF16),qkv[:,384:512],1,0)*(1.0/tot)
    of16[...]=o
    att16[...]=pltpu.roll(o,64,1).astype(BF16)
    lse16[...]=jnp.broadcast_to(top+jnp.log(tot),o.shape)

def allowed_mask(qinfo,kinfo):
    ks=kinfo[0:1,:]; kp=kinfo[1:2,:]
    return ((ks==qinfo[:,0:1])|(ks==qinfo[:,1:2])|(ks==qinfo[:,2:3]))&(kp<=qinfo[:,3:4])

def attention_forward(order,qkv,q16,qinfo,kinfo):
    n=qkv.shape[0]; r=q16.shape[0]
    sd=jax.ShapeDtypeStruct
    V=pl.BlockSpec(memory_space=pltpu.VMEM)
    return pl.pallas_call(fwd_kernel,
        in_specs=[pl.BlockSpec(memory_space=pltpu.SMEM)]+[V]*4,
        out_specs=[V]*7,
        out_shape=[sd((n,128),BF16),sd((r,128),BF16),sd((n,384),BF16),sd((n,128),F32),sd((n,128),F32),sd((r,128),F32),sd((r,128),F32)],
        compiler_params=pltpu.CompilerParams(vmem_limit_bytes=32<<20),
        cost_estimate=pl.CostEstimate(flops=20_000_000_000,bytes_accessed=8_000_000,transcendentals=7_000_000),
        name="tree_attention_forward",
    )(order,qkv,q16,qinfo,kinfo)

def bwd_kernel(order, canon, of, lse, datt, kv16, q16, of16, lse16, datt16, qinfo, kinfo, dqkv, dq16, dc, dacc):
    n_p=canon.shape[0]//PIECE
    for i in range(n_p):
        src=pl.ds(pl.multiple_of(order[i]*PIECE,PIECE),PIECE)
        dc[i*PIECE:(i+1)*PIECE,:]=datt[src,:]
    def rows(start,size,parts):
        r=pl.ds(start,size)
        qh=split_heads(canon[r,0:128])
        d=dc[r,:]
        dh=split_heads(d)
        prod=d.astype(F32)*of[r,:]
        delta=jnp.concatenate([jnp.sum(prod[:,0:64],axis=1,keepdims=True),jnp.sum(prod[:,64:128],axis=1,keepdims=True)],axis=0)
        l=jnp.concatenate([lse[r,0:1],lse[r,64:65]],axis=0)
        dq=0.
        for ks,kn,mask,first in parts:
            kk=canon[pl.ds(ks,kn),128:256]
            s=contract(qh,kk,1,1)
            if mask is not None:
                s=jnp.where(jnp.concatenate([mask,mask],axis=0),s,NEGATIVE)
            p=jnp.exp(s-l)
            dp=contract(dh,canon[pl.ds(ks,kn),256:384],1,1)
            ds=(p*(dp-delta)).astype(BF16)
            dv=contract(p.astype(BF16),dh,0,0)
            dk=contract(ds,qh,0,0)
            dq=dq+contract(ds,kk,1,0)
            if first:
                dacc[pl.ds(ks,kn),128:256]=dk
                dacc[pl.ds(ks,kn),256:384]=dv
            else:
                dacc[pl.ds(ks,kn),128:256]+=dk
                dacc[pl.ds(ks,kn),256:384]+=dv
        dacc[r,0:128]=join_heads(dq)
    t=tri(256)
    for b in range(4):
        parts=[(b*256,256,t,True)]
        if b: parts.insert(0,(0,b*256,None,False))
        rows(b*256,256,parts)
    bm=branch_mask()
    def branch(b,_):
        st=pl.multiple_of(TRUNK+b*BRANCH,PIECE)
        rows(st,BRANCH,[(0,TRUNK,None,False),(st,BRANCH,bm,True)])
        return 0
    lax.fori_loop(0,4,branch,0)
    for i in range(n_p):
        dst=pl.ds(pl.multiple_of(order[i]*PIECE,PIECE),PIECE)
        x=dacc[i*PIECE:(i+1)*PIECE,:]
        dqkv[dst,0:128]=(x[:,0:128]*0.125).astype(BF16)
        dqkv[dst,128:384]=x[:,128:384].astype(BF16)
    k16=kv16[:,384:512]
    s=contract(q16[...],k16,1,1)
    s=jnp.where(allowed_mask(qinfo,kinfo),s,NEGATIVE)
    p=jnp.exp(s-lse16[:,0:1])
    dp=contract(datt16[...],k16,1,1)
    delta=jnp.sum(datt16[...].astype(F32)*of16[...],axis=1,keepdims=True)
    ds=(p*(dp-delta)).astype(BF16)
    dqkv[:,384:512]=(contract(ds,q16[...],0,0)+contract(p.astype(BF16),datt16[...],0,0)).astype(BF16)
    lane=lax.broadcasted_iota(jnp.int32,(1,128),1)>=64
    dq=pltpu.roll(contract(ds,k16,1,0)*0.125,64,1)
    dq16[...]=jnp.where(lane,dq,0.0).astype(BF16)

def attention_backward(order,canon,of,lse,datt,qkv,q16,of16,lse16,datt16,qinfo,kinfo):
    n=canon.shape[0]; r=q16.shape[0]
    sd=jax.ShapeDtypeStruct
    V=pl.BlockSpec(memory_space=pltpu.VMEM)
    return pl.pallas_call(bwd_kernel,
        in_specs=[pl.BlockSpec(memory_space=pltpu.SMEM)]+[V]*11,
        out_specs=[V]*2,
        out_shape=[sd((n,512),BF16),sd((r,128),BF16)],
        scratch_shapes=[pltpu.VMEM((n,128),BF16),pltpu.VMEM((n,384),F32)],
        compiler_params=pltpu.CompilerParams(vmem_limit_bytes=40<<20),
        cost_estimate=pl.CostEstimate(flops=50_000_000_000,bytes_accessed=15_000_000,transcendentals=7_000_000),
        name="tree_attention_backward",
    )(order,canon,of,lse,datt,qkv,q16,of16,lse16,datt16,qinfo,kinfo)


def parent_lookup(identities, shifted_table):
    labels = jnp.arange(shifted_table.shape[0], dtype=jnp.int32)
    matches = identities[:, None] == labels[None, :]
    return jnp.sum(jnp.where(matches, shifted_table[None, :], 0), axis=1) - 1


def tree_order(segments, places, parent):
    own = segments.reshape(-1, PIECE)[:, 0]
    start = places.reshape(-1, PIECE)[:, 0]
    table = parent + 1
    first_up = parent_lookup(own, table)
    second_up = parent_lookup(first_up, table)
    is_branch = (first_up >= 0) & (second_up < 0)
    is_leaf = second_up >= 0
    branch = jnp.where(is_leaf, first_up, own)
    rank = jnp.sum((is_branch[None, :] & (own[None, :] < branch[:, None])).astype(jnp.int32), axis=1)
    twin = is_leaf[None, :] & (first_up[None, :] == first_up[:, None]) & (own[None, :] < own[:, None])
    leaf = 1 + jnp.sum(twin.astype(jnp.int32), axis=1)
    target = jnp.where(
        first_up < 0, start // PIECE, TRUNK // PIECE + 3 * rank + jnp.where(is_leaf, leaf, 0)
    )
    pieces = jnp.arange(own.shape[0], dtype=jnp.int32)
    order = jnp.sum(jnp.where(target[None, :] == pieces[:, None], pieces[None, :], 0), axis=1)
    return order, first_up, second_up


def local(
    tokens,
    cotangent,
    segment_of,
    position_of,
    parent,
    ln1_gain,
    ln1_bias,
    w_qkv,
    b_query,
    b_value,
    w_out,
    b_out,
    ln2_gain,
    ln2_bias,
    w_fc,
    b_fc,
    w_proj,
    b_proj,
):
    rows = tokens.shape[0]
    half = w_qkv.shape[0]
    shard = lax.axis_index("shard")
    tensor, context, me = place()
    members = 2 * lax.axis_size("tensor")
    tree_rows = members * rows
    low = shard == 0

    vectors = jnp.stack(
        [ln1_gain, ln1_bias, b_query, b_value, b_out, ln2_gain, ln2_bias, b_proj]
    ).astype(F32)
    zeros = jnp.zeros_like(vectors)
    half_vectors = jnp.concatenate(
        [jnp.where(low, vectors, zeros), jnp.where(low, zeros, vectors)], axis=1
    )
    proj_mine = w_proj.T
    normed_all, mixed, query_last, vectors, weight, fc_other = project(tokens, w_qkv, half_vectors, w_fc)
    proj_give, cotangent_give, mixed = lax.optimization_barrier((proj_mine, cotangent, mixed))
    proj_other = swap(proj_give, "shard", 0)
    cotangent_far = swap(cotangent_give, "tensor", 1)

    tree_start = lax.div(context, 2) * tree_rows
    segments = lax.dynamic_slice_in_dim(segment_of, tree_start, tree_rows)
    places = lax.dynamic_slice_in_dim(position_of, tree_start, tree_rows)
    order, first_up, second_up = tree_order(segments, places, parent)
    key_info = jnp.stack([segments, places])
    query_info = jnp.stack(
        [segments, jnp.repeat(first_up, PIECE), jnp.repeat(second_up, PIECE), places], axis=1
    )
    query_info = lax.dynamic_slice_in_dim(query_info, me * rows, rows, 0)

    gain_one = vectors[0]
    attended_pair, attended_last, sorted_qkv, exact, level, exact_last, level_last = attention_forward(
        order, mixed, query_last, query_info, key_info
    )
    residual, fed_give, d_middle, d_pair, d_last, joint_keep, joint_give, fc_keep, fc_give, proj_sum, sums = feed_forward(
        attended_pair,
        attended_last,
        tokens,
        cotangent,
        cotangent_far,
        w_out,
        w_fc,
        fc_other,
        proj_mine,
        proj_other,
        vectors,
        b_fc.astype(F32)[None, :],
    )

    fc_got = swap(fc_give, "shard", 0)
    joint_other = swap(joint_give, "tensor", 1)
    proj_sum = lax.psum(proj_sum, "context")

    d_mixed, d_query_last = attention_backward(
        order, sorted_qkv, exact, level, d_pair, mixed, query_last, exact_last, level_last, d_last,
        query_info, key_info,
    )
    fc_got, joint_other, d_mixed = lax.optimization_barrier((fc_got, joint_other, d_mixed))
    fc_sum = (fc_keep.astype(F32) + fc_got.astype(F32)).astype(BF16)
    fc_sum = lax.psum(
        fc_sum, "context", axis_index_groups=[list(range(lax.axis_size("context")))[::-1]]
    )
    output, d_inputs, own_mixer, own_out, sums = finish(
        d_mixed,
        d_query_last,
        normed_all,
        weight,
        tokens,
        d_middle,
        gain_one[None, :],
        joint_keep,
        joint_other,
        sums,
        residual,
        fed_give,
    )
    proj_sum, fc_sum, sums = lax.optimization_barrier((proj_sum, fc_sum, sums))
    own_fc, own_proj = fc_sum.astype(F32), proj_sum.T.astype(F32)
    mine = lax.dynamic_slice_in_dim(sums[:8], shard * half, half, 1)
    own_bias_fc = lax.dynamic_slice_in_dim(sums, 8 + tensor, 1, 0)[0]
    return (
        output,
        d_inputs,
        mine[0],
        mine[1],
        own_mixer,
        mine[2],
        mine[3],
        own_out,
        mine[4],
        mine[5],
        mine[6],
        own_fc,
        own_bias_fc,
        own_proj,
        mine[7],
    )


def solution(mesh):
    return jax.shard_map(
        local,
        mesh=mesh,
        in_specs=(
            P(("shard", "context", "tensor"), None),
            P(("shard", "context", "tensor"), None),
            P("shard"),
            P("shard"),
            P(),
            P("shard"),
            P("shard"),
            P("shard", None),
            P("shard"),
            P("shard"),
            P("shard", None),
            P("shard"),
            P("shard"),
            P("shard"),
            P("shard", "tensor"),
            P("tensor"),
            P("tensor", "shard"),
            P("shard"),
        ),
        out_specs=(
            P(("shard", "context", "tensor"), None),
            P(("shard", "context", "tensor"), None),
            P("shard"),
            P("shard"),
            P("shard", None),
            P("shard"),
            P("shard"),
            P("shard", None),
            P("shard"),
            P("shard"),
            P("shard"),
            P("shard", "tensor"),
            P("tensor"),
            P("tensor", "shard"),
            P("shard"),
        ),
        check_vma=False,
    )
```

```python
import functools

import jax
import jax.numpy as jnp
from jax import lax
from jax.experimental import pallas as pl
from jax.experimental.pallas import tpu as pltpu
from jax.sharding import PartitionSpec as P

HEAD_DIM = 64
PAIR = 2 * HEAD_DIM
PIECE = 128
TRUNK = 8 * PIECE
BRANCH = 3 * PIECE
EPSILON = 1e-05
NEGATIVE = -1e30
F32 = jnp.float32
BF16 = jnp.bfloat16
VMEM = pl.BlockSpec(memory_space=pltpu.VMEM)
SMEM = pl.BlockSpec(memory_space=pltpu.SMEM)
ANY = pl.BlockSpec(memory_space=pl.ANY)
MESH = pl.DeviceIdType.MESH


def contract(left, right, left_dim, right_dim):
    return lax.dot_general(
        left, right, (((left_dim,), (right_dim,)), ((), ())), preferred_element_type=F32
    )


def flip(value, bit):
    low = 1 << bit
    return value + low - 2 * low * lax.rem(lax.div(value, low), 2)


def place():
    tensor, context = lax.axis_index("tensor"), lax.axis_index("context")
    return tensor, context, lax.rem(context, 2) * lax.axis_size("tensor") + tensor


def member(mask):
    tensor, context, _ = place()
    size = lax.axis_size("tensor")
    bits = size.bit_length() - 1
    for bit in range(bits):
        if mask >> bit & 1:
            tensor = flip(tensor, bit)
    if mask >> bits & 1:
        context = flip(context, 0)
    return {"context": context, "tensor": tensor}, lax.rem(context, 2) * size + tensor


def swap(value, axis, bit):
    size = lax.axis_size(axis)
    return lax.ppermute(value, axis, [(i, i ^ 1 << bit) for i in range(size)])


class Wires:
    def __init__(self, send, recv):
        self.send, self.recv, self.used = send, recv, 0

    def start(self, source, target, device):
        assert self.used < self.send.shape[0]
        copy = pltpu.make_async_remote_copy(
            src_ref=source,
            dst_ref=target,
            send_sem=self.send.at[self.used],
            recv_sem=self.recv.at[self.used],
            device_id=device,
            device_id_type=MESH,
        )
        self.used += 1
        copy.start()
        return copy


def by_rows(rows, step, body, first=0):
    def run(i, carry):
        body(pl.ds(pl.multiple_of(first + i * step, step), step))
        return carry

    lax.fori_loop(0, rows // step, run, 0)


def norm_backward(values, grad, gain):
    average = jnp.mean(values, axis=1, keepdims=True)
    centered = values - average
    inverse = lax.rsqrt(jnp.mean(centered * centered, axis=1, keepdims=True) + EPSILON)
    normal = centered * inverse
    scaled = grad * gain
    result = inverse * (
        scaled
        - jnp.mean(scaled, axis=1, keepdims=True)
        - normal * jnp.mean(scaled * normal, axis=1, keepdims=True)
    )
    return result, jnp.sum(grad * normal, axis=0, keepdims=True), jnp.sum(grad, axis=0, keepdims=True)


def norm_forward(values, gain, shift):
    average = jnp.mean(values, axis=1, keepdims=True)
    centered = values - average
    spread = jnp.mean(centered * centered, axis=1, keepdims=True)
    return centered * lax.rsqrt(spread + EPSILON) * gain + shift


def project_kernel(
    tokens, w_all, half_vectors, w_fc, normed, mixed, query_last, vectors, weight, fc_other, everyone, w_qkv, seen, local_sem, send, recv
):
    tensor, context, me = place()
    shard = lax.axis_index("shard")
    members = 2 * lax.axis_size("tensor")
    rows, width = tokens.shape
    half = width // 2
    cut = rows // 2
    shared = width - HEAD_DIM
    across = {"shard": 1 - shard}
    wires = Wires(send, recv)
    turn = members // 2

    load = pltpu.make_async_copy(w_all, w_qkv, local_sem.at[1])
    load.start()
    barrier = pltpu.get_barrier_semaphore()
    peers = [member(mask)[0] for mask in (1, 2, turn)] + [across]
    rest = [m for m in range(4, members) if m & 1 == 0 and m not in (turn, turn + 2)]
    for peer in peers:
        pl.semaphore_signal(barrier, inc=1, device_id=peer, device_id_type=MESH)
    pl.semaphore_wait(barrier, len(peers))
    assert not rest

    def slot(owner, first=0, size=rows):
        index = member(owner)[1] * rows + first
        return everyone.at[pl.ds(pl.multiple_of(index, 16), size)]

    def hand(source, target):
        return wires.start(source, source, member(target)[0])

    own = pltpu.make_async_copy(tokens, slot(0), local_sem.at[0])
    own.start()
    far = {m: wires.start(tokens, slot(0), member(m)[0]) for m in (2, turn)}
    vector_wire = wires.start(half_vectors, seen, across)
    close = {0: wires.start(tokens, slot(0), member(1)[0])}
    lane = lax.broadcasted_iota(jnp.int32, (1, PAIR), 1) < HEAD_DIM

    def choose(i, carry):
        r = pl.ds(pl.multiple_of(i * 32, 32), 32)
        to = pl.ds(pl.multiple_of(shard * half + i * 32, 32), 32)

        def window(start, size=PAIR):
            return w_qkv[r, pl.ds(pl.multiple_of(start, PAIR), size)]

        def turned(value):
            return pltpu.roll(value.astype(F32), HEAD_DIM, 1)

        weight[to, 0:PAIR] = window(me * PAIR)
        left, right = window(shared + me * PAIR), window(shared + (me + 1) * PAIR)
        weight[to, PAIR : 2 * PAIR] = jnp.where(lane, turned(left), turned(right)).astype(BF16)
        weight[to, 2 * PAIR : 3 * PAIR] = window(2 * width + me * PAIR)
        value = w_qkv[r, 2 * width + shared :]
        value = jnp.concatenate([value, value], axis=1)
        key = turned(w_qkv[r, 2 * width - PAIR : 2 * width])
        weight[to, 3 * PAIR : 4 * PAIR] = jnp.where(lane, key, value.astype(F32)).astype(BF16)
        query = w_qkv[r, shared : shared + PAIR]
        weight[to, 4 * PAIR :] = jnp.where(lane, query, jnp.zeros_like(query))
        return carry

    load.wait()
    lax.fori_loop(0, half // 32, choose, 0)
    chosen = weight.at[pl.ds(pl.multiple_of(shard * half, half), half)]
    weight_wire = wires.start(chosen, chosen, across)
    fc_wire = wires.start(w_fc.at[0 : half // 2], fc_other, across)

    vector_wire.wait_recv()
    vectors[...] = half_vectors[...] + seen[...]
    gain, shift = vectors[0:1, :], vectors[1:2, :]
    scale = HEAD_DIM ** (-0.5)
    pair_lanes = pl.ds(pl.multiple_of(me * PAIR, PAIR), PAIR)
    bias_query, bias_value = vectors[2:3, pair_lanes], vectors[3:4, pair_lanes]
    value_tail = vectors[3:4, shared:]
    bias_last = jnp.where(lane, 0.0, jnp.concatenate([value_tail, value_tail], axis=1))
    query_tail = vectors[2:3, shared:]
    query_tail = jnp.where(lane, jnp.concatenate([query_tail, query_tail], axis=1), 0.0)

    def normalise(owner, first=0, size=rows):
        index = member(owner)[1] * rows + first

        def run(i, carry):
            r = pl.ds(pl.multiple_of(index + i * 32, 32), 32)
            normed[r, :] = norm_forward(everyone[r, :].astype(F32), gain, shift).astype(BF16)
            return carry

        lax.fori_loop(0, size // 32, run, 0)

    def multiply(owner, first=0, size=rows):
        r = pl.ds(pl.multiple_of(member(owner)[1] * rows + first, 32), size)
        result = jnp.dot(normed[r, :], weight[:, 0 : 4 * PAIR], preferred_element_type=F32)
        mixed[r, 0:PAIR] = ((result[:, 0:PAIR] + bias_query) * scale).astype(BF16)
        mixed[r, PAIR : 2 * PAIR] = result[:, PAIR : 2 * PAIR].astype(BF16)
        mixed[r, 2 * PAIR : 3 * PAIR] = (result[:, 2 * PAIR : 3 * PAIR] + bias_value).astype(BF16)
        mixed[r, 3 * PAIR :] = (result[:, 3 * PAIR :] + bias_last).astype(BF16)

    own.wait()
    normalise(0)
    close[0].wait_recv()
    normalise(1)
    pieces = {}
    for m, other, first in ((2, turn, 0), (turn, 2, cut)):
        far[m].wait_recv()
        close[m] = hand(slot(m), 1)
        pieces[other] = hand(slot(m, first, cut), other)
    weight_wire.wait_recv()
    multiply(0)
    last = jnp.dot(
        normed[pl.ds(pl.multiple_of(me * rows, 32), rows), :], weight[:, 4 * PAIR :], preferred_element_type=F32
    )
    query_last[...] = ((last + query_tail) * scale).astype(BF16)
    multiply(1)
    for m in (2, turn):
        normalise(m)
        multiply(m)
    for m in (2, turn):
        close[m].wait_recv()
        normalise(m ^ 1)
        multiply(m ^ 1)
    opposite = 2 ^ turn
    passed = []
    for m, first in ((turn, 0), (2, cut)):
        pieces[m].wait_recv()
        passed.append(hand(slot(opposite, first, cut), 1))
    normalise(opposite)
    multiply(opposite)
    for wire in passed:
        wire.wait_recv()
    normalise(opposite ^ 1)
    multiply(opposite ^ 1)
    fc_wire.wait_recv()
    for wire in list(far.values()) + list(close.values()) + list(pieces.values()) + passed + [vector_wire, weight_wire, fc_wire]:
        wire.wait_send()


def project(tokens, w_qkv, half_vectors, w_fc):
    rows, width = tokens.shape
    tree = 2 * lax.axis_size("tensor") * rows
    shape = jax.ShapeDtypeStruct
    return pl.pallas_call(
        project_kernel,
        in_specs=[VMEM, ANY, VMEM, ANY],
        out_specs=[VMEM] * 5 + [ANY],
        out_shape=[
            shape((tree, width), BF16),
            shape((tree, 4 * PAIR), BF16),
            shape((rows, PAIR), BF16),
            shape(half_vectors.shape, F32),
            shape((width, 5 * PAIR), BF16),
            shape((w_fc.shape[0] // 2, w_fc.shape[1]), BF16),
        ],
        scratch_shapes=[
            pltpu.VMEM((tree, width), BF16),
            pltpu.VMEM(w_qkv.shape, BF16),
            pltpu.VMEM(half_vectors.shape, F32),
            pltpu.SemaphoreType.DMA((2,)),
            pltpu.SemaphoreType.DMA((16,)),
            pltpu.SemaphoreType.DMA((16,)),
        ],
        compiler_params=pltpu.CompilerParams(
            collective_id=0, has_side_effects=True, vmem_limit_bytes=32 << 20
        ),
        name="project",
    )(tokens, w_qkv, half_vectors, w_fc)


def feed_forward_kernel(
    pair,
    last,
    tokens,
    cotangent,
    cotangent_far,
    out_mine,
    fc_mine,
    fc_other,
    proj_mine,
    proj_other,
    vectors,
    bias_fc,
    residual,
    fed_give,
    d_middle,
    d_pair,
    d_last,
    joint_keep,
    joint_give,
    fc_keep,
    fc_give,
    proj_sum,
    sums,
    w_out,
    w_fc,
    w_proj,
    attended,
    middle,
    normed,
    hidden,
    d_before,
    d_hidden,
    part,
    near,
    passing,
    far,
    d_attn,
    d_attended,
    grads,
    proj_keep,
    proj_give,
    proj_got,
    joint,
    joint_near,
    local_sem,
    send,
    recv,
):
    tensor, context, me = place()
    shard = lax.axis_index("shard")
    near_bit = lax.rem(tensor, 2)
    members = 2 * lax.axis_size("tensor")
    rows, width = tokens.shape
    half = width // 2
    shared = width - HEAD_DIM
    group = range(1, members)
    wires = Wires(send, recv)
    bias_out, gain, shift, bias_proj = (vectors[i : i + 1, :] for i in (4, 5, 6, 7))
    across = {"shard": 1 - shard}

    barrier = pltpu.get_barrier_semaphore()
    peers = [member(mask)[0] for mask in group] + [across]
    for peer in peers:
        pl.semaphore_signal(barrier, inc=1, device_id=peer, device_id_type=MESH)
    pl.semaphore_wait(barrier, len(peers))

    def slab(ref, index, size):
        return ref.at[pl.ds(pl.multiple_of(index * size, size), size)]

    def beside(ref, index):
        return ref.at[:, pl.ds(pl.multiple_of(index * PAIR, PAIR), PAIR)]

    moved = []
    for mask in group:
        device, index = member(mask)
        moved.append(wires.start(slab(pair, index, rows), beside(attended, me), device))
    quarter = half // 2
    out_wire = wires.start(
        slab(out_mine, near_bit, quarter), slab(w_out, 2 * shard + near_bit, quarter), across
    )
    local = [
        pltpu.make_async_copy(source, target, local_sem.at[i])
        for i, (source, target) in enumerate(
            (
                (slab(pair, me, rows), beside(attended, me)),
                (out_mine, slab(w_out, shard, half)),
                (fc_mine, slab(w_fc, shard, half)),
                (fc_other, slab(w_fc, 2 * (1 - shard), quarter)),
                (proj_mine, slab(w_proj, shard, half)),
                (proj_other, slab(w_proj, 1 - shard, half)),
                (cotangent, slab(grads, 0, rows)),
                (cotangent_far, slab(grads, 2, rows)),
            )
        )
    ]
    pulled_wires = [
        wires.start(source, slab(grads, index, rows), member(1)[0])
        for index, source in ((1, cotangent), (3, cotangent_far))
    ]
    for copy in local:
        copy.start()
    attended[:, shared:] = last[:, 0:HEAD_DIM]
    out_wire.wait_recv()
    out_part = slab(w_out, 2 * (1 - shard) + near_bit, quarter)
    out_near = wires.start(out_part, out_part, member(1)[0])
    fc_wire = wires.start(
        fc_mine.at[quarter:half], slab(w_fc, 2 * shard + 1, quarter), across
    )
    for copy in local:
        copy.wait()
    for wire in moved + [out_near]:
        wire.wait_recv()

    start = 0
    while start < width:
        stop = min(start + 2 * PAIR, width)
        middle[:, start:stop] = (
            tokens[:, start:stop].astype(F32)
            + jnp.dot(attended[...], w_out[:, start:stop], preferred_element_type=F32)
            + bias_out[:, start:stop]
        )
        start = stop

    def second_norm(r):
        normed[r, :] = norm_forward(middle[r, :], gain, shift).astype(BF16)

    cut = rows // 2

    def piece(mask, i):
        return slice(mask * rows + i * cut, mask * rows + (i + 1) * cut)

    cross = []
    for i in range(2):
        by_rows(cut, 32, second_norm, i * cut)
        cross.append(wires.start(normed.at[piece(0, i)], normed.at[piece(2, i)], member(2)[0]))

    def block(ref, mask):
        return ref.at[mask * rows : (mask + 1) * rows, :]

    close = wires.start(block(normed, 0), block(normed, 1), member(1)[0])
    for wire in pulled_wires:
        wire.wait_recv()
    for mask in range(4):
        block(d_hidden, mask)[...] = jnp.dot(
            block(grads, mask)[...], w_proj[...], preferred_element_type=F32
        )

    def feed(r):
        start = 0
        while start < width:
            stop = min(start + 2 * PAIR, width)
            c = slice(start, stop)
            before = jnp.dot(normed[r, :], w_fc[:, c], preferred_element_type=F32) + bias_fc[0:1, c]
            cumulative = 0.5 + 0.5 * lax.erf(before * (0.5**0.5))
            hidden[r, c] = (before * cumulative).astype(BF16)
            slope = cumulative + before * jnp.exp(-0.5 * before * before) * ((2 * jnp.pi) ** -0.5)
            d_before[r, c] = (d_hidden[r, c] * slope).astype(BF16)
            start = stop

    def back(r):
        return contract(d_before[r, :], w_fc[...], 1, 1)

    def ahead(mask):
        return contract(hidden[mask * rows : (mask + 1) * rows, :], w_proj[...], 1, 1)

    fc_wire.wait_recv()
    feed(slice(0, rows))
    close.wait_recv()
    feed(slice(rows, 2 * rows))
    part[0] = back(slice(rows, 2 * rows)).astype(BF16)
    to_near = wires.start(part.at[0], near.at[0], member(1)[0])
    relay, to_pass, to_far = [], [], []
    for i in range(2):
        h = slice(i * cut, (i + 1) * cut)
        cross[i].wait_recv()
        relay.append(wires.start(normed.at[piece(2, i)], normed.at[piece(3, i)], member(1)[0]))
        feed(piece(2, i))
        relay[i].wait_recv()
        feed(piece(3, i))
        part[1, h] = back(piece(3, i)).astype(BF16)
        to_pass.append(wires.start(part.at[1, h], near.at[1, h], member(1)[0]))
        mine = back(piece(2, i))
        to_pass[i].wait_recv()
        passing[h] = (mine + near[1, h].astype(F32)).astype(BF16)
        to_far.append(wires.start(passing.at[h], far.at[h], member(2)[0]))

    other_part = pl.ds(pl.multiple_of(2 * rows + (1 - shard) * half, 8), half)
    own_part = pl.ds(pl.multiple_of(2 * rows + shard * half, 8), half)
    proj_wires = []
    start = 0
    while start < width:
        stop = min(start + 2 * PAIR, width)
        c = slice(start, stop)
        d_hidden_part = d_hidden.at[2 * rows : 2 * rows + width, 0 : stop - start]
        d_hidden_part[...] = contract(grads[...], hidden[:, c], 0, 0)
        proj_give[:, c] = d_hidden[other_part, 0 : stop - start].astype(BF16)
        proj_wires.append(wires.start(proj_give.at[:, c], proj_got.at[:, c], across))
        proj_keep[:, c] = d_hidden[own_part, 0 : stop - start]
        start = stop
    start = 0
    while start < width:
        stop = min(start + 2 * PAIR, width)
        c = slice(start, stop)
        d_hidden_part = d_hidden.at[2 * rows : 2 * rows + width, 0 : stop - start]
        d_hidden_part[...] = contract(normed[...], d_before[:, c], 0, 0)
        fc_give[:, c] = d_hidden[other_part, 0 : stop - start].astype(BF16)
        fc_keep[:, c] = d_hidden[own_part, 0 : stop - start].astype(BF16)
        start = stop
    d_hidden[0:rows, :] = back(slice(0, rows))
    to_near.wait_recv()
    for wire in to_far:
        wire.wait_recv()

    sums[...] = jnp.zeros_like(sums)

    def second_back(r):
        grad = d_hidden[r, :] + near[0, r, :].astype(F32) + far[r, :].astype(F32)
        result, by_gain, by_shift = norm_backward(middle[r, :], grad, gain)
        pulled = cotangent[r, :].astype(F32)
        result = result + pulled
        d_middle[r, :] = result
        low = result.astype(BF16)
        d_attn[r, 0:width] = low
        d_attn[r, width:] = jnp.zeros((r.size, d_attn.shape[1] - width), BF16)
        sums[4:5, :] += jnp.sum(low.astype(F32), axis=0, keepdims=True)
        sums[5:6, :] += by_gain
        sums[6:7, :] += by_shift
        sums[7:8, :] += jnp.sum(pulled, axis=0, keepdims=True)

    by_rows(rows, 64, second_back)
    start = 0
    while start < width:
        stop = min(start + 2 * PAIR, width)
        d_attended[:, start:stop] = contract(d_attn[:, 0:width], w_out[start:stop, :], 1, 1).astype(BF16)
        start = stop
    returned = []
    for mask in group:
        device, index = member(mask)
        returned.append(wires.start(beside(d_attended, index), slab(d_pair, me, rows), device))
    own_copy = pltpu.make_async_copy(beside(d_attended, me), slab(d_pair, me, rows), local_sem.at[0])
    own_copy.start()
    lane = lax.broadcasted_iota(jnp.int32, (1, PAIR), 1) >= HEAD_DIM
    tail = jnp.concatenate([d_attended[:, shared:]] * 2, axis=1)
    d_last[...] = jnp.where(lane, tail, jnp.zeros_like(tail))
    joint[:, shared : shared + PAIR] = jnp.zeros((width, PAIR), BF16)
    start = 0
    while start < d_attn.shape[1]:
        stop = min(start + 2 * PAIR, d_attn.shape[1])
        to = start if start < shared else start + PAIR
        joint[:, to : to + stop - start] = contract(attended[...], d_attn[:, start:stop], 0, 0).astype(BF16)
        start = stop
    side = joint.shape[1] // 2
    kept = pl.ds(pl.multiple_of(near_bit * side, side), side)
    given = pl.ds(pl.multiple_of((1 - near_bit) * side, side), side)
    joint_wire = wires.start(joint.at[:, given], joint_near, member(1)[0])
    part[2] = ahead(3).astype(BF16)
    to_pass_out = wires.start(part.at[2], near.at[3], member(1)[0])
    part[3] = ahead(1).astype(BF16)
    to_near_out = wires.start(part.at[3], near.at[2], member(1)[0])
    d_hidden[2 * rows : 3 * rows, :] = ahead(2)
    d_hidden[rows : 2 * rows, :] = ahead(0)
    bias = jnp.zeros((1, width), F32)

    def add_bias(i, total):
        r = pl.ds(pl.multiple_of(i * 64, 64), 64)
        return total + jnp.sum(d_before[r, :].astype(F32), axis=0, keepdims=True)

    bias = lax.fori_loop(0, 4 * rows // 64, add_bias, bias)
    for i in range(lax.axis_size("tensor")):
        sums[8 + i : 9 + i, :] = jnp.where(tensor == i, bias, 0.0)
    to_near_out.wait_recv()
    to_pass_out.wait_recv()

    def finish_output(r):
        third = pl.ds(pl.multiple_of(2 * rows + r.start, 64), r.size)
        again = pl.ds(pl.multiple_of(rows + r.start, 64), r.size)
        fed_give[r, :] = (d_hidden[third, :] + near[3, r, :].astype(F32)).astype(BF16)
        residual[r, :] = middle[r, :] + d_hidden[again, :] + near[2, r, :].astype(F32) + bias_proj

    by_rows(rows, 64, finish_output)
    joint_wire.wait_recv()
    second = lax.rem(lax.div(tensor, 2), 2)

    def add_joint(target, which):
        for i in range(2):

            def run(r):
                source = pl.ds(pl.multiple_of((2 * i + which) * quarter - i * quarter + r.start, 16), r.size)
                total = joint[source, kept].astype(F32) + joint_near[source, :].astype(F32)
                target[r, :] = total.astype(BF16)

            by_rows(quarter, 16, run, i * quarter)

    add_joint(joint_keep, second)
    add_joint(joint_give, 1 - second)
    for wire in proj_wires:
        wire.wait_recv()

    def add_proj(r):
        proj_sum[r, :] = (proj_keep[r, :] + proj_got[r, :].astype(F32)).astype(BF16)

    by_rows(half, 32, add_proj)
    own_copy.wait()
    for wire in returned:
        wire.wait_recv()
    for wire in (
        moved + returned + [out_wire, out_near, fc_wire] + pulled_wires + proj_wires
        + cross + relay + to_pass + to_far + [joint_wire, close, to_near, to_near_out, to_pass_out]
    ):
        wire.wait_send()


def feed_forward(pair, last, tokens, cotangent, cotangent_far, out_mine, fc_mine, fc_other, proj_mine, proj_other, vectors, bias_fc):
    rows, width = tokens.shape
    members = 2 * lax.axis_size("tensor")
    hidden = fc_mine.shape[1]
    tall = 4 * rows
    shape = jax.ShapeDtypeStruct
    return pl.pallas_call(
        feed_forward_kernel,
        in_specs=[ANY] + [VMEM] * 4 + [ANY] * 5 + [VMEM] * 2,
        out_specs=[VMEM] * 3 + [ANY] + [VMEM] * 7,
        out_shape=[
            shape((rows, width), F32),
            shape((rows, width), BF16),
            shape((rows, width), F32),
            shape((members * rows, PAIR), BF16),
            shape((rows, PAIR), BF16),
            shape((width // 2, 5 * PAIR), BF16),
            shape((width // 2, 5 * PAIR), BF16),
            shape((width // 2, hidden), BF16),
            shape((width // 2, hidden), BF16),
            shape((width // 2, hidden), BF16),
            shape((16, width), F32),
        ],
        scratch_shapes=[
            pltpu.VMEM((width, width), BF16),
            pltpu.VMEM((width, hidden), BF16),
            pltpu.VMEM((width, hidden), BF16),
            pltpu.VMEM((rows, width), BF16),
            pltpu.VMEM((rows, width), F32),
            pltpu.VMEM((tall, width), BF16),
            pltpu.VMEM((tall, hidden), BF16),
            pltpu.VMEM((tall, hidden), BF16),
            pltpu.VMEM((2 * rows + max(2 * rows, width), hidden), F32),
            pltpu.VMEM((4, rows, width), BF16),
            pltpu.VMEM((4, rows, width), BF16),
            pltpu.VMEM((rows, width), BF16),
            pltpu.VMEM((rows, width), BF16),
            pltpu.VMEM((rows, 9 * PAIR), BF16),
            pltpu.VMEM((rows, width), BF16),
            pltpu.VMEM((tall, width), BF16),
            pltpu.VMEM((width // 2, hidden), F32),
            pltpu.VMEM((width // 2, hidden), BF16),
            pltpu.VMEM((width // 2, hidden), BF16),
            pltpu.VMEM((width, 10 * PAIR), BF16),
            pltpu.VMEM((width, 5 * PAIR), BF16),
            pltpu.SemaphoreType.DMA((8,)),
            pltpu.SemaphoreType.DMA((2 * members + 24,)),
            pltpu.SemaphoreType.DMA((2 * members + 24,)),
        ],
        compiler_params=pltpu.CompilerParams(
            collective_id=3, has_side_effects=True, vmem_limit_bytes=62 << 20
        ),
        name="feed_forward",
    )(pair, last, tokens, cotangent, cotangent_far, out_mine, fc_mine, fc_other, proj_mine, proj_other, vectors, bias_fc)


def finish_kernel(
    d_mixed,
    d_query_last,
    normed,
    weight,
    tokens,
    d_middle,
    gain,
    joint_keep,
    joint_other,
    vectors,
    residual,
    fed_other,
    output,
    d_tokens,
    pairs,
    joint_all,
    sums,
    near_give,
    near_got,
    row_sum,
    second_got,
    turn_last,
    last_low,
    pair_t,
    pair,
    pair_give,
    pair_got,
    pair_low,
    pair_seen,
    tail,
    tail_near,
    tail_sum,
    tail_give,
    tail_got,
    joint_give,
    joint_got,
    half_low,
    half_seen,
    pair_sum,
    half_sum,
    vec,
    vec_give,
    vec_got,
    send,
    recv,
):
    tensor, context, me = place()
    shard = lax.axis_index("shard")
    near = lax.rem(tensor, 2)
    second = lax.rem(lax.div(tensor, 2), 2)
    contexts = lax.axis_size("context")
    members = 2 * lax.axis_size("tensor")
    turn = members // 2
    rows, width = tokens.shape
    half = width // 2
    quarter = half // 2
    side = joint_keep.shape[1]
    shared = width - HEAD_DIM
    block = 4 * PAIR
    across = {"shard": 1 - shard}
    higher = [
        {"context": flip(context, bit)} for bit in range(1, contexts.bit_length() - 1)
    ]
    group = range(1, members)
    wires = Wires(send, recv)

    barrier = pltpu.get_barrier_semaphore()
    peers = [member(mask)[0] for mask in group] + [across] + higher
    for peer in peers:
        pl.semaphore_signal(barrier, inc=1, device_id=peer, device_id_type=MESH)
    pl.semaphore_wait(barrier, len(peers))

    def part(ref, index, size):
        return ref.at[pl.ds(pl.multiple_of(index * size, size), size)]

    def term(mask):
        r = pl.ds(pl.multiple_of(member(mask)[1] * rows, rows), rows)
        return contract(d_mixed[r, :], weight[:, 0:block], 1, 1)

    steps = d_mixed.shape[0] // (2 * rows)
    pair_t[...] = jnp.zeros_like(pair_t)

    def accumulate(i, carry):
        r = pl.ds(pl.multiple_of(i * 2 * rows, 2 * rows), 2 * rows)
        pair_t[...] += contract(d_mixed[r, :], normed[r, :], 0, 0)
        return carry

    lax.fori_loop(0, steps, accumulate, 0)
    pair[...] = pair_t[...].T
    other = pl.ds(pl.multiple_of((1 - shard) * half, half), half)
    own = pl.ds(pl.multiple_of(shard * half, half), half)
    pair_give[...] = pair[other, 0 : 3 * PAIR].astype(BF16)
    pair_wire = wires.start(pair_give, pair_got, across)
    mine = pl.ds(pl.multiple_of(me * rows, rows), rows)
    tail[:, 0:PAIR] = pair[:, 3 * PAIR :].astype(BF16)
    tail[:, PAIR:] = contract(d_query_last[...], normed[mine, :], 0, 0).T.astype(BF16)
    tail_near_wire = wires.start(tail, tail_near, member(1)[0])

    order = [6, 2, 4, 0]
    near_wires = {}
    for i, mask in enumerate(order):
        near_give[i] = term(mask ^ 1).astype(BF16)
        near_wires[mask] = wires.start(near_give.at[i], near_got.at[i], member(1)[0])

    tail_near_wire.wait_recv()

    def add_tail_near(r):
        tail_sum[r, :] = tail[r, :].astype(F32) + tail_near[r, :].astype(F32)

    by_rows(width, 64, add_tail_near)
    to_second, to_turn = member(2)[0], member(turn)[0]
    for i in range(2):
        source = pl.ds(pl.multiple_of(i * half + (1 - second) * quarter, 16), quarter)
        tail_give[i * quarter : (i + 1) * quarter, :] = tail_sum[source, :].astype(BF16)
    tail_wire = wires.start(tail_give, tail_got, to_second)

    second_wires = []
    for i, mask in enumerate(order):
        total = term(mask)
        if mask == 0:
            query = pltpu.roll(d_query_last[...].astype(F32), HEAD_DIM, 1).astype(BF16)
            total = total + contract(query, weight[:, block:], 1, 1)
        near_wires[mask].wait_recv()
        total = total + near_got[i].astype(F32)
        if i >= 2:
            row_sum[i - 2] = total
        if mask & 2:
            near_got[i] = total.astype(BF16)
            second_wires.append(wires.start(near_got.at[i], second_got.at[i], to_second))

    pair_wire.wait_recv()
    pair_own = pair[own, 0 : 3 * PAIR] + pair_got[...].astype(F32)
    pair_wires = []
    for i, device in enumerate(higher):
        pair_low[i] = pair_own.astype(BF16)
        wire = wires.start(pair_low.at[i], pair_seen.at[i], device)
        pair_wires.append(wire)
        if i < len(higher) - 1:
            wire.wait_recv()
            pair_own = pair_own + pair_seen[i].astype(F32)
    pair_sum[...] = pair_own

    tail_wire.wait_recv()
    wide = joint_keep.shape[1] - 2 * PAIR

    def joint_term(which):
        r = pl.ds(pl.multiple_of(which * quarter, quarter), quarter)
        s = pl.ds(pl.multiple_of(which * half + second * quarter, quarter), quarter)
        total = joint_keep[r, :].astype(F32) + joint_other[r, :].astype(F32)
        last = jnp.where(near == 1, tail_sum[s, :] + tail_got[r, :].astype(F32), 0.0)
        return jnp.concatenate([total[:, :wide], total[:, wide:] + last], axis=1)

    joint_give[...] = joint_term(1 - shard).astype(BF16)
    joint_wire = wires.start(joint_give, joint_got, across)

    vec[...] = vectors[...]

    def add_columns(i, total):
        r = pl.ds(pl.multiple_of(i * 64, 64), 64)
        return total + jnp.sum(d_mixed[r, :].astype(F32), axis=0, keepdims=True)

    columns = lax.fori_loop(0, d_mixed.shape[0] // 64, add_columns, jnp.zeros((1, block), F32))
    pair_lanes = pl.ds(pl.multiple_of(me * PAIR, PAIR), PAIR)
    vec[2:3, pair_lanes] = columns[:, 0:PAIR]
    vec[3:4, pair_lanes] = columns[:, 2 * PAIR : 3 * PAIR]
    query = jnp.sum(d_query_last[...].astype(F32), axis=0, keepdims=True)
    vec[2:3, shared:] = pltpu.roll(query, HEAD_DIM, 1)[:, :HEAD_DIM]
    vec[3:4, shared:] = pltpu.roll(columns[:, 3 * PAIR :], HEAD_DIM, 1)[:, :HEAD_DIM]


    def add_fed(r):
        output[r, :] = (residual[r, :] + fed_other[r, :].astype(F32)).astype(BF16)

    by_rows(rows, 64, add_fed)

    joint_wire.wait_recv()
    half_sum[...] = joint_term(shard) + joint_got[...].astype(F32)
    hops = [to_turn] + higher
    joint_wires = []

    def joint_hop(i):
        if i:
            joint_wires[-1].wait_recv()
            half_sum[...] += half_seen[i - 1].astype(F32)
        if i < len(hops):
            half_low[i] = half_sum[...].astype(BF16)
            joint_wires.append(wires.start(half_low.at[i], half_seen.at[i], hops[i]))

    joint_hop(0)

    second_wires[0].wait_recv()
    last_low[...] = (row_sum[0] + second_got[0].astype(F32)).astype(BF16)
    turn_wire = wires.start(last_low, turn_last, to_turn)

    for i in range(1, len(hops)):
        joint_hop(i)

    if pair_wires:
        pair_wires[-1].wait_recv()
        pair_sum[...] += pair_seen[len(higher) - 1].astype(F32)

    def slot(owner, start=0, size=half):
        return pairs.at[pl.ds(pl.multiple_of(member(owner)[1] * half + start, 16), size)]

    def hand(source, target):
        return wires.start(source, source, member(target)[0])

    pairs[pl.ds(pl.multiple_of(me * half, half), half), :] = pair_sum[...].astype(BF16)
    far = {mask: hand(slot(0), mask) for mask in (turn, 2)}
    close = {0: hand(slot(0), 1)}

    second_wires[1].wait_recv()
    turn_wire.wait_recv()

    def first_norm(r):
        grad = row_sum[1, r, :] + second_got[1, r, :].astype(F32) + turn_last[r, :].astype(F32)
        result, by_gain, by_shift = norm_backward(tokens[r, :].astype(F32), grad, gain[0:1, :])
        d_tokens[r, :] = result + d_middle[r, :]
        vec[0:1, :] += by_gain
        vec[1:2, :] += by_shift

    by_rows(rows, 64, first_norm)
    vec_wires = []

    def vec_send(i, device):
        vec_give[i] = vec[...]
        vec_wires.append(wires.start(vec_give.at[i], vec_got.at[i], device))

    def vec_add():
        i = len(vec_wires) - 1
        vec_wires[i].wait_recv()
        vec[...] += vec_got[i]

    vec_stops = [member(1)[0], to_second, to_turn, across] + higher
    vec_send(0, vec_stops[0])

    opposite = 2 ^ turn
    far[turn].wait_recv()
    far[opposite] = hand(slot(turn), 2)
    close[turn] = hand(slot(turn), 1)
    far[2].wait_recv()
    close[2] = hand(slot(2), 1)
    vec_add()
    vec_send(1, vec_stops[1])

    joint_hop(len(hops))
    keep = pl.ds(pl.multiple_of(second * quarter, quarter), quarter)
    kept = pl.ds(pl.multiple_of(near * side, side), side)
    joint_all[keep, kept] = half_sum[...].astype(BF16)
    joint_mine = joint_all.at[keep, kept]
    back = wires.start(joint_mine, joint_mine, to_second)
    vec_add()
    vec_send(2, vec_stops[2])
    far[opposite].wait_recv()
    close[opposite] = hand(slot(opposite), 1)
    vec_add()
    vec_send(3, vec_stops[3])
    back.wait_recv()
    joint_side = joint_all.at[:, kept]
    back_near = wires.start(joint_side, joint_side, member(1)[0])
    vec_add()
    for i in range(4, len(vec_stops)):
        vec_send(i, vec_stops[i])
        vec_add()
    sums[...] = vec[...]
    for wire in close.values():
        wire.wait_recv()
    back_near.wait_recv()

    for wire in (
        [pair_wire, tail_near_wire, tail_wire, joint_wire, back, back_near]
        + list(near_wires.values()) + second_wires + [turn_wire] + pair_wires + list(far.values())
        + list(close.values()) + joint_wires + vec_wires
    ):
        wire.wait_send()


def finish(d_mixed, d_query_last, normed, weight, tokens, d_middle, gain, joint_keep, joint_other, vectors, residual, fed_other):
    rows, width = tokens.shape
    half = width // 2
    members = 2 * lax.axis_size("tensor")
    higher = lax.axis_size("context").bit_length() - 2
    side = joint_keep.shape[1]
    tall = vectors.shape[0]
    scratch = [
        pltpu.VMEM((4, rows, width), BF16),
        pltpu.VMEM((4, rows, width), BF16),
        pltpu.VMEM((2, rows, width), F32),
        pltpu.VMEM((2, rows, width), BF16),
        pltpu.VMEM((rows, width), BF16),
        pltpu.VMEM((rows, width), BF16),
        pltpu.VMEM((4 * PAIR, width), F32),
        pltpu.VMEM((width, 4 * PAIR), F32),
        pltpu.VMEM((half, 3 * PAIR), BF16),
        pltpu.VMEM((half, 3 * PAIR), BF16),
        pltpu.VMEM((max(higher, 1), half, 3 * PAIR), BF16),
        pltpu.VMEM((max(higher, 1), half, 3 * PAIR), BF16),
        pltpu.VMEM((width, 2 * PAIR), BF16),
        pltpu.VMEM((width, 2 * PAIR), BF16),
        pltpu.VMEM((width, 2 * PAIR), F32),
        pltpu.VMEM((half, 2 * PAIR), BF16),
        pltpu.VMEM((half, 2 * PAIR), BF16),
        pltpu.VMEM((half // 2, side), BF16),
        pltpu.VMEM((half // 2, side), BF16),
        pltpu.VMEM((higher + 1, half // 2, side), BF16),
        pltpu.VMEM((higher + 1, half // 2, side), BF16),
        pltpu.VMEM((half, 3 * PAIR), F32),
        pltpu.VMEM((half // 2, side), F32),
        pltpu.VMEM((tall, width), F32),
        pltpu.VMEM((higher + 4, tall, width), F32),
        pltpu.VMEM((higher + 4, tall, width), F32),
        pltpu.SemaphoreType.DMA((3 * members + 3 * higher + 20,)),
        pltpu.SemaphoreType.DMA((3 * members + 3 * higher + 20,)),
    ]
    return pl.pallas_call(
        finish_kernel,
        in_specs=[VMEM] * 12,
        out_specs=[VMEM] * 5,
        out_shape=[
            jax.ShapeDtypeStruct((rows, width), BF16),
            jax.ShapeDtypeStruct((rows, width), F32),
            jax.ShapeDtypeStruct((members * half, 3 * PAIR), BF16),
            jax.ShapeDtypeStruct((half, 2 * side), BF16),
            jax.ShapeDtypeStruct((tall, width), F32),
        ],
        scratch_shapes=scratch,
        compiler_params=pltpu.CompilerParams(
            collective_id=6, has_side_effects=True, vmem_limit_bytes=63 << 20
        ),
        name="finish",
    )(d_mixed, d_query_last, normed, weight, tokens, d_middle, gain, joint_keep, joint_other, vectors, residual, fed_other)


def write_kernel(pairs, joint, fc, own_mixer, own_out, own_fc):
    members = pairs.shape[0]
    width = own_out.shape[1]
    shared = width - HEAD_DIM
    lane = lax.broadcasted_iota(jnp.int32, (1, PAIR), 1) < HEAD_DIM

    def write(r):
        own_out[r, 0:shared] = joint[r, 0:shared].astype(F32)
        eighth = joint[r, shared : shared + PAIR].astype(F32)
        ninth = joint[r, shared + PAIR :].astype(F32)
        own_out[r, shared:] = ninth[:, :HEAD_DIM]
        own_fc[r, :] = fc[r, :].astype(F32)
        keys = []
        for k in range(members):
            value = pairs[k, r, :].astype(F32)
            own_mixer[r, k * PAIR : (k + 1) * PAIR] = value[:, 0:PAIR]
            own_mixer[r, 2 * width + k * PAIR : 2 * width + (k + 1) * PAIR] = value[:, 2 * PAIR :]
            keys.append(value[:, PAIR : 2 * PAIR])
        keys = jnp.concatenate(keys + [jnp.where(lane, eighth, ninth)], axis=1)
        own_mixer[r, shared : 2 * width] = pltpu.roll(keys, HEAD_DIM, 1)
        own_mixer[r, 2 * width + shared :] = pltpu.roll(eighth, HEAD_DIM, 1)[:, :HEAD_DIM]

    by_rows(fc.shape[0], 16, write)


def write_gradients(pairs, joint, fc):
    half, width = fc.shape
    members = pairs.shape[0] // half
    step = half // 2

    def block(*shape):
        return pl.BlockSpec(shape, lambda i: (0,) * (len(shape) - 2) + (i, 0))

    return pl.pallas_call(
        write_kernel,
        grid=(half // step,),
        in_specs=[block(members, step, 3 * PAIR), block(step, joint.shape[1]), block(step, width)],
        out_specs=[block(step, 3 * width), block(step, width), block(step, width)],
        out_shape=[
            jax.ShapeDtypeStruct((half, 3 * width), F32),
            jax.ShapeDtypeStruct((half, width), F32),
            jax.ShapeDtypeStruct((half, width), F32),
        ],
        compiler_params=pltpu.CompilerParams(vmem_limit_bytes=40 << 20),
        name="write_gradients",
    )(pairs.reshape(members, half, 3 * PAIR), joint, fc)


def tri(n):
    r=lax.broadcasted_iota(jnp.int32,(n,n),0); c=lax.broadcasted_iota(jnp.int32,(n,n),1)
    return c<=r

def branch_mask():
    r=lax.broadcasted_iota(jnp.int32,(BRANCH,BRANCH),0); c=lax.broadcasted_iota(jnp.int32,(BRANCH,BRANCH),1)
    return (c<=r)&((c<PIECE)|(c//PIECE==r//PIECE))

def split_heads(x):
    lane=lax.broadcasted_iota(jnp.int32,(1,2*64),1)<64
    z=jnp.zeros_like(x)
    return jnp.concatenate([jnp.where(lane,x,z),jnp.where(lane,z,x)],axis=0)

def join_heads(x):
    n=x.shape[0]//2
    lane=lax.broadcasted_iota(jnp.int32,(1,2*64),1)<64
    return jnp.where(lane,x[:n],x[n:])

def fwd_kernel(order, qkv, q16, qinfo, kinfo, att, att16, canon, of, lse, of16, lse16):
    n_p=qkv.shape[0]//PIECE
    for i in range(n_p):
        src=pl.ds(pl.multiple_of(order[i]*PIECE,PIECE),PIECE)
        canon[i*PIECE:(i+1)*PIECE,:]=qkv[src,0:384]
    def rows(start,size,parts):
        qh=split_heads(canon[pl.ds(start,size),0:128])
        ss=[]
        for ks,kn,mask in parts:
            s=contract(qh,canon[pl.ds(ks,kn),128:256],1,1)
            if mask is not None:
                m2=jnp.concatenate([mask,mask],axis=0)
                s=jnp.where(m2,s,NEGATIVE)
            ss.append(s)
        top=functools.reduce(jnp.maximum,[jnp.max(s,axis=1,keepdims=True) for s in ss])
        tot=0.; o=0.
        for (ks,kn,_),s in zip(parts,ss):
            e=jnp.exp(s-top)
            tot=tot+jnp.sum(e,axis=1,keepdims=True)
            o=o+contract(e.astype(BF16),canon[pl.ds(ks,kn),256:384],1,0)
        o=join_heads(o*(1.0/tot))
        of[pl.ds(start,size),:]=o
        l=top+jnp.log(tot)
        lse[pl.ds(start,size),:]=join_heads(jnp.broadcast_to(l,(2*size,128)))
    t=tri(256)
    for b in range(4):
        parts=[(b*256,256,t)]
        if b: parts.insert(0,(0,b*256,None))
        rows(b*256,256,parts)
    bm=branch_mask()
    def branch(b,_):
        st=pl.multiple_of(TRUNK+b*BRANCH,PIECE)
        rows(st,BRANCH,[(0,TRUNK,None),(st,BRANCH,bm)])
        return 0
    lax.fori_loop(0,4,branch,0)
    for i in range(n_p):
        dst=pl.ds(pl.multiple_of(order[i]*PIECE,PIECE),PIECE)
        att[dst,:]=of[i*PIECE:(i+1)*PIECE,:].astype(BF16)
    s=contract(q16[...],qkv[:,384:512],1,1)
    s=jnp.where(allowed_mask(qinfo,kinfo),s,NEGATIVE)
    top=jnp.max(s,axis=1,keepdims=True)
    e=jnp.exp(s-top)
    tot=jnp.sum(e,axis=1,keepdims=True)
    o=contract(e.astype(BF16),qkv[:,384:512],1,0)*(1.0/tot)
    of16[...]=o
    att16[...]=pltpu.roll(o,64,1).astype(BF16)
    lse16[...]=jnp.broadcast_to(top+jnp.log(tot),o.shape)

def allowed_mask(qinfo,kinfo):
    ks=kinfo[0:1,:]; kp=kinfo[1:2,:]
    return ((ks==qinfo[:,0:1])|(ks==qinfo[:,1:2])|(ks==qinfo[:,2:3]))&(kp<=qinfo[:,3:4])

def attention_forward(order,qkv,q16,qinfo,kinfo):
    n=qkv.shape[0]; r=q16.shape[0]
    sd=jax.ShapeDtypeStruct
    V=pl.BlockSpec(memory_space=pltpu.VMEM)
    return pl.pallas_call(fwd_kernel,
        in_specs=[pl.BlockSpec(memory_space=pltpu.SMEM)]+[V]*4,
        out_specs=[V]*7,
        out_shape=[sd((n,128),BF16),sd((r,128),BF16),sd((n,384),BF16),sd((n,128),F32),sd((n,128),F32),sd((r,128),F32),sd((r,128),F32)],
        compiler_params=pltpu.CompilerParams(vmem_limit_bytes=32<<20),
        cost_estimate=pl.CostEstimate(flops=20_000_000_000,bytes_accessed=8_000_000,transcendentals=7_000_000),
        name="tree_attention_forward",
    )(order,qkv,q16,qinfo,kinfo)

def bwd_kernel(order, canon, of, lse, datt, kv16, q16, of16, lse16, datt16, qinfo, kinfo, dqkv, dq16, dc, dacc):
    n_p=canon.shape[0]//PIECE
    for i in range(n_p):
        src=pl.ds(pl.multiple_of(order[i]*PIECE,PIECE),PIECE)
        dc[i*PIECE:(i+1)*PIECE,:]=datt[src,:]
    def rows(start,size,parts):
        r=pl.ds(start,size)
        qh=split_heads(canon[r,0:128])
        d=dc[r,:]
        dh=split_heads(d)
        prod=d.astype(F32)*of[r,:]
        delta=jnp.concatenate([jnp.sum(prod[:,0:64],axis=1,keepdims=True),jnp.sum(prod[:,64:128],axis=1,keepdims=True)],axis=0)
        l=jnp.concatenate([lse[r,0:1],lse[r,64:65]],axis=0)
        dq=0.
        for ks,kn,mask,first in parts:
            kk=canon[pl.ds(ks,kn),128:256]
            s=contract(qh,kk,1,1)
            if mask is not None:
                s=jnp.where(jnp.concatenate([mask,mask],axis=0),s,NEGATIVE)
            p=jnp.exp(s-l)
            dp=contract(dh,canon[pl.ds(ks,kn),256:384],1,1)
            ds=(p*(dp-delta)).astype(BF16)
            dv=contract(p.astype(BF16),dh,0,0)
            dk=contract(ds,qh,0,0)
            dq=dq+contract(ds,kk,1,0)
            if first:
                dacc[pl.ds(ks,kn),128:256]=dk
                dacc[pl.ds(ks,kn),256:384]=dv
            else:
                dacc[pl.ds(ks,kn),128:256]+=dk
                dacc[pl.ds(ks,kn),256:384]+=dv
        dacc[r,0:128]=join_heads(dq)
    t=tri(256)
    for b in range(4):
        parts=[(b*256,256,t,True)]
        if b: parts.insert(0,(0,b*256,None,False))
        rows(b*256,256,parts)
    bm=branch_mask()
    def branch(b,_):
        st=pl.multiple_of(TRUNK+b*BRANCH,PIECE)
        rows(st,BRANCH,[(0,TRUNK,None,False),(st,BRANCH,bm,True)])
        return 0
    lax.fori_loop(0,4,branch,0)
    for i in range(n_p):
        dst=pl.ds(pl.multiple_of(order[i]*PIECE,PIECE),PIECE)
        x=dacc[i*PIECE:(i+1)*PIECE,:]
        dqkv[dst,0:128]=(x[:,0:128]*0.125).astype(BF16)
        dqkv[dst,128:384]=x[:,128:384].astype(BF16)
    k16=kv16[:,384:512]
    s=contract(q16[...],k16,1,1)
    s=jnp.where(allowed_mask(qinfo,kinfo),s,NEGATIVE)
    p=jnp.exp(s-lse16[:,0:1])
    dp=contract(datt16[...],k16,1,1)
    delta=jnp.sum(datt16[...].astype(F32)*of16[...],axis=1,keepdims=True)
    ds=(p*(dp-delta)).astype(BF16)
    dqkv[:,384:512]=(contract(ds,q16[...],0,0)+contract(p.astype(BF16),datt16[...],0,0)).astype(BF16)
    lane=lax.broadcasted_iota(jnp.int32,(1,128),1)>=64
    dq=pltpu.roll(contract(ds,k16,1,0)*0.125,64,1)
    dq16[...]=jnp.where(lane,dq,0.0).astype(BF16)

def attention_backward(order,canon,of,lse,datt,qkv,q16,of16,lse16,datt16,qinfo,kinfo):
    n=canon.shape[0]; r=q16.shape[0]
    sd=jax.ShapeDtypeStruct
    V=pl.BlockSpec(memory_space=pltpu.VMEM)
    return pl.pallas_call(bwd_kernel,
        in_specs=[pl.BlockSpec(memory_space=pltpu.SMEM)]+[V]*11,
        out_specs=[V]*2,
        out_shape=[sd((n,512),BF16),sd((r,128),BF16)],
        scratch_shapes=[pltpu.VMEM((n,128),BF16),pltpu.VMEM((n,384),F32)],
        compiler_params=pltpu.CompilerParams(vmem_limit_bytes=40<<20),
        cost_estimate=pl.CostEstimate(flops=50_000_000_000,bytes_accessed=15_000_000,transcendentals=7_000_000),
        name="tree_attention_backward",
    )(order,canon,of,lse,datt,qkv,q16,of16,lse16,datt16,qinfo,kinfo)


def parent_lookup(identities, shifted_table):
    labels = jnp.arange(shifted_table.shape[0], dtype=jnp.int32)
    matches = identities[:, None] == labels[None, :]
    return jnp.sum(jnp.where(matches, shifted_table[None, :], 0), axis=1) - 1


def tree_order(segments, places, parent):
    own = segments.reshape(-1, PIECE)[:, 0]
    start = places.reshape(-1, PIECE)[:, 0]
    table = parent + 1
    first_up = parent_lookup(own, table)
    second_up = parent_lookup(first_up, table)
    is_branch = (first_up >= 0) & (second_up < 0)
    is_leaf = second_up >= 0
    branch = jnp.where(is_leaf, first_up, own)
    rank = jnp.sum((is_branch[None, :] & (own[None, :] < branch[:, None])).astype(jnp.int32), axis=1)
    twin = is_leaf[None, :] & (first_up[None, :] == first_up[:, None]) & (own[None, :] < own[:, None])
    leaf = 1 + jnp.sum(twin.astype(jnp.int32), axis=1)
    target = jnp.where(
        first_up < 0, start // PIECE, TRUNK // PIECE + 3 * rank + jnp.where(is_leaf, leaf, 0)
    )
    pieces = jnp.arange(own.shape[0], dtype=jnp.int32)
    order = jnp.sum(jnp.where(target[None, :] == pieces[:, None], pieces[None, :], 0), axis=1)
    return order, first_up, second_up


def local(
    tokens,
    cotangent,
    segment_of,
    position_of,
    parent,
    ln1_gain,
    ln1_bias,
    w_qkv,
    b_query,
    b_value,
    w_out,
    b_out,
    ln2_gain,
    ln2_bias,
    w_fc,
    b_fc,
    w_proj,
    b_proj,
):
    rows = tokens.shape[0]
    half = w_qkv.shape[0]
    shard = lax.axis_index("shard")
    tensor, context, me = place()
    members = 2 * lax.axis_size("tensor")
    tree_rows = members * rows
    low = shard == 0

    held = (ln1_gain, ln1_bias, b_query, b_value, b_out, ln2_gain, ln2_bias, b_proj)
    shape = (len(held), half)
    line = lax.broadcasted_iota(jnp.int32, shape, 0)
    vectors = jnp.zeros(shape, F32)
    for i, value in enumerate(held):
        vectors = jnp.where(line == i, lax.broadcast_in_dim(value.astype(F32), shape, (1,)), vectors)
    zeros = jnp.zeros_like(vectors)
    half_vectors = jnp.concatenate(
        [jnp.where(low, vectors, zeros), jnp.where(low, zeros, vectors)], axis=1
    )
    proj_mine = w_proj.T
    normed_all, mixed, query_last, vectors, weight, fc_other = project(tokens, w_qkv, half_vectors, w_fc)
    proj_give, cotangent_give, mixed = lax.optimization_barrier((proj_mine, cotangent, mixed))
    proj_other = swap(proj_give, "shard", 0)
    cotangent_far = swap(cotangent_give, "tensor", 1)

    tree_start = lax.div(context, 2) * tree_rows
    segments = lax.dynamic_slice_in_dim(segment_of, tree_start, tree_rows)
    places = lax.dynamic_slice_in_dim(position_of, tree_start, tree_rows)
    order, first_up, second_up = tree_order(segments, places, parent)
    key_info = jnp.stack([segments, places])
    query_info = jnp.stack(
        [segments, jnp.repeat(first_up, PIECE), jnp.repeat(second_up, PIECE), places], axis=1
    )
    query_info = lax.dynamic_slice_in_dim(query_info, me * rows, rows, 0)

    attended_pair, attended_last, sorted_qkv, exact, level, exact_last, level_last = attention_forward(
        order, mixed, query_last, query_info, key_info
    )
    residual, fed_give, d_middle, d_pair, d_last, joint_keep, joint_give, fc_keep, fc_give, proj_sum, sums = feed_forward(
        attended_pair,
        attended_last,
        tokens,
        cotangent,
        cotangent_far,
        w_out,
        w_fc,
        fc_other,
        proj_mine,
        proj_other,
        vectors,
        b_fc.astype(F32)[None, :],
    )

    fc_got = swap(fc_give, "shard", 0)
    joint_other = swap(joint_give, "tensor", 1)
    fed_other = swap(fed_give, "tensor", 1)
    proj_sum = lax.psum(proj_sum, "context")

    d_mixed, d_query_last = attention_backward(
        order, sorted_qkv, exact, level, d_pair, mixed, query_last, exact_last, level_last, d_last,
        query_info, key_info,
    )
    fc_got, joint_other, fed_other, d_mixed = lax.optimization_barrier(
        (fc_got, joint_other, fed_other, d_mixed)
    )
    fc_sum = (fc_keep.astype(F32) + fc_got.astype(F32)).astype(BF16)
    fc_sum = lax.psum(
        fc_sum, "context", axis_index_groups=[list(range(lax.axis_size("context")))[::-1]]
    )
    output, d_inputs, pairs, joint_all, sums = finish(
        d_mixed,
        d_query_last,
        normed_all,
        weight,
        tokens,
        d_middle,
        vectors,
        joint_keep,
        joint_other,
        sums,
        residual,
        fed_other,
    )
    proj_sum, fc_sum, sums = lax.optimization_barrier((proj_sum, fc_sum, sums))
    own_mixer, own_out, own_fc = write_gradients(pairs, joint_all, fc_sum)
    own_proj = proj_sum.T.astype(F32)
    mine = lax.dynamic_slice_in_dim(sums[:8], shard * half, half, 1)
    own_bias_fc = lax.dynamic_slice_in_dim(sums, 8 + tensor, 1, 0)[0]
    return (
        output,
        d_inputs,
        mine[0],
        mine[1],
        own_mixer,
        mine[2],
        mine[3],
        own_out,
        mine[4],
        mine[5],
        mine[6],
        own_fc,
        own_bias_fc,
        own_proj,
        mine[7],
    )


def solution(mesh):
    return jax.shard_map(
        local,
        mesh=mesh,
        in_specs=(
            P(("shard", "context", "tensor"), None),
            P(("shard", "context", "tensor"), None),
            P("shard"),
            P("shard"),
            P(),
            P("shard"),
            P("shard"),
            P("shard", None),
            P("shard"),
            P("shard"),
            P("shard", None),
            P("shard"),
            P("shard"),
            P("shard"),
            P("shard", "tensor"),
            P("tensor"),
            P("tensor", "shard"),
            P("shard"),
        ),
        out_specs=(
            P(("shard", "context", "tensor"), None),
            P(("shard", "context", "tensor"), None),
            P("shard"),
            P("shard"),
            P("shard", None),
            P("shard"),
            P("shard"),
            P("shard", None),
            P("shard"),
            P("shard"),
            P("shard"),
            P("shard", "tensor"),
            P("tensor"),
            P("tensor", "shard"),
            P("shard"),
        ),
        check_vma=False,
    )
```

```python
import functools

import jax
import jax.numpy as jnp
from jax import lax
from jax.experimental import pallas as pl
from jax.experimental.pallas import tpu as pltpu
from jax.sharding import PartitionSpec as P

HEAD_DIM = 64
PAIR = 2 * HEAD_DIM
PIECE = 128
TRUNK = 8 * PIECE
BRANCH = 3 * PIECE
EPSILON = 1e-05
NEGATIVE = -1e30
F32 = jnp.float32
BF16 = jnp.bfloat16
VMEM = pl.BlockSpec(memory_space=pltpu.VMEM)
SMEM = pl.BlockSpec(memory_space=pltpu.SMEM)
ANY = pl.BlockSpec(memory_space=pl.ANY)
MESH = pl.DeviceIdType.MESH


def contract(left, right, left_dim, right_dim):
    return lax.dot_general(
        left, right, (((left_dim,), (right_dim,)), ((), ())), preferred_element_type=F32
    )


def flip(value, bit):
    low = 1 << bit
    return value + low - 2 * low * lax.rem(lax.div(value, low), 2)


def place():
    tensor, context = lax.axis_index("tensor"), lax.axis_index("context")
    return tensor, context, lax.rem(context, 2) * lax.axis_size("tensor") + tensor


def member(mask):
    tensor, context, _ = place()
    size = lax.axis_size("tensor")
    bits = size.bit_length() - 1
    for bit in range(bits):
        if mask >> bit & 1:
            tensor = flip(tensor, bit)
    if mask >> bits & 1:
        context = flip(context, 0)
    return {"context": context, "tensor": tensor}, lax.rem(context, 2) * size + tensor


def swap(value, axis, bit):
    size = lax.axis_size(axis)
    return lax.ppermute(value, axis, [(i, i ^ 1 << bit) for i in range(size)])


class Wires:
    def __init__(self, send, recv):
        self.send, self.recv, self.used = send, recv, 0

    def start(self, source, target, device):
        assert self.used < self.send.shape[0]
        copy = pltpu.make_async_remote_copy(
            src_ref=source,
            dst_ref=target,
            send_sem=self.send.at[self.used],
            recv_sem=self.recv.at[self.used],
            device_id=device,
            device_id_type=MESH,
        )
        self.used += 1
        copy.start()
        return copy


def by_rows(rows, step, body, first=0):
    def run(i, carry):
        body(pl.ds(pl.multiple_of(first + i * step, step), step))
        return carry

    lax.fori_loop(0, rows // step, run, 0)


def norm_backward(values, grad, gain):
    average = jnp.mean(values, axis=1, keepdims=True)
    centered = values - average
    inverse = lax.rsqrt(jnp.mean(centered * centered, axis=1, keepdims=True) + EPSILON)
    normal = centered * inverse
    scaled = grad * gain
    result = inverse * (
        scaled
        - jnp.mean(scaled, axis=1, keepdims=True)
        - normal * jnp.mean(scaled * normal, axis=1, keepdims=True)
    )
    return result, jnp.sum(grad * normal, axis=0, keepdims=True), jnp.sum(grad, axis=0, keepdims=True)


def norm_forward(values, gain, shift):
    average = jnp.mean(values, axis=1, keepdims=True)
    centered = values - average
    spread = jnp.mean(centered * centered, axis=1, keepdims=True)
    return centered * lax.rsqrt(spread + EPSILON) * gain + shift


def project_kernel(
    tokens, w_all, half_vectors, w_fc, normed_out, mixed_out, query_last, vectors, weight, fc_other, normed, mixed, everyone, w_qkv, seen, local_sem, out_sem, send, recv
):
    tensor, context, me = place()
    shard = lax.axis_index("shard")
    members = 2 * lax.axis_size("tensor")
    rows, width = tokens.shape
    half = width // 2
    cut = rows // 2
    shared = width - HEAD_DIM
    across = {"shard": 1 - shard}
    wires = Wires(send, recv)
    turn = members // 2

    load = pltpu.make_async_copy(w_all, w_qkv, local_sem.at[1])
    load.start()
    barrier = pltpu.get_barrier_semaphore()
    peers = [member(mask)[0] for mask in (1, 2, turn)] + [across]
    rest = [m for m in range(4, members) if m & 1 == 0 and m not in (turn, turn + 2)]
    for peer in peers:
        pl.semaphore_signal(barrier, inc=1, device_id=peer, device_id_type=MESH)
    pl.semaphore_wait(barrier, len(peers))
    assert not rest

    def slot(owner, first=0, size=rows):
        index = member(owner)[1] * rows + first
        return everyone.at[pl.ds(pl.multiple_of(index, 16), size)]

    def hand(source, target):
        return wires.start(source, source, member(target)[0])

    own = pltpu.make_async_copy(tokens, slot(0), local_sem.at[0])
    own.start()
    far = {m: wires.start(tokens, slot(0), member(m)[0]) for m in (2, turn)}
    vector_wire = wires.start(half_vectors, seen, across)
    close = {0: wires.start(tokens, slot(0), member(1)[0])}
    lane = lax.broadcasted_iota(jnp.int32, (1, PAIR), 1) < HEAD_DIM

    def choose(i, carry):
        r = pl.ds(pl.multiple_of(i * 32, 32), 32)
        to = pl.ds(pl.multiple_of(shard * half + i * 32, 32), 32)

        def window(start, size=PAIR):
            return w_qkv[r, pl.ds(pl.multiple_of(start, PAIR), size)]

        def turned(value):
            return pltpu.roll(value.astype(F32), HEAD_DIM, 1)

        weight[to, 0:PAIR] = window(me * PAIR)
        left, right = window(shared + me * PAIR), window(shared + (me + 1) * PAIR)
        weight[to, PAIR : 2 * PAIR] = jnp.where(lane, turned(left), turned(right)).astype(BF16)
        weight[to, 2 * PAIR : 3 * PAIR] = window(2 * width + me * PAIR)
        value = w_qkv[r, 2 * width + shared :]
        value = jnp.concatenate([value, value], axis=1)
        key = turned(w_qkv[r, 2 * width - PAIR : 2 * width])
        weight[to, 3 * PAIR : 4 * PAIR] = jnp.where(lane, key, value.astype(F32)).astype(BF16)
        query = w_qkv[r, shared : shared + PAIR]
        weight[to, 4 * PAIR :] = jnp.where(lane, query, jnp.zeros_like(query))
        return carry

    load.wait()
    lax.fori_loop(0, half // 32, choose, 0)
    chosen = weight.at[pl.ds(pl.multiple_of(shard * half, half), half)]
    weight_wire = wires.start(chosen, chosen, across)
    fc_wire = wires.start(w_fc.at[0 : half // 2], fc_other, across)

    vector_wire.wait_recv()
    vectors[...] = half_vectors[...] + seen[...]
    gain, shift = vectors[0:1, :], vectors[1:2, :]
    scale = HEAD_DIM ** (-0.5)
    pair_lanes = pl.ds(pl.multiple_of(me * PAIR, PAIR), PAIR)
    bias_query, bias_value = vectors[2:3, pair_lanes], vectors[3:4, pair_lanes]
    value_tail = vectors[3:4, shared:]
    bias_last = jnp.where(lane, 0.0, jnp.concatenate([value_tail, value_tail], axis=1))
    query_tail = vectors[2:3, shared:]
    query_tail = jnp.where(lane, jnp.concatenate([query_tail, query_tail], axis=1), 0.0)

    stored = []

    def put(source, target, owner, first):
        r = pl.ds(pl.multiple_of(member(owner)[1] * rows, rows), rows)
        stored.append(pltpu.make_async_copy(source.at[r], target.at[r], out_sem.at[first + owner]))
        stored[-1].start()

    def normalise(owner, first=0, size=rows):
        index = member(owner)[1] * rows + first

        def run(i, carry):
            r = pl.ds(pl.multiple_of(index + i * 32, 32), 32)
            normed[r, :] = norm_forward(everyone[r, :].astype(F32), gain, shift).astype(BF16)
            return carry

        lax.fori_loop(0, size // 32, run, 0)
        put(normed, normed_out, owner, 0)

    def multiply(owner, first=0, size=rows):
        r = pl.ds(pl.multiple_of(member(owner)[1] * rows + first, 32), size)
        result = jnp.dot(normed[r, :], weight[:, 0 : 4 * PAIR], preferred_element_type=F32)
        mixed[r, 0:PAIR] = ((result[:, 0:PAIR] + bias_query) * scale).astype(BF16)
        mixed[r, PAIR : 2 * PAIR] = result[:, PAIR : 2 * PAIR].astype(BF16)
        mixed[r, 2 * PAIR : 3 * PAIR] = (result[:, 2 * PAIR : 3 * PAIR] + bias_value).astype(BF16)
        mixed[r, 3 * PAIR :] = (result[:, 3 * PAIR :] + bias_last).astype(BF16)
        put(mixed, mixed_out, owner, members)

    own.wait()
    normalise(0)
    close[0].wait_recv()
    normalise(1)
    pieces = {}
    for m, other, first in ((2, turn, 0), (turn, 2, cut)):
        far[m].wait_recv()
        close[m] = hand(slot(m), 1)
        pieces[other] = hand(slot(m, first, cut), other)
    weight_wire.wait_recv()
    multiply(0)
    last = jnp.dot(
        normed[pl.ds(pl.multiple_of(me * rows, 32), rows), :], weight[:, 4 * PAIR :], preferred_element_type=F32
    )
    query_last[...] = ((last + query_tail) * scale).astype(BF16)
    multiply(1)
    for m in (2, turn):
        normalise(m)
        multiply(m)
    for m in (2, turn):
        close[m].wait_recv()
        normalise(m ^ 1)
        multiply(m ^ 1)
    opposite = 2 ^ turn
    passed = []
    for m, first in ((turn, 0), (2, cut)):
        pieces[m].wait_recv()
        passed.append(hand(slot(opposite, first, cut), 1))
    normalise(opposite)
    multiply(opposite)
    for wire in passed:
        wire.wait_recv()
    normalise(opposite ^ 1)
    multiply(opposite ^ 1)
    fc_wire.wait_recv()
    for copy in stored:
        copy.wait()
    for wire in list(far.values()) + list(close.values()) + list(pieces.values()) + passed + [vector_wire, weight_wire, fc_wire]:
        wire.wait_send()


def project(tokens, w_qkv, half_vectors, w_fc):
    rows, width = tokens.shape
    tree = 2 * lax.axis_size("tensor") * rows
    shape = jax.ShapeDtypeStruct
    return pl.pallas_call(
        project_kernel,
        in_specs=[VMEM, ANY, VMEM, ANY],
        out_specs=[ANY] * 2 + [VMEM] * 3 + [ANY],
        out_shape=[
            shape((tree, width), BF16),
            shape((tree, 4 * PAIR), BF16),
            shape((rows, PAIR), BF16),
            shape(half_vectors.shape, F32),
            shape((width, 5 * PAIR), BF16),
            shape((w_fc.shape[0] // 2, w_fc.shape[1]), BF16),
        ],
        scratch_shapes=[
            pltpu.VMEM((tree, width), BF16),
            pltpu.VMEM((tree, 4 * PAIR), BF16),
            pltpu.VMEM((tree, width), BF16),
            pltpu.VMEM(w_qkv.shape, BF16),
            pltpu.VMEM(half_vectors.shape, F32),
            pltpu.SemaphoreType.DMA((2,)),
            pltpu.SemaphoreType.DMA((2 * (tree // rows),)),
            pltpu.SemaphoreType.DMA((16,)),
            pltpu.SemaphoreType.DMA((16,)),
        ],
        compiler_params=pltpu.CompilerParams(
            collective_id=0, has_side_effects=True, vmem_limit_bytes=60 << 20
        ),
        name="project",
    )(tokens, w_qkv, half_vectors, w_fc)


def feed_forward_kernel(
    pair,
    last,
    tokens_all,
    cotangent,
    cotangent_far,
    out_mine,
    fc_mine,
    fc_other,
    proj_mine,
    proj_other,
    vectors,
    bias_fc,
    residual,
    fed_give,
    d_middle,
    d_pair,
    d_last,
    joint_keep,
    joint_give,
    fc_keep,
    fc_give,
    proj_sum,
    sums,
    w_out,
    w_fc,
    w_proj,
    attended,
    middle,
    normed,
    hidden,
    d_before,
    d_hidden,
    part,
    near,
    passing,
    far,
    d_attn,
    d_attended,
    grads,
    proj_keep,
    proj_give,
    proj_got,
    joint,
    joint_near,
    tokens,
    local_sem,
    send,
    recv,
):
    tensor, context, me = place()
    shard = lax.axis_index("shard")
    near_bit = lax.rem(tensor, 2)
    members = 2 * lax.axis_size("tensor")
    rows, width = tokens.shape
    half = width // 2
    shared = width - HEAD_DIM
    group = range(1, members)
    wires = Wires(send, recv)
    bias_out, gain, shift, bias_proj = (vectors[i : i + 1, :] for i in (4, 5, 6, 7))
    across = {"shard": 1 - shard}

    barrier = pltpu.get_barrier_semaphore()
    peers = [member(mask)[0] for mask in group] + [across]
    for peer in peers:
        pl.semaphore_signal(barrier, inc=1, device_id=peer, device_id_type=MESH)
    pl.semaphore_wait(barrier, len(peers))

    def slab(ref, index, size):
        return ref.at[pl.ds(pl.multiple_of(index * size, size), size)]

    def beside(ref, index):
        return ref.at[:, pl.ds(pl.multiple_of(index * PAIR, PAIR), PAIR)]

    moved = []
    for mask in group:
        device, index = member(mask)
        moved.append(wires.start(slab(pair, index, rows), beside(attended, me), device))
    quarter = half // 2
    out_wire = wires.start(
        slab(out_mine, near_bit, quarter), slab(w_out, 2 * shard + near_bit, quarter), across
    )
    local = [
        pltpu.make_async_copy(source, target, local_sem.at[i])
        for i, (source, target) in enumerate(
            (
                (slab(pair, me, rows), beside(attended, me)),
                (out_mine, slab(w_out, shard, half)),
                (fc_mine, slab(w_fc, shard, half)),
                (fc_other, slab(w_fc, 2 * (1 - shard), quarter)),
                (proj_mine, slab(w_proj, shard, half)),
                (proj_other, slab(w_proj, 1 - shard, half)),
                (tokens_all, tokens),
                (cotangent, slab(grads, 0, rows)),
                (cotangent_far, slab(grads, 2, rows)),
            )
        )
    ]
    pulled_wires = [
        wires.start(source, slab(grads, index, rows), member(1)[0])
        for index, source in ((1, cotangent), (3, cotangent_far))
    ]
    for copy in local:
        copy.start()
    attended[:, shared:] = last[:, 0:HEAD_DIM]
    out_wire.wait_recv()
    out_part = slab(w_out, 2 * (1 - shard) + near_bit, quarter)
    out_near = wires.start(out_part, out_part, member(1)[0])
    fc_wire = wires.start(
        fc_mine.at[quarter:half], slab(w_fc, 2 * shard + 1, quarter), across
    )
    for copy in local:
        copy.wait()
    for wire in moved + [out_near]:
        wire.wait_recv()

    start = 0
    while start < width:
        stop = min(start + 2 * PAIR, width)
        middle[:, start:stop] = (
            tokens[:, start:stop].astype(F32)
            + jnp.dot(attended[...], w_out[:, start:stop], preferred_element_type=F32)
            + bias_out[:, start:stop]
        )
        start = stop

    def second_norm(r):
        normed[r, :] = norm_forward(middle[r, :], gain, shift).astype(BF16)

    cut = rows // 2

    def piece(mask, i):
        return slice(mask * rows + i * cut, mask * rows + (i + 1) * cut)

    cross = []
    for i in range(2):
        by_rows(cut, 32, second_norm, i * cut)
        cross.append(wires.start(normed.at[piece(0, i)], normed.at[piece(2, i)], member(2)[0]))

    def block(ref, mask):
        return ref.at[mask * rows : (mask + 1) * rows, :]

    close = wires.start(block(normed, 0), block(normed, 1), member(1)[0])
    for wire in pulled_wires:
        wire.wait_recv()
    for mask in range(4):
        block(d_hidden, mask)[...] = jnp.dot(
            block(grads, mask)[...], w_proj[...], preferred_element_type=F32
        )

    def feed(r):
        start = 0
        while start < width:
            stop = min(start + 2 * PAIR, width)
            c = slice(start, stop)
            before = jnp.dot(normed[r, :], w_fc[:, c], preferred_element_type=F32) + bias_fc[0:1, c]
            cumulative = 0.5 + 0.5 * lax.erf(before * (0.5**0.5))
            hidden[r, c] = (before * cumulative).astype(BF16)
            slope = cumulative + before * jnp.exp(-0.5 * before * before) * ((2 * jnp.pi) ** -0.5)
            d_before[r, c] = (d_hidden[r, c] * slope).astype(BF16)
            start = stop

    def back(r):
        return contract(d_before[r, :], w_fc[...], 1, 1)

    def ahead(mask):
        return contract(hidden[mask * rows : (mask + 1) * rows, :], w_proj[...], 1, 1)

    fc_wire.wait_recv()
    feed(slice(0, rows))
    close.wait_recv()
    feed(slice(rows, 2 * rows))
    part[0] = back(slice(rows, 2 * rows)).astype(BF16)
    to_near = wires.start(part.at[0], near.at[0], member(1)[0])
    relay, to_pass, to_far = [], [], []
    for i in range(2):
        h = slice(i * cut, (i + 1) * cut)
        cross[i].wait_recv()
        relay.append(wires.start(normed.at[piece(2, i)], normed.at[piece(3, i)], member(1)[0]))
        feed(piece(2, i))
        relay[i].wait_recv()
        feed(piece(3, i))
        part[1, h] = back(piece(3, i)).astype(BF16)
        to_pass.append(wires.start(part.at[1, h], near.at[1, h], member(1)[0]))
        mine = back(piece(2, i))
        to_pass[i].wait_recv()
        passing[h] = (mine + near[1, h].astype(F32)).astype(BF16)
        to_far.append(wires.start(passing.at[h], far.at[h], member(2)[0]))

    other_part = pl.ds(pl.multiple_of(2 * rows + (1 - shard) * half, 8), half)
    own_part = pl.ds(pl.multiple_of(2 * rows + shard * half, 8), half)
    proj_wires = []
    start = 0
    while start < width:
        stop = min(start + 2 * PAIR, width)
        c = slice(start, stop)
        d_hidden_part = d_hidden.at[2 * rows : 2 * rows + width, 0 : stop - start]
        d_hidden_part[...] = contract(grads[...], hidden[:, c], 0, 0)
        proj_give[:, c] = d_hidden[other_part, 0 : stop - start].astype(BF16)
        proj_wires.append(wires.start(proj_give.at[:, c], proj_got.at[:, c], across))
        proj_keep[:, c] = d_hidden[own_part, 0 : stop - start]
        start = stop
    start = 0
    while start < width:
        stop = min(start + 2 * PAIR, width)
        c = slice(start, stop)
        d_hidden_part = d_hidden.at[2 * rows : 2 * rows + width, 0 : stop - start]
        d_hidden_part[...] = contract(normed[...], d_before[:, c], 0, 0)
        fc_give[:, c] = d_hidden[other_part, 0 : stop - start].astype(BF16)
        fc_keep[:, c] = d_hidden[own_part, 0 : stop - start].astype(BF16)
        start = stop
    d_hidden[0:rows, :] = back(slice(0, rows))
    to_near.wait_recv()
    for wire in to_far:
        wire.wait_recv()

    sums[...] = jnp.zeros_like(sums)

    def second_back(r):
        grad = d_hidden[r, :] + near[0, r, :].astype(F32) + far[r, :].astype(F32)
        result, by_gain, by_shift = norm_backward(middle[r, :], grad, gain)
        pulled = grads[r, :].astype(F32)
        result = result + pulled
        d_middle[r, :] = result
        low = result.astype(BF16)
        d_attn[r, 0:width] = low
        d_attn[r, width:] = jnp.zeros((r.size, d_attn.shape[1] - width), BF16)
        sums[4:5, :] += jnp.sum(low.astype(F32), axis=0, keepdims=True)
        sums[5:6, :] += by_gain
        sums[6:7, :] += by_shift
        sums[7:8, :] += jnp.sum(pulled, axis=0, keepdims=True)

    by_rows(rows, 64, second_back)
    start = 0
    while start < width:
        stop = min(start + 2 * PAIR, width)
        d_attended[:, start:stop] = contract(d_attn[:, 0:width], w_out[start:stop, :], 1, 1).astype(BF16)
        start = stop
    returned = []
    for mask in group:
        device, index = member(mask)
        returned.append(wires.start(beside(d_attended, index), slab(d_pair, me, rows), device))
    own_copy = pltpu.make_async_copy(beside(d_attended, me), slab(d_pair, me, rows), local_sem.at[0])
    own_copy.start()
    lane = lax.broadcasted_iota(jnp.int32, (1, PAIR), 1) >= HEAD_DIM
    tail = jnp.concatenate([d_attended[:, shared:]] * 2, axis=1)
    d_last[...] = jnp.where(lane, tail, jnp.zeros_like(tail))
    joint[:, shared : shared + PAIR] = jnp.zeros((width, PAIR), BF16)
    start = 0
    while start < d_attn.shape[1]:
        stop = min(start + 2 * PAIR, d_attn.shape[1])
        to = start if start < shared else start + PAIR
        joint[:, to : to + stop - start] = contract(attended[...], d_attn[:, start:stop], 0, 0).astype(BF16)
        start = stop
    side = joint.shape[1] // 2
    kept = pl.ds(pl.multiple_of(near_bit * side, side), side)
    given = pl.ds(pl.multiple_of((1 - near_bit) * side, side), side)
    joint_wire = wires.start(joint.at[:, given], joint_near, member(1)[0])
    part[2] = ahead(3).astype(BF16)
    to_pass_out = wires.start(part.at[2], near.at[3], member(1)[0])
    part[3] = ahead(1).astype(BF16)
    to_near_out = wires.start(part.at[3], near.at[2], member(1)[0])
    d_hidden[2 * rows : 3 * rows, :] = ahead(2)
    d_hidden[rows : 2 * rows, :] = ahead(0)
    bias = jnp.zeros((1, width), F32)

    def add_bias(i, total):
        r = pl.ds(pl.multiple_of(i * 64, 64), 64)
        return total + jnp.sum(d_before[r, :].astype(F32), axis=0, keepdims=True)

    bias = lax.fori_loop(0, 4 * rows // 64, add_bias, bias)
    for i in range(lax.axis_size("tensor")):
        sums[8 + i : 9 + i, :] = jnp.where(tensor == i, bias, 0.0)
    to_near_out.wait_recv()
    to_pass_out.wait_recv()

    def finish_output(r):
        third = pl.ds(pl.multiple_of(2 * rows + r.start, 64), r.size)
        again = pl.ds(pl.multiple_of(rows + r.start, 64), r.size)
        fed_give[r, :] = (d_hidden[third, :] + near[3, r, :].astype(F32)).astype(BF16)
        residual[r, :] = middle[r, :] + d_hidden[again, :] + near[2, r, :].astype(F32) + bias_proj

    by_rows(rows, 64, finish_output)
    joint_wire.wait_recv()
    second = lax.rem(lax.div(tensor, 2), 2)

    def add_joint(target, which):
        for i in range(2):

            def run(r):
                source = pl.ds(pl.multiple_of((2 * i + which) * quarter - i * quarter + r.start, 16), r.size)
                total = joint[source, kept].astype(F32) + joint_near[source, :].astype(F32)
                target[r, :] = total.astype(BF16)

            by_rows(quarter, 16, run, i * quarter)

    add_joint(joint_keep, second)
    add_joint(joint_give, 1 - second)
    for wire in proj_wires:
        wire.wait_recv()

    def add_proj(r):
        proj_sum[r, :] = (proj_keep[r, :] + proj_got[r, :].astype(F32)).astype(BF16)

    by_rows(half, 32, add_proj)
    own_copy.wait()
    for wire in returned:
        wire.wait_recv()
    for wire in (
        moved + returned + [out_wire, out_near, fc_wire] + pulled_wires + proj_wires
        + cross + relay + to_pass + to_far + [joint_wire, close, to_near, to_near_out, to_pass_out]
    ):
        wire.wait_send()


def feed_forward(pair, last, tokens, cotangent, cotangent_far, out_mine, fc_mine, fc_other, proj_mine, proj_other, vectors, bias_fc):
    rows, width = tokens.shape
    members = 2 * lax.axis_size("tensor")
    hidden = fc_mine.shape[1]
    tall = 4 * rows
    shape = jax.ShapeDtypeStruct
    return pl.pallas_call(
        feed_forward_kernel,
        in_specs=[ANY, VMEM] + [ANY] * 8 + [VMEM] * 2,
        out_specs=[VMEM] * 3 + [ANY] + [VMEM] * 7,
        out_shape=[
            shape((rows, width), F32),
            shape((rows, width), BF16),
            shape((rows, width), F32),
            shape((members * rows, PAIR), BF16),
            shape((rows, PAIR), BF16),
            shape((width // 2, 5 * PAIR), BF16),
            shape((width // 2, 5 * PAIR), BF16),
            shape((width // 2, hidden), BF16),
            shape((width // 2, hidden), BF16),
            shape((width // 2, hidden), BF16),
            shape((16, width), F32),
        ],
        scratch_shapes=[
            pltpu.VMEM((width, width), BF16),
            pltpu.VMEM((width, hidden), BF16),
            pltpu.VMEM((width, hidden), BF16),
            pltpu.VMEM((rows, width), BF16),
            pltpu.VMEM((rows, width), F32),
            pltpu.VMEM((tall, width), BF16),
            pltpu.VMEM((tall, hidden), BF16),
            pltpu.VMEM((tall, hidden), BF16),
            pltpu.VMEM((2 * rows + max(2 * rows, width), hidden), F32),
            pltpu.VMEM((4, rows, width), BF16),
            pltpu.VMEM((4, rows, width), BF16),
            pltpu.VMEM((rows, width), BF16),
            pltpu.VMEM((rows, width), BF16),
            pltpu.VMEM((rows, 9 * PAIR), BF16),
            pltpu.VMEM((rows, width), BF16),
            pltpu.VMEM((tall, width), BF16),
            pltpu.VMEM((width // 2, hidden), F32),
            pltpu.VMEM((width // 2, hidden), BF16),
            pltpu.VMEM((width // 2, hidden), BF16),
            pltpu.VMEM((width, 10 * PAIR), BF16),
            pltpu.VMEM((width, 5 * PAIR), BF16),
            pltpu.VMEM((rows, width), BF16),
            pltpu.SemaphoreType.DMA((9,)),
            pltpu.SemaphoreType.DMA((2 * members + 24,)),
            pltpu.SemaphoreType.DMA((2 * members + 24,)),
        ],
        compiler_params=pltpu.CompilerParams(
            collective_id=3, has_side_effects=True, vmem_limit_bytes=62 << 20
        ),
        name="feed_forward",
    )(pair, last, tokens, cotangent, cotangent_far, out_mine, fc_mine, fc_other, proj_mine, proj_other, vectors, bias_fc)


def finish_kernel(
    d_mixed_all,
    d_query_last,
    normed_all,
    weight_all,
    tokens_all,
    d_middle_all,
    gain,
    joint_keep_all,
    joint_other_all,
    vectors,
    residual_all,
    fed_other_all,
    output,
    d_tokens,
    pairs,
    joint_all,
    sums,
    near_give,
    near_got,
    row_sum,
    second_got,
    turn_last,
    last_low,
    pair_t,
    pair,
    pair_give,
    pair_got,
    pair_low,
    pair_seen,
    tail,
    tail_near,
    tail_sum,
    tail_give,
    tail_got,
    joint_give,
    joint_got,
    half_low,
    half_seen,
    pair_sum,
    half_sum,
    vec,
    vec_give,
    vec_got,
    d_mixed,
    normed,
    weight,
    tokens,
    d_middle,
    joint_keep,
    joint_other,
    residual,
    fed_other,
    load_sem,
    send,
    recv,
):
    tensor, context, me = place()
    shard = lax.axis_index("shard")
    near = lax.rem(tensor, 2)
    second = lax.rem(lax.div(tensor, 2), 2)
    contexts = lax.axis_size("context")
    members = 2 * lax.axis_size("tensor")
    turn = members // 2
    rows, width = tokens.shape
    half = width // 2
    quarter = half // 2
    side = joint_keep.shape[1]
    shared = width - HEAD_DIM
    block = 4 * PAIR
    across = {"shard": 1 - shard}
    higher = [
        {"context": flip(context, bit)} for bit in range(1, contexts.bit_length() - 1)
    ]
    group = range(1, members)
    wires = Wires(send, recv)

    loads = [
        pltpu.make_async_copy(source, target, load_sem.at[i])
        for i, (source, target) in enumerate(
            (
                (d_mixed_all, d_mixed),
                (normed_all, normed),
                (weight_all, weight),
                (tokens_all, tokens),
                (d_middle_all, d_middle),
                (joint_keep_all, joint_keep),
                (joint_other_all, joint_other),
                (residual_all, residual),
                (fed_other_all, fed_other),
            )
        )
    ]
    for copy in loads:
        copy.start()
    barrier = pltpu.get_barrier_semaphore()
    peers = [member(mask)[0] for mask in group] + [across] + higher
    for peer in peers:
        pl.semaphore_signal(barrier, inc=1, device_id=peer, device_id_type=MESH)
    pl.semaphore_wait(barrier, len(peers))
    for copy in loads:
        copy.wait()

    def part(ref, index, size):
        return ref.at[pl.ds(pl.multiple_of(index * size, size), size)]

    def term(mask):
        r = pl.ds(pl.multiple_of(member(mask)[1] * rows, rows), rows)
        return contract(d_mixed[r, :], weight[:, 0:block], 1, 1)

    steps = d_mixed.shape[0] // (2 * rows)
    pair_t[...] = jnp.zeros_like(pair_t)

    def accumulate(i, carry):
        r = pl.ds(pl.multiple_of(i * 2 * rows, 2 * rows), 2 * rows)
        pair_t[...] += contract(d_mixed[r, :], normed[r, :], 0, 0)
        return carry

    lax.fori_loop(0, steps, accumulate, 0)
    pair[...] = pair_t[...].T
    other = pl.ds(pl.multiple_of((1 - shard) * half, half), half)
    own = pl.ds(pl.multiple_of(shard * half, half), half)
    pair_give[...] = pair[other, 0 : 3 * PAIR].astype(BF16)
    pair_wire = wires.start(pair_give, pair_got, across)
    mine = pl.ds(pl.multiple_of(me * rows, rows), rows)
    tail[:, 0:PAIR] = pair[:, 3 * PAIR :].astype(BF16)
    tail[:, PAIR:] = contract(d_query_last[...], normed[mine, :], 0, 0).T.astype(BF16)
    tail_near_wire = wires.start(tail, tail_near, member(1)[0])

    order = [6, 2, 4, 0]
    near_wires = {}
    for i, mask in enumerate(order):
        near_give[i] = term(mask ^ 1).astype(BF16)
        near_wires[mask] = wires.start(near_give.at[i], near_got.at[i], member(1)[0])

    tail_near_wire.wait_recv()

    def add_tail_near(r):
        tail_sum[r, :] = tail[r, :].astype(F32) + tail_near[r, :].astype(F32)

    by_rows(width, 64, add_tail_near)
    to_second, to_turn = member(2)[0], member(turn)[0]
    for i in range(2):
        source = pl.ds(pl.multiple_of(i * half + (1 - second) * quarter, 16), quarter)
        tail_give[i * quarter : (i + 1) * quarter, :] = tail_sum[source, :].astype(BF16)
    tail_wire = wires.start(tail_give, tail_got, to_second)

    second_wires = []
    for i, mask in enumerate(order):
        total = term(mask)
        if mask == 0:
            query = pltpu.roll(d_query_last[...].astype(F32), HEAD_DIM, 1).astype(BF16)
            total = total + contract(query, weight[:, block:], 1, 1)
        near_wires[mask].wait_recv()
        total = total + near_got[i].astype(F32)
        if i >= 2:
            row_sum[i - 2] = total
        if mask & 2:
            near_got[i] = total.astype(BF16)
            second_wires.append(wires.start(near_got.at[i], second_got.at[i], to_second))

    pair_wire.wait_recv()
    pair_own = pair[own, 0 : 3 * PAIR] + pair_got[...].astype(F32)
    pair_wires = []
    for i, device in enumerate(higher):
        pair_low[i] = pair_own.astype(BF16)
        wire = wires.start(pair_low.at[i], pair_seen.at[i], device)
        pair_wires.append(wire)
        if i < len(higher) - 1:
            wire.wait_recv()
            pair_own = pair_own + pair_seen[i].astype(F32)
    pair_sum[...] = pair_own

    tail_wire.wait_recv()
    wide = joint_keep.shape[1] - 2 * PAIR

    def joint_term(which):
        r = pl.ds(pl.multiple_of(which * quarter, quarter), quarter)
        s = pl.ds(pl.multiple_of(which * half + second * quarter, quarter), quarter)
        total = joint_keep[r, :].astype(F32) + joint_other[r, :].astype(F32)
        last = jnp.where(near == 1, tail_sum[s, :] + tail_got[r, :].astype(F32), 0.0)
        return jnp.concatenate([total[:, :wide], total[:, wide:] + last], axis=1)

    joint_give[...] = joint_term(1 - shard).astype(BF16)
    joint_wire = wires.start(joint_give, joint_got, across)

    vec[...] = vectors[...]

    def add_columns(i, total):
        r = pl.ds(pl.multiple_of(i * 64, 64), 64)
        return total + jnp.sum(d_mixed[r, :].astype(F32), axis=0, keepdims=True)

    columns = lax.fori_loop(0, d_mixed.shape[0] // 64, add_columns, jnp.zeros((1, block), F32))
    pair_lanes = pl.ds(pl.multiple_of(me * PAIR, PAIR), PAIR)
    vec[2:3, pair_lanes] = columns[:, 0:PAIR]
    vec[3:4, pair_lanes] = columns[:, 2 * PAIR : 3 * PAIR]
    query = jnp.sum(d_query_last[...].astype(F32), axis=0, keepdims=True)
    vec[2:3, shared:] = pltpu.roll(query, HEAD_DIM, 1)[:, :HEAD_DIM]
    vec[3:4, shared:] = pltpu.roll(columns[:, 3 * PAIR :], HEAD_DIM, 1)[:, :HEAD_DIM]


    def add_fed(r):
        output[r, :] = (residual[r, :] + fed_other[r, :].astype(F32)).astype(BF16)

    by_rows(rows, 64, add_fed)

    joint_wire.wait_recv()
    half_sum[...] = joint_term(shard) + joint_got[...].astype(F32)
    hops = [to_turn] + higher
    joint_wires = []

    def joint_hop(i):
        if i:
            joint_wires[-1].wait_recv()
            half_sum[...] += half_seen[i - 1].astype(F32)
        if i < len(hops):
            half_low[i] = half_sum[...].astype(BF16)
            joint_wires.append(wires.start(half_low.at[i], half_seen.at[i], hops[i]))

    joint_hop(0)

    second_wires[0].wait_recv()
    last_low[...] = (row_sum[0] + second_got[0].astype(F32)).astype(BF16)
    turn_wire = wires.start(last_low, turn_last, to_turn)

    for i in range(1, len(hops)):
        joint_hop(i)

    if pair_wires:
        pair_wires[-1].wait_recv()
        pair_sum[...] += pair_seen[len(higher) - 1].astype(F32)

    def slot(owner, start=0, size=half):
        return pairs.at[pl.ds(pl.multiple_of(member(owner)[1] * half + start, 16), size)]

    def hand(source, target):
        return wires.start(source, source, member(target)[0])

    pairs[pl.ds(pl.multiple_of(me * half, half), half), :] = pair_sum[...].astype(BF16)
    far = {mask: hand(slot(0), mask) for mask in (turn, 2)}
    close = {0: hand(slot(0), 1)}

    second_wires[1].wait_recv()
    turn_wire.wait_recv()

    def first_norm(r):
        grad = row_sum[1, r, :] + second_got[1, r, :].astype(F32) + turn_last[r, :].astype(F32)
        result, by_gain, by_shift = norm_backward(tokens[r, :].astype(F32), grad, gain[0:1, :])
        d_tokens[r, :] = result + d_middle[r, :]
        vec[0:1, :] += by_gain
        vec[1:2, :] += by_shift

    by_rows(rows, 64, first_norm)
    vec_wires = []

    def vec_send(i, device):
        vec_give[i] = vec[...]
        vec_wires.append(wires.start(vec_give.at[i], vec_got.at[i], device))

    def vec_add():
        i = len(vec_wires) - 1
        vec_wires[i].wait_recv()
        vec[...] += vec_got[i]

    vec_stops = [member(1)[0], to_second, to_turn, across] + higher
    vec_send(0, vec_stops[0])

    opposite = 2 ^ turn
    far[turn].wait_recv()
    far[opposite] = hand(slot(turn), 2)
    close[turn] = hand(slot(turn), 1)
    far[2].wait_recv()
    close[2] = hand(slot(2), 1)
    vec_add()
    vec_send(1, vec_stops[1])

    joint_hop(len(hops))
    keep = pl.ds(pl.multiple_of(second * quarter, quarter), quarter)
    kept = pl.ds(pl.multiple_of(near * side, side), side)
    joint_all[keep, kept] = half_sum[...].astype(BF16)
    joint_mine = joint_all.at[keep, kept]
    back = wires.start(joint_mine, joint_mine, to_second)
    vec_add()
    vec_send(2, vec_stops[2])
    far[opposite].wait_recv()
    close[opposite] = hand(slot(opposite), 1)
    vec_add()
    vec_send(3, vec_stops[3])
    back.wait_recv()
    joint_side = joint_all.at[:, kept]
    back_near = wires.start(joint_side, joint_side, member(1)[0])
    vec_add()
    for i in range(4, len(vec_stops)):
        vec_send(i, vec_stops[i])
        vec_add()
    sums[...] = vec[...]
    for wire in close.values():
        wire.wait_recv()
    back_near.wait_recv()

    for wire in (
        [pair_wire, tail_near_wire, tail_wire, joint_wire, back, back_near]
        + list(near_wires.values()) + second_wires + [turn_wire] + pair_wires + list(far.values())
        + list(close.values()) + joint_wires + vec_wires
    ):
        wire.wait_send()


def finish(d_mixed, d_query_last, normed, weight, tokens, d_middle, gain, joint_keep, joint_other, vectors, residual, fed_other):
    rows, width = tokens.shape
    half = width // 2
    members = 2 * lax.axis_size("tensor")
    higher = lax.axis_size("context").bit_length() - 2
    side = joint_keep.shape[1]
    tall = vectors.shape[0]
    scratch = [
        pltpu.VMEM((4, rows, width), BF16),
        pltpu.VMEM((4, rows, width), BF16),
        pltpu.VMEM((2, rows, width), F32),
        pltpu.VMEM((2, rows, width), BF16),
        pltpu.VMEM((rows, width), BF16),
        pltpu.VMEM((rows, width), BF16),
        pltpu.VMEM((4 * PAIR, width), F32),
        pltpu.VMEM((width, 4 * PAIR), F32),
        pltpu.VMEM((half, 3 * PAIR), BF16),
        pltpu.VMEM((half, 3 * PAIR), BF16),
        pltpu.VMEM((max(higher, 1), half, 3 * PAIR), BF16),
        pltpu.VMEM((max(higher, 1), half, 3 * PAIR), BF16),
        pltpu.VMEM((width, 2 * PAIR), BF16),
        pltpu.VMEM((width, 2 * PAIR), BF16),
        pltpu.VMEM((width, 2 * PAIR), F32),
        pltpu.VMEM((half, 2 * PAIR), BF16),
        pltpu.VMEM((half, 2 * PAIR), BF16),
        pltpu.VMEM((half // 2, side), BF16),
        pltpu.VMEM((half // 2, side), BF16),
        pltpu.VMEM((higher + 1, half // 2, side), BF16),
        pltpu.VMEM((higher + 1, half // 2, side), BF16),
        pltpu.VMEM((half, 3 * PAIR), F32),
        pltpu.VMEM((half // 2, side), F32),
        pltpu.VMEM((tall, width), F32),
        pltpu.VMEM((higher + 4, tall, width), F32),
        pltpu.VMEM((higher + 4, tall, width), F32),
        pltpu.VMEM(d_mixed.shape, d_mixed.dtype),
        pltpu.VMEM(normed.shape, normed.dtype),
        pltpu.VMEM(weight.shape, weight.dtype),
        pltpu.VMEM(tokens.shape, tokens.dtype),
        pltpu.VMEM(d_middle.shape, d_middle.dtype),
        pltpu.VMEM(joint_keep.shape, joint_keep.dtype),
        pltpu.VMEM(joint_other.shape, joint_other.dtype),
        pltpu.VMEM(residual.shape, residual.dtype),
        pltpu.VMEM(fed_other.shape, fed_other.dtype),
        pltpu.SemaphoreType.DMA((9,)),
        pltpu.SemaphoreType.DMA((3 * members + 3 * higher + 20,)),
        pltpu.SemaphoreType.DMA((3 * members + 3 * higher + 20,)),
    ]
    return pl.pallas_call(
        finish_kernel,
        in_specs=[ANY, VMEM] + [ANY] * 4 + [VMEM] + [ANY] * 2 + [VMEM] + [ANY] * 2,
        out_specs=[VMEM] * 5,
        out_shape=[
            jax.ShapeDtypeStruct((rows, width), BF16),
            jax.ShapeDtypeStruct((rows, width), F32),
            jax.ShapeDtypeStruct((members * half, 3 * PAIR), BF16),
            jax.ShapeDtypeStruct((half, 2 * side), BF16),
            jax.ShapeDtypeStruct((tall, width), F32),
        ],
        scratch_shapes=scratch,
        compiler_params=pltpu.CompilerParams(
            collective_id=6, has_side_effects=True, vmem_limit_bytes=63 << 20
        ),
        name="finish",
    )(d_mixed, d_query_last, normed, weight, tokens, d_middle, gain, joint_keep, joint_other, vectors, residual, fed_other)


def write_kernel(pairs, joint, fc, own_mixer, own_out, own_fc):
    members = pairs.shape[0]
    width = own_out.shape[1]
    shared = width - HEAD_DIM
    lane = lax.broadcasted_iota(jnp.int32, (1, PAIR), 1) < HEAD_DIM

    def write(r):
        own_out[r, 0:shared] = joint[r, 0:shared].astype(F32)
        eighth = joint[r, shared : shared + PAIR].astype(F32)
        ninth = joint[r, shared + PAIR :].astype(F32)
        own_out[r, shared:] = ninth[:, :HEAD_DIM]
        own_fc[r, :] = fc[r, :].astype(F32)
        keys = []
        for k in range(members):
            value = pairs[k, r, :].astype(F32)
            own_mixer[r, k * PAIR : (k + 1) * PAIR] = value[:, 0:PAIR]
            own_mixer[r, 2 * width + k * PAIR : 2 * width + (k + 1) * PAIR] = value[:, 2 * PAIR :]
            keys.append(value[:, PAIR : 2 * PAIR])
        keys = jnp.concatenate(keys + [jnp.where(lane, eighth, ninth)], axis=1)
        own_mixer[r, shared : 2 * width] = pltpu.roll(keys, HEAD_DIM, 1)
        own_mixer[r, 2 * width + shared :] = pltpu.roll(eighth, HEAD_DIM, 1)[:, :HEAD_DIM]

    by_rows(fc.shape[0], 16, write)


def write_gradients(pairs, joint, fc):
    half, width = fc.shape
    members = pairs.shape[0] // half
    step = half // 2

    def block(*shape):
        return pl.BlockSpec(shape, lambda i: (0,) * (len(shape) - 2) + (i, 0))

    return pl.pallas_call(
        write_kernel,
        grid=(half // step,),
        in_specs=[block(members, step, 3 * PAIR), block(step, joint.shape[1]), block(step, width)],
        out_specs=[block(step, 3 * width), block(step, width), block(step, width)],
        out_shape=[
            jax.ShapeDtypeStruct((half, 3 * width), F32),
            jax.ShapeDtypeStruct((half, width), F32),
            jax.ShapeDtypeStruct((half, width), F32),
        ],
        compiler_params=pltpu.CompilerParams(vmem_limit_bytes=40 << 20),
        name="write_gradients",
    )(pairs.reshape(members, half, 3 * PAIR), joint, fc)


def tri(n):
    r=lax.broadcasted_iota(jnp.int32,(n,n),0); c=lax.broadcasted_iota(jnp.int32,(n,n),1)
    return c<=r

def branch_mask():
    r=lax.broadcasted_iota(jnp.int32,(BRANCH,BRANCH),0); c=lax.broadcasted_iota(jnp.int32,(BRANCH,BRANCH),1)
    return (c<=r)&((c<PIECE)|(c//PIECE==r//PIECE))

def split_heads(x):
    lane=lax.broadcasted_iota(jnp.int32,(1,2*64),1)<64
    z=jnp.zeros_like(x)
    return jnp.concatenate([jnp.where(lane,x,z),jnp.where(lane,z,x)],axis=0)

def join_heads(x):
    n=x.shape[0]//2
    lane=lax.broadcasted_iota(jnp.int32,(1,2*64),1)<64
    return jnp.where(lane,x[:n],x[n:])

def fwd_kernel(order, qkv, q16, qinfo, kinfo, att, att16, canon, of, lse, of16, lse16):
    n_p=qkv.shape[0]//PIECE
    for i in range(n_p):
        src=pl.ds(pl.multiple_of(order[i]*PIECE,PIECE),PIECE)
        canon[i*PIECE:(i+1)*PIECE,:]=qkv[src,0:384]
    def rows(start,size,parts):
        qh=split_heads(canon[pl.ds(start,size),0:128])
        ss=[]
        for ks,kn,mask in parts:
            s=contract(qh,canon[pl.ds(ks,kn),128:256],1,1)
            if mask is not None:
                m2=jnp.concatenate([mask,mask],axis=0)
                s=jnp.where(m2,s,NEGATIVE)
            ss.append(s)
        top=functools.reduce(jnp.maximum,[jnp.max(s,axis=1,keepdims=True) for s in ss])
        tot=0.; o=0.
        for (ks,kn,_),s in zip(parts,ss):
            e=jnp.exp(s-top)
            tot=tot+jnp.sum(e,axis=1,keepdims=True)
            o=o+contract(e.astype(BF16),canon[pl.ds(ks,kn),256:384],1,0)
        o=join_heads(o*(1.0/tot))
        of[pl.ds(start,size),:]=o
        l=top+jnp.log(tot)
        lse[pl.ds(start,size),:]=join_heads(jnp.broadcast_to(l,(2*size,128)))
    t=tri(256)
    for b in range(4):
        parts=[(b*256,256,t)]
        if b: parts.insert(0,(0,b*256,None))
        rows(b*256,256,parts)
    bm=branch_mask()
    def branch(b,_):
        st=pl.multiple_of(TRUNK+b*BRANCH,PIECE)
        rows(st,BRANCH,[(0,TRUNK,None),(st,BRANCH,bm)])
        return 0
    lax.fori_loop(0,4,branch,0)
    for i in range(n_p):
        dst=pl.ds(pl.multiple_of(order[i]*PIECE,PIECE),PIECE)
        att[dst,:]=of[i*PIECE:(i+1)*PIECE,:].astype(BF16)
    s=contract(q16[...],qkv[:,384:512],1,1)
    s=jnp.where(allowed_mask(qinfo,kinfo),s,NEGATIVE)
    top=jnp.max(s,axis=1,keepdims=True)
    e=jnp.exp(s-top)
    tot=jnp.sum(e,axis=1,keepdims=True)
    o=contract(e.astype(BF16),qkv[:,384:512],1,0)*(1.0/tot)
    of16[...]=o
    att16[...]=pltpu.roll(o,64,1).astype(BF16)
    lse16[...]=jnp.broadcast_to(top+jnp.log(tot),o.shape)

def allowed_mask(qinfo,kinfo):
    ks=kinfo[0:1,:]; kp=kinfo[1:2,:]
    return ((ks==qinfo[:,0:1])|(ks==qinfo[:,1:2])|(ks==qinfo[:,2:3]))&(kp<=qinfo[:,3:4])

def attention_forward(order,qkv,q16,qinfo,kinfo):
    n=qkv.shape[0]; r=q16.shape[0]
    sd=jax.ShapeDtypeStruct
    V=pl.BlockSpec(memory_space=pltpu.VMEM)
    return pl.pallas_call(fwd_kernel,
        in_specs=[pl.BlockSpec(memory_space=pltpu.SMEM)]+[V]*4,
        out_specs=[V]*7,
        out_shape=[sd((n,128),BF16),sd((r,128),BF16),sd((n,384),BF16),sd((n,128),F32),sd((n,128),F32),sd((r,128),F32),sd((r,128),F32)],
        compiler_params=pltpu.CompilerParams(vmem_limit_bytes=60<<20),
        cost_estimate=pl.CostEstimate(flops=20_000_000_000,bytes_accessed=8_000_000,transcendentals=7_000_000),
        name="tree_attention_forward",
    )(order,qkv,q16,qinfo,kinfo)

def bwd_kernel(order, canon, of, lse, datt, kv16, q16, of16, lse16, datt16, qinfo, kinfo, dqkv, dq16, dc, dacc):
    n_p=canon.shape[0]//PIECE
    for i in range(n_p):
        src=pl.ds(pl.multiple_of(order[i]*PIECE,PIECE),PIECE)
        dc[i*PIECE:(i+1)*PIECE,:]=datt[src,:]
    def rows(start,size,parts):
        r=pl.ds(start,size)
        qh=split_heads(canon[r,0:128])
        d=dc[r,:]
        dh=split_heads(d)
        prod=d.astype(F32)*of[r,:]
        delta=jnp.concatenate([jnp.sum(prod[:,0:64],axis=1,keepdims=True),jnp.sum(prod[:,64:128],axis=1,keepdims=True)],axis=0)
        l=jnp.concatenate([lse[r,0:1],lse[r,64:65]],axis=0)
        dq=0.
        for ks,kn,mask,first in parts:
            kk=canon[pl.ds(ks,kn),128:256]
            s=contract(qh,kk,1,1)
            if mask is not None:
                s=jnp.where(jnp.concatenate([mask,mask],axis=0),s,NEGATIVE)
            p=jnp.exp(s-l)
            dp=contract(dh,canon[pl.ds(ks,kn),256:384],1,1)
            ds=(p*(dp-delta)).astype(BF16)
            dv=contract(p.astype(BF16),dh,0,0)
            dk=contract(ds,qh,0,0)
            dq=dq+contract(ds,kk,1,0)
            if first:
                dacc[pl.ds(ks,kn),128:256]=dk
                dacc[pl.ds(ks,kn),256:384]=dv
            else:
                dacc[pl.ds(ks,kn),128:256]+=dk
                dacc[pl.ds(ks,kn),256:384]+=dv
        dacc[r,0:128]=join_heads(dq)
    t=tri(256)
    for b in range(4):
        parts=[(b*256,256,t,True)]
        if b: parts.insert(0,(0,b*256,None,False))
        rows(b*256,256,parts)
    bm=branch_mask()
    def branch(b,_):
        st=pl.multiple_of(TRUNK+b*BRANCH,PIECE)
        rows(st,BRANCH,[(0,TRUNK,None,False),(st,BRANCH,bm,True)])
        return 0
    lax.fori_loop(0,4,branch,0)
    for i in range(n_p):
        dst=pl.ds(pl.multiple_of(order[i]*PIECE,PIECE),PIECE)
        x=dacc[i*PIECE:(i+1)*PIECE,:]
        dqkv[dst,0:128]=(x[:,0:128]*0.125).astype(BF16)
        dqkv[dst,128:384]=x[:,128:384].astype(BF16)
    k16=kv16[:,384:512]
    s=contract(q16[...],k16,1,1)
    s=jnp.where(allowed_mask(qinfo,kinfo),s,NEGATIVE)
    p=jnp.exp(s-lse16[:,0:1])
    dp=contract(datt16[...],k16,1,1)
    delta=jnp.sum(datt16[...].astype(F32)*of16[...],axis=1,keepdims=True)
    ds=(p*(dp-delta)).astype(BF16)
    dqkv[:,384:512]=(contract(ds,q16[...],0,0)+contract(p.astype(BF16),datt16[...],0,0)).astype(BF16)
    lane=lax.broadcasted_iota(jnp.int32,(1,128),1)>=64
    dq=pltpu.roll(contract(ds,k16,1,0)*0.125,64,1)
    dq16[...]=jnp.where(lane,dq,0.0).astype(BF16)

def attention_backward(order,canon,of,lse,datt,qkv,q16,of16,lse16,datt16,qinfo,kinfo):
    n=canon.shape[0]; r=q16.shape[0]
    sd=jax.ShapeDtypeStruct
    V=pl.BlockSpec(memory_space=pltpu.VMEM)
    return pl.pallas_call(bwd_kernel,
        in_specs=[pl.BlockSpec(memory_space=pltpu.SMEM)]+[V]*11,
        out_specs=[V]*2,
        out_shape=[sd((n,512),BF16),sd((r,128),BF16)],
        scratch_shapes=[pltpu.VMEM((n,128),BF16),pltpu.VMEM((n,384),F32)],
        compiler_params=pltpu.CompilerParams(vmem_limit_bytes=60<<20),
        cost_estimate=pl.CostEstimate(flops=50_000_000_000,bytes_accessed=15_000_000,transcendentals=7_000_000),
        name="tree_attention_backward",
    )(order,canon,of,lse,datt,qkv,q16,of16,lse16,datt16,qinfo,kinfo)


def parent_lookup(identities, shifted_table):
    labels = jnp.arange(shifted_table.shape[0], dtype=jnp.int32)
    matches = identities[:, None] == labels[None, :]
    return jnp.sum(jnp.where(matches, shifted_table[None, :], 0), axis=1) - 1


def tree_order(segments, places, parent):
    own = segments.reshape(-1, PIECE)[:, 0]
    start = places.reshape(-1, PIECE)[:, 0]
    table = parent + 1
    first_up = parent_lookup(own, table)
    second_up = parent_lookup(first_up, table)
    is_branch = (first_up >= 0) & (second_up < 0)
    is_leaf = second_up >= 0
    branch = jnp.where(is_leaf, first_up, own)
    rank = jnp.sum((is_branch[None, :] & (own[None, :] < branch[:, None])).astype(jnp.int32), axis=1)
    twin = is_leaf[None, :] & (first_up[None, :] == first_up[:, None]) & (own[None, :] < own[:, None])
    leaf = 1 + jnp.sum(twin.astype(jnp.int32), axis=1)
    target = jnp.where(
        first_up < 0, start // PIECE, TRUNK // PIECE + 3 * rank + jnp.where(is_leaf, leaf, 0)
    )
    pieces = jnp.arange(own.shape[0], dtype=jnp.int32)
    order = jnp.sum(jnp.where(target[None, :] == pieces[:, None], pieces[None, :], 0), axis=1)
    return order, first_up, second_up


def local(
    tokens,
    cotangent,
    segment_of,
    position_of,
    parent,
    ln1_gain,
    ln1_bias,
    w_qkv,
    b_query,
    b_value,
    w_out,
    b_out,
    ln2_gain,
    ln2_bias,
    w_fc,
    b_fc,
    w_proj,
    b_proj,
):
    rows = tokens.shape[0]
    half = w_qkv.shape[0]
    shard = lax.axis_index("shard")
    tensor, context, me = place()
    members = 2 * lax.axis_size("tensor")
    tree_rows = members * rows
    low = shard == 0

    held = (ln1_gain, ln1_bias, b_query, b_value, b_out, ln2_gain, ln2_bias, b_proj)
    spare = -half % PIECE
    flat = jnp.concatenate([part for value in held for part in (value, jnp.zeros((spare,), BF16))])
    vectors = flat.reshape(len(held), half + spare)[:, :half].astype(F32)
    zeros = jnp.zeros_like(vectors)
    half_vectors = jnp.concatenate(
        [jnp.where(low, vectors, zeros), jnp.where(low, zeros, vectors)], axis=1
    )
    proj_mine = w_proj.T
    normed_all, mixed, query_last, vectors, weight, fc_other = project(tokens, w_qkv, half_vectors, w_fc)
    proj_give, cotangent_give, mixed = lax.optimization_barrier((proj_mine, cotangent, mixed))
    proj_other = swap(proj_give, "shard", 0)
    cotangent_far = swap(cotangent_give, "tensor", 1)

    tree_start = lax.div(context, 2) * tree_rows
    segments = lax.dynamic_slice_in_dim(segment_of, tree_start, tree_rows)
    places = lax.dynamic_slice_in_dim(position_of, tree_start, tree_rows)
    order, first_up, second_up = tree_order(segments, places, parent)
    key_info = jnp.stack([segments, places])
    query_info = jnp.stack(
        [segments, jnp.repeat(first_up, PIECE), jnp.repeat(second_up, PIECE), places], axis=1
    )
    query_info = lax.dynamic_slice_in_dim(query_info, me * rows, rows, 0)

    attended_pair, attended_last, sorted_qkv, exact, level, exact_last, level_last = attention_forward(
        order, mixed, query_last, query_info, key_info
    )
    residual, fed_give, d_middle, d_pair, d_last, joint_keep, joint_give, fc_keep, fc_give, proj_sum, sums = feed_forward(
        attended_pair,
        attended_last,
        tokens,
        cotangent,
        cotangent_far,
        w_out,
        w_fc,
        fc_other,
        proj_mine,
        proj_other,
        vectors,
        b_fc.astype(F32)[None, :],
    )

    fc_got = swap(fc_give, "shard", 0)
    joint_other = swap(joint_give, "tensor", 1)
    fed_other = swap(fed_give, "tensor", 1)
    proj_sum = lax.psum(proj_sum, "context")

    d_mixed, d_query_last = attention_backward(
        order, sorted_qkv, exact, level, d_pair, mixed, query_last, exact_last, level_last, d_last,
        query_info, key_info,
    )
    fc_got, joint_other, fed_other, d_mixed = lax.optimization_barrier(
        (fc_got, joint_other, fed_other, d_mixed)
    )
    fc_sum = (fc_keep.astype(F32) + fc_got.astype(F32)).astype(BF16)
    fc_sum = lax.psum(
        fc_sum, "context", axis_index_groups=[list(range(lax.axis_size("context")))[::-1]]
    )
    output, d_inputs, pairs, joint_all, sums = finish(
        d_mixed,
        d_query_last,
        normed_all,
        weight,
        tokens,
        d_middle,
        vectors,
        joint_keep,
        joint_other,
        sums,
        residual,
        fed_other,
    )
    proj_sum, fc_sum, sums = lax.optimization_barrier((proj_sum, fc_sum, sums))
    own_mixer, own_out, own_fc = write_gradients(pairs, joint_all, fc_sum)
    own_proj = proj_sum.T.astype(F32)
    mine = lax.dynamic_slice_in_dim(sums[:8], shard * half, half, 1)
    own_bias_fc = lax.dynamic_slice_in_dim(sums, 8 + tensor, 1, 0)[0]
    return (
        output,
        d_inputs,
        mine[0],
        mine[1],
        own_mixer,
        mine[2],
        mine[3],
        own_out,
        mine[4],
        mine[5],
        mine[6],
        own_fc,
        own_bias_fc,
        own_proj,
        mine[7],
    )


def solution(mesh):
    return jax.shard_map(
        local,
        mesh=mesh,
        in_specs=(
            P(("shard", "context", "tensor"), None),
            P(("shard", "context", "tensor"), None),
            P("shard"),
            P("shard"),
            P(),
            P("shard"),
            P("shard"),
            P("shard", None),
            P("shard"),
            P("shard"),
            P("shard", None),
            P("shard"),
            P("shard"),
            P("shard"),
            P("shard", "tensor"),
            P("tensor"),
            P("tensor", "shard"),
            P("shard"),
        ),
        out_specs=(
            P(("shard", "context", "tensor"), None),
            P(("shard", "context", "tensor"), None),
            P("shard"),
            P("shard"),
            P("shard", None),
            P("shard"),
            P("shard"),
            P("shard", None),
            P("shard"),
            P("shard"),
            P("shard"),
            P("shard", "tensor"),
            P("tensor"),
            P("tensor", "shard"),
            P("shard"),
        ),
        check_vma=False,
    )
```

```python
import functools

import jax
import jax.numpy as jnp
from jax import lax
from jax.experimental import pallas as pl
from jax.experimental.pallas import tpu as pltpu
from jax.sharding import PartitionSpec as P

HEAD_DIM = 64
PAIR = 2 * HEAD_DIM
PIECE = 128
TRUNK = 8 * PIECE
BRANCH = 3 * PIECE
EPSILON = 1e-05
NEGATIVE = -1e30
F32 = jnp.float32
BF16 = jnp.bfloat16
VMEM = pl.BlockSpec(memory_space=pltpu.VMEM)
SMEM = pl.BlockSpec(memory_space=pltpu.SMEM)
ANY = pl.BlockSpec(memory_space=pl.ANY)
MESH = pl.DeviceIdType.MESH


def contract(left, right, left_dim, right_dim):
    return lax.dot_general(
        left, right, (((left_dim,), (right_dim,)), ((), ())), preferred_element_type=F32
    )


def flip(value, bit):
    low = 1 << bit
    return value + low - 2 * low * lax.rem(lax.div(value, low), 2)


def place():
    tensor, context = lax.axis_index("tensor"), lax.axis_index("context")
    return tensor, context, lax.rem(context, 2) * lax.axis_size("tensor") + tensor


def member(mask):
    tensor, context, _ = place()
    size = lax.axis_size("tensor")
    bits = size.bit_length() - 1
    for bit in range(bits):
        if mask >> bit & 1:
            tensor = flip(tensor, bit)
    if mask >> bits & 1:
        context = flip(context, 0)
    return {"context": context, "tensor": tensor}, lax.rem(context, 2) * size + tensor


def swap(value, axis, bit):
    size = lax.axis_size(axis)
    return lax.ppermute(value, axis, [(i, i ^ 1 << bit) for i in range(size)])


class Wires:
    def __init__(self, send, recv):
        self.send, self.recv, self.used = send, recv, 0

    def start(self, source, target, device):
        assert self.used < self.send.shape[0]
        copy = pltpu.make_async_remote_copy(
            src_ref=source,
            dst_ref=target,
            send_sem=self.send.at[self.used],
            recv_sem=self.recv.at[self.used],
            device_id=device,
            device_id_type=MESH,
        )
        self.used += 1
        copy.start()
        return copy


def by_rows(rows, step, body, first=0):
    def run(i, carry):
        body(pl.ds(pl.multiple_of(first + i * step, step), step))
        return carry

    lax.fori_loop(0, rows // step, run, 0)


def norm_backward(values, grad, gain):
    average = jnp.mean(values, axis=1, keepdims=True)
    centered = values - average
    inverse = lax.rsqrt(jnp.mean(centered * centered, axis=1, keepdims=True) + EPSILON)
    normal = centered * inverse
    scaled = grad * gain
    result = inverse * (
        scaled
        - jnp.mean(scaled, axis=1, keepdims=True)
        - normal * jnp.mean(scaled * normal, axis=1, keepdims=True)
    )
    return result, jnp.sum(grad * normal, axis=0, keepdims=True), jnp.sum(grad, axis=0, keepdims=True)


def norm_forward(values, gain, shift):
    average = jnp.mean(values, axis=1, keepdims=True)
    centered = values - average
    spread = jnp.mean(centered * centered, axis=1, keepdims=True)
    return centered * lax.rsqrt(spread + EPSILON) * gain + shift


def project_kernel(
    tokens, w_all, half_vectors, w_fc, normed_out, mixed_out, query_last, vectors, weight, fc_other, normed, mixed, everyone, w_qkv, seen, local_sem, out_sem, send, recv
):
    tensor, context, me = place()
    shard = lax.axis_index("shard")
    members = 2 * lax.axis_size("tensor")
    rows, width = tokens.shape
    half = width // 2
    cut = rows // 2
    shared = width - HEAD_DIM
    across = {"shard": 1 - shard}
    wires = Wires(send, recv)
    turn = members // 2

    load = pltpu.make_async_copy(w_all, w_qkv, local_sem.at[1])
    load.start()
    barrier = pltpu.get_barrier_semaphore()
    peers = [member(mask)[0] for mask in (1, 2, turn)] + [across]
    rest = [m for m in range(4, members) if m & 1 == 0 and m not in (turn, turn + 2)]
    for peer in peers:
        pl.semaphore_signal(barrier, inc=1, device_id=peer, device_id_type=MESH)
    pl.semaphore_wait(barrier, len(peers))
    assert not rest

    def slot(owner, first=0, size=rows):
        index = member(owner)[1] * rows + first
        return everyone.at[pl.ds(pl.multiple_of(index, 16), size)]

    def hand(source, target):
        return wires.start(source, source, member(target)[0])

    own = pltpu.make_async_copy(tokens, slot(0), local_sem.at[0])
    own.start()
    far = {m: wires.start(tokens, slot(0), member(m)[0]) for m in (2, turn)}
    vector_wire = wires.start(half_vectors, seen, across)
    close = {0: wires.start(tokens, slot(0), member(1)[0])}
    lane = lax.broadcasted_iota(jnp.int32, (1, PAIR), 1) < HEAD_DIM

    def choose(i, carry):
        r = pl.ds(pl.multiple_of(i * 32, 32), 32)
        to = pl.ds(pl.multiple_of(shard * half + i * 32, 32), 32)

        def window(start, size=PAIR):
            return w_qkv[r, pl.ds(pl.multiple_of(start, PAIR), size)]

        def turned(value):
            return pltpu.roll(value.astype(F32), HEAD_DIM, 1)

        weight[to, 0:PAIR] = window(me * PAIR)
        left, right = window(shared + me * PAIR), window(shared + (me + 1) * PAIR)
        weight[to, PAIR : 2 * PAIR] = jnp.where(lane, turned(left), turned(right)).astype(BF16)
        weight[to, 2 * PAIR : 3 * PAIR] = window(2 * width + me * PAIR)
        value = w_qkv[r, 2 * width + shared :]
        value = jnp.concatenate([value, value], axis=1)
        key = turned(w_qkv[r, 2 * width - PAIR : 2 * width])
        weight[to, 3 * PAIR : 4 * PAIR] = jnp.where(lane, key, value.astype(F32)).astype(BF16)
        query = w_qkv[r, shared : shared + PAIR]
        weight[to, 4 * PAIR :] = jnp.where(lane, query, jnp.zeros_like(query))
        return carry

    load.wait()
    lax.fori_loop(0, half // 32, choose, 0)
    chosen = weight.at[pl.ds(pl.multiple_of(shard * half, half), half)]
    weight_wire = wires.start(chosen, chosen, across)
    fc_wire = wires.start(w_fc.at[0 : half // 2], fc_other, across)

    vector_wire.wait_recv()
    vectors[...] = half_vectors[...] + seen[...]
    gain, shift = vectors[0:1, :], vectors[1:2, :]
    scale = HEAD_DIM ** (-0.5)
    pair_lanes = pl.ds(pl.multiple_of(me * PAIR, PAIR), PAIR)
    bias_query, bias_value = vectors[2:3, pair_lanes], vectors[3:4, pair_lanes]
    value_tail = vectors[3:4, shared:]
    bias_last = jnp.where(lane, 0.0, jnp.concatenate([value_tail, value_tail], axis=1))
    query_tail = vectors[2:3, shared:]
    query_tail = jnp.where(lane, jnp.concatenate([query_tail, query_tail], axis=1), 0.0)

    stored = []

    def put(source, target, owner, first):
        r = pl.ds(pl.multiple_of(member(owner)[1] * rows, rows), rows)
        stored.append(pltpu.make_async_copy(source.at[r], target.at[r], out_sem.at[first + owner]))
        stored[-1].start()

    def normalise(owner, first=0, size=rows):
        index = member(owner)[1] * rows + first

        def run(i, carry):
            r = pl.ds(pl.multiple_of(index + i * 32, 32), 32)
            normed[r, :] = norm_forward(everyone[r, :].astype(F32), gain, shift).astype(BF16)
            return carry

        lax.fori_loop(0, size // 32, run, 0)
        put(normed, normed_out, owner, 0)

    def multiply(owner, first=0, size=rows):
        r = pl.ds(pl.multiple_of(member(owner)[1] * rows + first, 32), size)
        result = jnp.dot(normed[r, :], weight[:, 0 : 4 * PAIR], preferred_element_type=F32)
        mixed[r, 0:PAIR] = ((result[:, 0:PAIR] + bias_query) * scale).astype(BF16)
        mixed[r, PAIR : 2 * PAIR] = result[:, PAIR : 2 * PAIR].astype(BF16)
        mixed[r, 2 * PAIR : 3 * PAIR] = (result[:, 2 * PAIR : 3 * PAIR] + bias_value).astype(BF16)
        mixed[r, 3 * PAIR :] = (result[:, 3 * PAIR :] + bias_last).astype(BF16)
        put(mixed, mixed_out, owner, members)

    own.wait()
    normalise(0)
    close[0].wait_recv()
    normalise(1)
    pieces = {}
    for m, other, first in ((2, turn, 0), (turn, 2, cut)):
        far[m].wait_recv()
        close[m] = hand(slot(m), 1)
        pieces[other] = hand(slot(m, first, cut), other)
    weight_wire.wait_recv()
    multiply(0)
    last = jnp.dot(
        normed[pl.ds(pl.multiple_of(me * rows, 32), rows), :], weight[:, 4 * PAIR :], preferred_element_type=F32
    )
    query_last[...] = ((last + query_tail) * scale).astype(BF16)
    multiply(1)
    for m in (2, turn):
        normalise(m)
        multiply(m)
    for m in (2, turn):
        close[m].wait_recv()
        normalise(m ^ 1)
        multiply(m ^ 1)
    opposite = 2 ^ turn
    passed = []
    for m, first in ((turn, 0), (2, cut)):
        pieces[m].wait_recv()
        passed.append(hand(slot(opposite, first, cut), 1))
    normalise(opposite)
    multiply(opposite)
    for wire in passed:
        wire.wait_recv()
    normalise(opposite ^ 1)
    multiply(opposite ^ 1)
    fc_wire.wait_recv()
    for copy in stored:
        copy.wait()
    for wire in list(far.values()) + list(close.values()) + list(pieces.values()) + passed + [vector_wire, weight_wire, fc_wire]:
        wire.wait_send()


def project(tokens, w_qkv, half_vectors, w_fc):
    rows, width = tokens.shape
    tree = 2 * lax.axis_size("tensor") * rows
    shape = jax.ShapeDtypeStruct
    return pl.pallas_call(
        project_kernel,
        in_specs=[VMEM, ANY, VMEM, ANY],
        out_specs=[ANY] * 2 + [VMEM] * 3 + [ANY],
        out_shape=[
            shape((tree, width), BF16),
            shape((tree, 4 * PAIR), BF16),
            shape((rows, PAIR), BF16),
            shape(half_vectors.shape, F32),
            shape((width, 5 * PAIR), BF16),
            shape((w_fc.shape[0] // 2, w_fc.shape[1]), BF16),
        ],
        scratch_shapes=[
            pltpu.VMEM((tree, width), BF16),
            pltpu.VMEM((tree, 4 * PAIR), BF16),
            pltpu.VMEM((tree, width), BF16),
            pltpu.VMEM(w_qkv.shape, BF16),
            pltpu.VMEM(half_vectors.shape, F32),
            pltpu.SemaphoreType.DMA((2,)),
            pltpu.SemaphoreType.DMA((2 * (tree // rows),)),
            pltpu.SemaphoreType.DMA((16,)),
            pltpu.SemaphoreType.DMA((16,)),
        ],
        compiler_params=pltpu.CompilerParams(
            collective_id=0, has_side_effects=True, vmem_limit_bytes=60 << 20
        ),
        name="project",
    )(tokens, w_qkv, half_vectors, w_fc)


def feed_forward_kernel(
    pair,
    last,
    tokens_all,
    cotangent,
    cotangent_far,
    out_mine,
    fc_mine,
    fc_other,
    proj_mine,
    proj_other,
    vectors,
    bias_fc,
    residual,
    fed_give,
    d_middle,
    d_pair,
    d_last,
    joint_keep,
    joint_give,
    fc_keep,
    fc_give,
    proj_sum,
    sums,
    w_out,
    w_fc,
    w_proj,
    attended,
    middle,
    normed,
    hidden,
    d_before,
    d_hidden,
    part,
    near,
    passing,
    far,
    d_attn,
    d_attended,
    grads,
    proj_keep,
    proj_give,
    proj_got,
    joint,
    joint_near,
    tokens,
    local_sem,
    send,
    recv,
):
    tensor, context, me = place()
    shard = lax.axis_index("shard")
    near_bit = lax.rem(tensor, 2)
    members = 2 * lax.axis_size("tensor")
    rows, width = tokens.shape
    half = width // 2
    shared = width - HEAD_DIM
    group = range(1, members)
    wires = Wires(send, recv)
    bias_out, gain, shift, bias_proj = (vectors[i : i + 1, :] for i in (4, 5, 6, 7))
    across = {"shard": 1 - shard}

    barrier = pltpu.get_barrier_semaphore()
    peers = [member(mask)[0] for mask in group] + [across]
    for peer in peers:
        pl.semaphore_signal(barrier, inc=1, device_id=peer, device_id_type=MESH)
    pl.semaphore_wait(barrier, len(peers))

    def slab(ref, index, size):
        return ref.at[pl.ds(pl.multiple_of(index * size, size), size)]

    def beside(ref, index):
        return ref.at[:, pl.ds(pl.multiple_of(index * PAIR, PAIR), PAIR)]

    moved = []
    for mask in group:
        device, index = member(mask)
        moved.append(wires.start(slab(pair, index, rows), beside(attended, me), device))
    quarter = half // 2
    out_wire = wires.start(
        slab(out_mine, near_bit, quarter), slab(w_out, 2 * shard + near_bit, quarter), across
    )
    local = [
        pltpu.make_async_copy(source, target, local_sem.at[i])
        for i, (source, target) in enumerate(
            (
                (slab(pair, me, rows), beside(attended, me)),
                (out_mine, slab(w_out, shard, half)),
                (fc_mine, slab(w_fc, shard, half)),
                (fc_other, slab(w_fc, 2 * (1 - shard), quarter)),
                (proj_mine, slab(w_proj, shard, half)),
                (proj_other, slab(w_proj, 1 - shard, half)),
                (tokens_all, tokens),
                (cotangent, slab(grads, 0, rows)),
                (cotangent_far, slab(grads, 2, rows)),
            )
        )
    ]
    pulled_wires = [
        wires.start(source, slab(grads, index, rows), member(1)[0])
        for index, source in ((1, cotangent), (3, cotangent_far))
    ]
    for copy in local:
        copy.start()
    attended[:, shared:] = last[:, 0:HEAD_DIM]
    out_wire.wait_recv()
    out_part = slab(w_out, 2 * (1 - shard) + near_bit, quarter)
    out_near = wires.start(out_part, out_part, member(1)[0])
    fc_wire = wires.start(
        fc_mine.at[quarter:half], slab(w_fc, 2 * shard + 1, quarter), across
    )
    for copy in local:
        copy.wait()
    for wire in moved + [out_near]:
        wire.wait_recv()

    start = 0
    while start < width:
        stop = min(start + 2 * PAIR, width)
        middle[:, start:stop] = (
            tokens[:, start:stop].astype(F32)
            + jnp.dot(attended[...], w_out[:, start:stop], preferred_element_type=F32)
            + bias_out[:, start:stop]
        )
        start = stop

    def second_norm(r):
        normed[r, :] = norm_forward(middle[r, :], gain, shift).astype(BF16)

    cut = rows // 2

    def piece(mask, i):
        return slice(mask * rows + i * cut, mask * rows + (i + 1) * cut)

    cross = []
    for i in range(2):
        by_rows(cut, 32, second_norm, i * cut)
        cross.append(wires.start(normed.at[piece(0, i)], normed.at[piece(2, i)], member(2)[0]))

    def block(ref, mask):
        return ref.at[mask * rows : (mask + 1) * rows, :]

    close = wires.start(block(normed, 0), block(normed, 1), member(1)[0])
    for wire in pulled_wires:
        wire.wait_recv()
    for mask in range(4):
        block(d_hidden, mask)[...] = jnp.dot(
            block(grads, mask)[...], w_proj[...], preferred_element_type=F32
        )

    def feed(r):
        start = 0
        while start < width:
            stop = min(start + 2 * PAIR, width)
            c = slice(start, stop)
            before = jnp.dot(normed[r, :], w_fc[:, c], preferred_element_type=F32) + bias_fc[0:1, c]
            cumulative = 0.5 + 0.5 * lax.erf(before * (0.5**0.5))
            hidden[r, c] = (before * cumulative).astype(BF16)
            slope = cumulative + before * jnp.exp(-0.5 * before * before) * ((2 * jnp.pi) ** -0.5)
            d_before[r, c] = (d_hidden[r, c] * slope).astype(BF16)
            start = stop

    def back(r):
        return contract(d_before[r, :], w_fc[...], 1, 1)

    def ahead(mask):
        return contract(hidden[mask * rows : (mask + 1) * rows, :], w_proj[...], 1, 1)

    fc_wire.wait_recv()
    feed(slice(0, rows))
    close.wait_recv()
    feed(slice(rows, 2 * rows))
    part[0] = back(slice(rows, 2 * rows)).astype(BF16)
    to_near = wires.start(part.at[0], near.at[0], member(1)[0])
    relay, to_pass, to_far = [], [], []
    for i in range(2):
        h = slice(i * cut, (i + 1) * cut)
        cross[i].wait_recv()
        relay.append(wires.start(normed.at[piece(2, i)], normed.at[piece(3, i)], member(1)[0]))
        feed(piece(2, i))
        relay[i].wait_recv()
        feed(piece(3, i))
        part[1, h] = back(piece(3, i)).astype(BF16)
        to_pass.append(wires.start(part.at[1, h], near.at[1, h], member(1)[0]))
        mine = back(piece(2, i))
        to_pass[i].wait_recv()
        passing[h] = (mine + near[1, h].astype(F32)).astype(BF16)
        to_far.append(wires.start(passing.at[h], far.at[h], member(2)[0]))

    other_part = pl.ds(pl.multiple_of(2 * rows + (1 - shard) * half, 8), half)
    own_part = pl.ds(pl.multiple_of(2 * rows + shard * half, 8), half)
    proj_wires = []
    start = 0
    while start < width:
        stop = min(start + 2 * PAIR, width)
        c = slice(start, stop)
        d_hidden_part = d_hidden.at[2 * rows : 2 * rows + width, 0 : stop - start]
        d_hidden_part[...] = contract(grads[...], hidden[:, c], 0, 0)
        proj_give[:, c] = d_hidden[other_part, 0 : stop - start].astype(BF16)
        proj_wires.append(wires.start(proj_give.at[:, c], proj_got.at[:, c], across))
        proj_keep[:, c] = d_hidden[own_part, 0 : stop - start]
        start = stop
    start = 0
    while start < width:
        stop = min(start + 2 * PAIR, width)
        c = slice(start, stop)
        d_hidden_part = d_hidden.at[2 * rows : 2 * rows + width, 0 : stop - start]
        d_hidden_part[...] = contract(normed[...], d_before[:, c], 0, 0)
        fc_give[:, c] = d_hidden[other_part, 0 : stop - start].astype(BF16)
        fc_keep[:, c] = d_hidden[own_part, 0 : stop - start].astype(BF16)
        start = stop
    d_hidden[0:rows, :] = back(slice(0, rows))
    to_near.wait_recv()
    for wire in to_far:
        wire.wait_recv()

    sums[...] = jnp.zeros_like(sums)

    def second_back(r):
        grad = d_hidden[r, :] + near[0, r, :].astype(F32) + far[r, :].astype(F32)
        result, by_gain, by_shift = norm_backward(middle[r, :], grad, gain)
        pulled = grads[r, :].astype(F32)
        result = result + pulled
        d_middle[r, :] = result
        low = result.astype(BF16)
        d_attn[r, 0:width] = low
        d_attn[r, width:] = jnp.zeros((r.size, d_attn.shape[1] - width), BF16)
        sums[4:5, :] += jnp.sum(low.astype(F32), axis=0, keepdims=True)
        sums[5:6, :] += by_gain
        sums[6:7, :] += by_shift
        sums[7:8, :] += jnp.sum(pulled, axis=0, keepdims=True)

    by_rows(rows, 64, second_back)
    start = 0
    while start < width:
        stop = min(start + 2 * PAIR, width)
        d_attended[:, start:stop] = contract(d_attn[:, 0:width], w_out[start:stop, :], 1, 1).astype(BF16)
        start = stop
    returned = []
    for mask in group:
        device, index = member(mask)
        returned.append(wires.start(beside(d_attended, index), slab(d_pair, me, rows), device))
    own_copy = pltpu.make_async_copy(beside(d_attended, me), slab(d_pair, me, rows), local_sem.at[0])
    own_copy.start()
    lane = lax.broadcasted_iota(jnp.int32, (1, PAIR), 1) >= HEAD_DIM
    tail = jnp.concatenate([d_attended[:, shared:]] * 2, axis=1)
    d_last[...] = jnp.where(lane, tail, jnp.zeros_like(tail))
    joint[:, shared : shared + PAIR] = jnp.zeros((width, PAIR), BF16)
    start = 0
    while start < d_attn.shape[1]:
        stop = min(start + 2 * PAIR, d_attn.shape[1])
        to = start if start < shared else start + PAIR
        joint[:, to : to + stop - start] = contract(attended[...], d_attn[:, start:stop], 0, 0).astype(BF16)
        start = stop
    side = joint.shape[1] // 2
    kept = pl.ds(pl.multiple_of(near_bit * side, side), side)
    given = pl.ds(pl.multiple_of((1 - near_bit) * side, side), side)
    joint_wire = wires.start(joint.at[:, given], joint_near, member(1)[0])
    part[2] = ahead(3).astype(BF16)
    to_pass_out = wires.start(part.at[2], near.at[3], member(1)[0])
    part[3] = ahead(1).astype(BF16)
    to_near_out = wires.start(part.at[3], near.at[2], member(1)[0])
    d_hidden[2 * rows : 3 * rows, :] = ahead(2)
    d_hidden[rows : 2 * rows, :] = ahead(0)
    bias = jnp.zeros((1, width), F32)

    def add_bias(i, total):
        r = pl.ds(pl.multiple_of(i * 64, 64), 64)
        return total + jnp.sum(d_before[r, :].astype(F32), axis=0, keepdims=True)

    bias = lax.fori_loop(0, 4 * rows // 64, add_bias, bias)
    for i in range(lax.axis_size("tensor")):
        sums[8 + i : 9 + i, :] = jnp.where(tensor == i, bias, 0.0)
    to_near_out.wait_recv()
    to_pass_out.wait_recv()

    def finish_output(r):
        third = pl.ds(pl.multiple_of(2 * rows + r.start, 64), r.size)
        again = pl.ds(pl.multiple_of(rows + r.start, 64), r.size)
        fed_give[r, :] = (d_hidden[third, :] + near[3, r, :].astype(F32)).astype(BF16)
        residual[r, :] = middle[r, :] + d_hidden[again, :] + near[2, r, :].astype(F32) + bias_proj

    by_rows(rows, 64, finish_output)
    joint_wire.wait_recv()
    second = lax.rem(lax.div(tensor, 2), 2)

    def add_joint(target, which):
        for i in range(2):

            def run(r):
                source = pl.ds(pl.multiple_of((2 * i + which) * quarter - i * quarter + r.start, 16), r.size)
                total = joint[source, kept].astype(F32) + joint_near[source, :].astype(F32)
                target[r, :] = total.astype(BF16)

            by_rows(quarter, 16, run, i * quarter)

    add_joint(joint_keep, second)
    add_joint(joint_give, 1 - second)
    for wire in proj_wires:
        wire.wait_recv()

    def add_proj(r):
        proj_sum[r, :] = (proj_keep[r, :] + proj_got[r, :].astype(F32)).astype(BF16)

    by_rows(half, 32, add_proj)
    own_copy.wait()
    for wire in returned:
        wire.wait_recv()
    for wire in (
        moved + returned + [out_wire, out_near, fc_wire] + pulled_wires + proj_wires
        + cross + relay + to_pass + to_far + [joint_wire, close, to_near, to_near_out, to_pass_out]
    ):
        wire.wait_send()


def feed_forward(pair, last, tokens, cotangent, cotangent_far, out_mine, fc_mine, fc_other, proj_mine, proj_other, vectors, bias_fc):
    rows, width = tokens.shape
    members = 2 * lax.axis_size("tensor")
    hidden = fc_mine.shape[1]
    tall = 4 * rows
    shape = jax.ShapeDtypeStruct
    return pl.pallas_call(
        feed_forward_kernel,
        in_specs=[ANY, VMEM] + [ANY] * 8 + [VMEM] * 2,
        out_specs=[VMEM] * 3 + [ANY] + [VMEM] * 7,
        out_shape=[
            shape((rows, width), F32),
            shape((rows, width), BF16),
            shape((rows, width), F32),
            shape((members * rows, PAIR), BF16),
            shape((rows, PAIR), BF16),
            shape((width // 2, 5 * PAIR), BF16),
            shape((width // 2, 5 * PAIR), BF16),
            shape((width // 2, hidden), BF16),
            shape((width // 2, hidden), BF16),
            shape((width // 2, hidden), BF16),
            shape((16, width), F32),
        ],
        scratch_shapes=[
            pltpu.VMEM((width, width), BF16),
            pltpu.VMEM((width, hidden), BF16),
            pltpu.VMEM((width, hidden), BF16),
            pltpu.VMEM((rows, width), BF16),
            pltpu.VMEM((rows, width), F32),
            pltpu.VMEM((tall, width), BF16),
            pltpu.VMEM((tall, hidden), BF16),
            pltpu.VMEM((tall, hidden), BF16),
            pltpu.VMEM((2 * rows + max(2 * rows, width), hidden), F32),
            pltpu.VMEM((4, rows, width), BF16),
            pltpu.VMEM((4, rows, width), BF16),
            pltpu.VMEM((rows, width), BF16),
            pltpu.VMEM((rows, width), BF16),
            pltpu.VMEM((rows, 9 * PAIR), BF16),
            pltpu.VMEM((rows, width), BF16),
            pltpu.VMEM((tall, width), BF16),
            pltpu.VMEM((width // 2, hidden), F32),
            pltpu.VMEM((width // 2, hidden), BF16),
            pltpu.VMEM((width // 2, hidden), BF16),
            pltpu.VMEM((width, 10 * PAIR), BF16),
            pltpu.VMEM((width, 5 * PAIR), BF16),
            pltpu.VMEM((rows, width), BF16),
            pltpu.SemaphoreType.DMA((9,)),
            pltpu.SemaphoreType.DMA((2 * members + 24,)),
            pltpu.SemaphoreType.DMA((2 * members + 24,)),
        ],
        compiler_params=pltpu.CompilerParams(
            collective_id=3, has_side_effects=True, vmem_limit_bytes=62 << 20
        ),
        name="feed_forward",
    )(pair, last, tokens, cotangent, cotangent_far, out_mine, fc_mine, fc_other, proj_mine, proj_other, vectors, bias_fc)


def finish_kernel(
    d_mixed_all,
    d_query_last,
    normed_all,
    weight_all,
    tokens_all,
    d_middle_all,
    gain,
    joint_keep_all,
    joint_other_all,
    vectors,
    residual_all,
    fed_other_all,
    output,
    d_tokens,
    pairs,
    joint_all,
    sums,
    near_give,
    near_got,
    row_sum,
    second_got,
    turn_last,
    last_low,
    pair_t,
    pair,
    pair_give,
    pair_got,
    pair_low,
    pair_seen,
    tail,
    tail_near,
    tail_sum,
    tail_give,
    tail_got,
    joint_give,
    joint_got,
    half_low,
    half_seen,
    pair_sum,
    half_sum,
    vec,
    vec_give,
    vec_got,
    d_mixed,
    normed,
    weight,
    tokens,
    d_middle,
    joint_keep,
    joint_other,
    residual,
    fed_other,
    load_sem,
    send,
    recv,
):
    tensor, context, me = place()
    shard = lax.axis_index("shard")
    near = lax.rem(tensor, 2)
    second = lax.rem(lax.div(tensor, 2), 2)
    contexts = lax.axis_size("context")
    members = 2 * lax.axis_size("tensor")
    turn = members // 2
    rows, width = tokens.shape
    half = width // 2
    quarter = half // 2
    side = joint_keep.shape[1]
    shared = width - HEAD_DIM
    block = 4 * PAIR
    across = {"shard": 1 - shard}
    higher = [
        {"context": flip(context, bit)} for bit in range(1, contexts.bit_length() - 1)
    ]
    group = range(1, members)
    wires = Wires(send, recv)

    loads = [
        pltpu.make_async_copy(source, target, load_sem.at[i])
        for i, (source, target) in enumerate(
            (
                (d_mixed_all, d_mixed),
                (normed_all, normed),
                (weight_all, weight),
                (tokens_all, tokens),
                (d_middle_all, d_middle),
                (joint_keep_all, joint_keep),
                (joint_other_all, joint_other),
                (residual_all, residual),
                (fed_other_all, fed_other),
            )
        )
    ]
    for copy in loads:
        copy.start()
    barrier = pltpu.get_barrier_semaphore()
    peers = [member(mask)[0] for mask in group] + [across] + higher
    for peer in peers:
        pl.semaphore_signal(barrier, inc=1, device_id=peer, device_id_type=MESH)
    pl.semaphore_wait(barrier, len(peers))
    for copy in loads:
        copy.wait()

    def part(ref, index, size):
        return ref.at[pl.ds(pl.multiple_of(index * size, size), size)]

    def term(mask):
        r = pl.ds(pl.multiple_of(member(mask)[1] * rows, rows), rows)
        return contract(d_mixed[r, :], weight[:, 0:block], 1, 1)

    steps = d_mixed.shape[0] // (2 * rows)
    pair_t[...] = jnp.zeros_like(pair_t)

    def accumulate(i, carry):
        r = pl.ds(pl.multiple_of(i * 2 * rows, 2 * rows), 2 * rows)
        pair_t[...] += contract(d_mixed[r, :], normed[r, :], 0, 0)
        return carry

    lax.fori_loop(0, steps, accumulate, 0)
    pair[...] = pair_t[...].T
    other = pl.ds(pl.multiple_of((1 - shard) * half, half), half)
    own = pl.ds(pl.multiple_of(shard * half, half), half)
    pair_give[...] = pair[other, 0 : 3 * PAIR].astype(BF16)
    pair_wire = wires.start(pair_give, pair_got, across)
    mine = pl.ds(pl.multiple_of(me * rows, rows), rows)
    tail[:, 0:PAIR] = pair[:, 3 * PAIR :].astype(BF16)
    tail[:, PAIR:] = contract(d_query_last[...], normed[mine, :], 0, 0).T.astype(BF16)
    tail_near_wire = wires.start(tail, tail_near, member(1)[0])

    order = [6, 2, 4, 0]
    near_wires = {}
    for i, mask in enumerate(order):
        near_give[i] = term(mask ^ 1).astype(BF16)
        near_wires[mask] = wires.start(near_give.at[i], near_got.at[i], member(1)[0])

    tail_near_wire.wait_recv()

    def add_tail_near(r):
        tail_sum[r, :] = tail[r, :].astype(F32) + tail_near[r, :].astype(F32)

    by_rows(width, 64, add_tail_near)
    to_second, to_turn = member(2)[0], member(turn)[0]
    for i in range(2):
        source = pl.ds(pl.multiple_of(i * half + (1 - second) * quarter, 16), quarter)
        tail_give[i * quarter : (i + 1) * quarter, :] = tail_sum[source, :].astype(BF16)
    tail_wire = wires.start(tail_give, tail_got, to_second)

    second_wires = []
    for i, mask in enumerate(order):
        total = term(mask)
        if mask == 0:
            query = pltpu.roll(d_query_last[...].astype(F32), HEAD_DIM, 1).astype(BF16)
            total = total + contract(query, weight[:, block:], 1, 1)
        near_wires[mask].wait_recv()
        total = total + near_got[i].astype(F32)
        if i >= 2:
            row_sum[i - 2] = total
        if mask & 2:
            near_got[i] = total.astype(BF16)
            second_wires.append(wires.start(near_got.at[i], second_got.at[i], to_second))

    pair_wire.wait_recv()
    pair_own = pair[own, 0 : 3 * PAIR] + pair_got[...].astype(F32)
    pair_wires = []
    for i, device in enumerate(higher):
        pair_low[i] = pair_own.astype(BF16)
        wire = wires.start(pair_low.at[i], pair_seen.at[i], device)
        pair_wires.append(wire)
        if i < len(higher) - 1:
            wire.wait_recv()
            pair_own = pair_own + pair_seen[i].astype(F32)
    pair_sum[...] = pair_own

    tail_wire.wait_recv()
    wide = joint_keep.shape[1] - 2 * PAIR

    def joint_term(which):
        r = pl.ds(pl.multiple_of(which * quarter, quarter), quarter)
        s = pl.ds(pl.multiple_of(which * half + second * quarter, quarter), quarter)
        total = joint_keep[r, :].astype(F32) + joint_other[r, :].astype(F32)
        last = jnp.where(near == 1, tail_sum[s, :] + tail_got[r, :].astype(F32), 0.0)
        return jnp.concatenate([total[:, :wide], total[:, wide:] + last], axis=1)

    joint_give[...] = joint_term(1 - shard).astype(BF16)
    joint_wire = wires.start(joint_give, joint_got, across)

    vec[...] = vectors[...]

    def add_columns(i, total):
        r = pl.ds(pl.multiple_of(i * 64, 64), 64)
        return total + jnp.sum(d_mixed[r, :].astype(F32), axis=0, keepdims=True)

    columns = lax.fori_loop(0, d_mixed.shape[0] // 64, add_columns, jnp.zeros((1, block), F32))
    pair_lanes = pl.ds(pl.multiple_of(me * PAIR, PAIR), PAIR)
    vec[2:3, pair_lanes] = columns[:, 0:PAIR]
    vec[3:4, pair_lanes] = columns[:, 2 * PAIR : 3 * PAIR]
    query = jnp.sum(d_query_last[...].astype(F32), axis=0, keepdims=True)
    vec[2:3, shared:] = pltpu.roll(query, HEAD_DIM, 1)[:, :HEAD_DIM]
    vec[3:4, shared:] = pltpu.roll(columns[:, 3 * PAIR :], HEAD_DIM, 1)[:, :HEAD_DIM]


    def add_fed(r):
        output[r, :] = (residual[r, :] + fed_other[r, :].astype(F32)).astype(BF16)

    by_rows(rows, 64, add_fed)

    joint_wire.wait_recv()
    half_sum[...] = joint_term(shard) + joint_got[...].astype(F32)
    hops = [to_turn] + higher
    joint_wires = []

    def joint_hop(i):
        if i:
            joint_wires[-1].wait_recv()
            half_sum[...] += half_seen[i - 1].astype(F32)
        if i < len(hops):
            half_low[i] = half_sum[...].astype(BF16)
            joint_wires.append(wires.start(half_low.at[i], half_seen.at[i], hops[i]))

    joint_hop(0)

    second_wires[0].wait_recv()
    last_low[...] = (row_sum[0] + second_got[0].astype(F32)).astype(BF16)
    turn_wire = wires.start(last_low, turn_last, to_turn)

    for i in range(1, len(hops)):
        joint_hop(i)

    if pair_wires:
        pair_wires[-1].wait_recv()
        pair_sum[...] += pair_seen[len(higher) - 1].astype(F32)

    def slot(owner, start=0, size=half):
        return pairs.at[pl.ds(pl.multiple_of(member(owner)[1] * half + start, 16), size)]

    def hand(source, target):
        return wires.start(source, source, member(target)[0])

    pairs[pl.ds(pl.multiple_of(me * half, half), half), :] = pair_sum[...].astype(BF16)
    far = {mask: hand(slot(0), mask) for mask in (turn, 2)}
    close = {0: hand(slot(0), 1)}

    second_wires[1].wait_recv()
    turn_wire.wait_recv()

    def first_norm(r):
        grad = row_sum[1, r, :] + second_got[1, r, :].astype(F32) + turn_last[r, :].astype(F32)
        result, by_gain, by_shift = norm_backward(tokens[r, :].astype(F32), grad, gain[0:1, :])
        d_tokens[r, :] = result + d_middle[r, :]
        vec[0:1, :] += by_gain
        vec[1:2, :] += by_shift

    by_rows(rows, 64, first_norm)
    vec_wires = []
    opposite = 2 ^ turn

    def vec_send(devices):
        for device in devices:
            i = len(vec_wires)
            vec_give[i] = vec[...]
            vec_wires.append(wires.start(vec_give.at[i], vec_got.at[i], device))

    def vec_add(count):
        for i in range(len(vec_wires) - count, len(vec_wires)):
            vec_wires[i].wait_recv()
            vec[...] += vec_got[i]

    vec_send([member(1)[0]])

    far[turn].wait_recv()
    far[opposite] = hand(slot(turn), 2)
    close[turn] = hand(slot(turn), 1)
    far[2].wait_recv()
    close[2] = hand(slot(2), 1)
    vec_add(1)
    vec_send([member(mask)[0] for mask in (2, turn, opposite)])

    joint_hop(len(hops))
    keep = pl.ds(pl.multiple_of(second * quarter, quarter), quarter)
    kept = pl.ds(pl.multiple_of(near * side, side), side)
    joint_all[keep, kept] = half_sum[...].astype(BF16)
    joint_mine = joint_all.at[keep, kept]
    back = wires.start(joint_mine, joint_mine, to_second)
    vec_add(3)
    vec_send([across])
    far[opposite].wait_recv()
    close[opposite] = hand(slot(opposite), 1)
    vec_add(1)
    if higher:
        vec_send(higher[:1])
    back.wait_recv()
    joint_side = joint_all.at[:, kept]
    back_near = wires.start(joint_side, joint_side, member(1)[0])
    if higher:
        vec_add(1)
    for device in higher[1:]:
        vec_send([device])
        vec_add(1)
    sums[...] = vec[...]
    for wire in close.values():
        wire.wait_recv()
    back_near.wait_recv()

    for wire in (
        [pair_wire, tail_near_wire, tail_wire, joint_wire, back, back_near]
        + list(near_wires.values()) + second_wires + [turn_wire] + pair_wires + list(far.values())
        + list(close.values()) + joint_wires + vec_wires
    ):
        wire.wait_send()


def finish(d_mixed, d_query_last, normed, weight, tokens, d_middle, gain, joint_keep, joint_other, vectors, residual, fed_other):
    rows, width = tokens.shape
    half = width // 2
    members = 2 * lax.axis_size("tensor")
    higher = lax.axis_size("context").bit_length() - 2
    side = joint_keep.shape[1]
    tall = vectors.shape[0]
    scratch = [
        pltpu.VMEM((4, rows, width), BF16),
        pltpu.VMEM((4, rows, width), BF16),
        pltpu.VMEM((2, rows, width), F32),
        pltpu.VMEM((2, rows, width), BF16),
        pltpu.VMEM((rows, width), BF16),
        pltpu.VMEM((rows, width), BF16),
        pltpu.VMEM((4 * PAIR, width), F32),
        pltpu.VMEM((width, 4 * PAIR), F32),
        pltpu.VMEM((half, 3 * PAIR), BF16),
        pltpu.VMEM((half, 3 * PAIR), BF16),
        pltpu.VMEM((max(higher, 1), half, 3 * PAIR), BF16),
        pltpu.VMEM((max(higher, 1), half, 3 * PAIR), BF16),
        pltpu.VMEM((width, 2 * PAIR), BF16),
        pltpu.VMEM((width, 2 * PAIR), BF16),
        pltpu.VMEM((width, 2 * PAIR), F32),
        pltpu.VMEM((half, 2 * PAIR), BF16),
        pltpu.VMEM((half, 2 * PAIR), BF16),
        pltpu.VMEM((half // 2, side), BF16),
        pltpu.VMEM((half // 2, side), BF16),
        pltpu.VMEM((higher + 1, half // 2, side), BF16),
        pltpu.VMEM((higher + 1, half // 2, side), BF16),
        pltpu.VMEM((half, 3 * PAIR), F32),
        pltpu.VMEM((half // 2, side), F32),
        pltpu.VMEM((tall, width), F32),
        pltpu.VMEM((higher + 5, tall, width), F32),
        pltpu.VMEM((higher + 5, tall, width), F32),
        pltpu.VMEM(d_mixed.shape, d_mixed.dtype),
        pltpu.VMEM(normed.shape, normed.dtype),
        pltpu.VMEM(weight.shape, weight.dtype),
        pltpu.VMEM(tokens.shape, tokens.dtype),
        pltpu.VMEM(d_middle.shape, d_middle.dtype),
        pltpu.VMEM(joint_keep.shape, joint_keep.dtype),
        pltpu.VMEM(joint_other.shape, joint_other.dtype),
        pltpu.VMEM(residual.shape, residual.dtype),
        pltpu.VMEM(fed_other.shape, fed_other.dtype),
        pltpu.SemaphoreType.DMA((9,)),
        pltpu.SemaphoreType.DMA((3 * members + 3 * higher + 20,)),
        pltpu.SemaphoreType.DMA((3 * members + 3 * higher + 20,)),
    ]
    return pl.pallas_call(
        finish_kernel,
        in_specs=[ANY, VMEM] + [ANY] * 4 + [VMEM] + [ANY] * 2 + [VMEM] + [ANY] * 2,
        out_specs=[VMEM] * 5,
        out_shape=[
            jax.ShapeDtypeStruct((rows, width), BF16),
            jax.ShapeDtypeStruct((rows, width), F32),
            jax.ShapeDtypeStruct((members * half, 3 * PAIR), BF16),
            jax.ShapeDtypeStruct((half, 2 * side), BF16),
            jax.ShapeDtypeStruct((tall, width), F32),
        ],
        scratch_shapes=scratch,
        compiler_params=pltpu.CompilerParams(
            collective_id=6, has_side_effects=True, vmem_limit_bytes=63 << 20
        ),
        name="finish",
    )(d_mixed, d_query_last, normed, weight, tokens, d_middle, gain, joint_keep, joint_other, vectors, residual, fed_other)


def write_kernel(pairs, joint, fc, own_mixer, own_out, own_fc):
    members = pairs.shape[0]
    width = own_out.shape[1]
    shared = width - HEAD_DIM
    lane = lax.broadcasted_iota(jnp.int32, (1, PAIR), 1) < HEAD_DIM

    def write(r):
        own_out[r, 0:shared] = joint[r, 0:shared].astype(F32)
        eighth = joint[r, shared : shared + PAIR].astype(F32)
        ninth = joint[r, shared + PAIR :].astype(F32)
        own_out[r, shared:] = ninth[:, :HEAD_DIM]
        own_fc[r, :] = fc[r, :].astype(F32)
        keys = []
        for k in range(members):
            value = pairs[k, r, :].astype(F32)
            own_mixer[r, k * PAIR : (k + 1) * PAIR] = value[:, 0:PAIR]
            own_mixer[r, 2 * width + k * PAIR : 2 * width + (k + 1) * PAIR] = value[:, 2 * PAIR :]
            keys.append(value[:, PAIR : 2 * PAIR])
        keys = jnp.concatenate(keys + [jnp.where(lane, eighth, ninth)], axis=1)
        own_mixer[r, shared : 2 * width] = pltpu.roll(keys, HEAD_DIM, 1)
        own_mixer[r, 2 * width + shared :] = pltpu.roll(eighth, HEAD_DIM, 1)[:, :HEAD_DIM]

    by_rows(fc.shape[0], 16, write)


def write_gradients(pairs, joint, fc):
    half, width = fc.shape
    members = pairs.shape[0] // half
    step = half // 2

    def block(*shape):
        return pl.BlockSpec(shape, lambda i: (0,) * (len(shape) - 2) + (i, 0))

    return pl.pallas_call(
        write_kernel,
        grid=(half // step,),
        in_specs=[block(members, step, 3 * PAIR), block(step, joint.shape[1]), block(step, width)],
        out_specs=[block(step, 3 * width), block(step, width), block(step, width)],
        out_shape=[
            jax.ShapeDtypeStruct((half, 3 * width), F32),
            jax.ShapeDtypeStruct((half, width), F32),
            jax.ShapeDtypeStruct((half, width), F32),
        ],
        compiler_params=pltpu.CompilerParams(vmem_limit_bytes=40 << 20),
        name="write_gradients",
    )(pairs.reshape(members, half, 3 * PAIR), joint, fc)


def tri(n):
    r=lax.broadcasted_iota(jnp.int32,(n,n),0); c=lax.broadcasted_iota(jnp.int32,(n,n),1)
    return c<=r

def branch_mask():
    r=lax.broadcasted_iota(jnp.int32,(BRANCH,BRANCH),0); c=lax.broadcasted_iota(jnp.int32,(BRANCH,BRANCH),1)
    return (c<=r)&((c<PIECE)|(c//PIECE==r//PIECE))

def split_heads(x):
    lane=lax.broadcasted_iota(jnp.int32,(1,2*64),1)<64
    z=jnp.zeros_like(x)
    return jnp.concatenate([jnp.where(lane,x,z),jnp.where(lane,z,x)],axis=0)

def join_heads(x):
    n=x.shape[0]//2
    lane=lax.broadcasted_iota(jnp.int32,(1,2*64),1)<64
    return jnp.where(lane,x[:n],x[n:])

def fwd_kernel(order, qkv, q16, qinfo, kinfo, att, att16, canon, of, lse, of16, lse16):
    n_p=qkv.shape[0]//PIECE
    for i in range(n_p):
        src=pl.ds(pl.multiple_of(order[i]*PIECE,PIECE),PIECE)
        canon[i*PIECE:(i+1)*PIECE,:]=qkv[src,0:384]
    def rows(start,size,parts):
        qh=split_heads(canon[pl.ds(start,size),0:128])
        ss=[]
        for ks,kn,mask in parts:
            s=contract(qh,canon[pl.ds(ks,kn),128:256],1,1)
            if mask is not None:
                m2=jnp.concatenate([mask,mask],axis=0)
                s=jnp.where(m2,s,NEGATIVE)
            ss.append(s)
        top=functools.reduce(jnp.maximum,[jnp.max(s,axis=1,keepdims=True) for s in ss])
        tot=0.; o=0.
        for (ks,kn,_),s in zip(parts,ss):
            e=jnp.exp(s-top)
            tot=tot+jnp.sum(e,axis=1,keepdims=True)
            o=o+contract(e.astype(BF16),canon[pl.ds(ks,kn),256:384],1,0)
        o=join_heads(o*(1.0/tot))
        of[pl.ds(start,size),:]=o
        l=top+jnp.log(tot)
        lse[pl.ds(start,size),:]=join_heads(jnp.broadcast_to(l,(2*size,128)))
    t=tri(256)
    for b in range(4):
        parts=[(b*256,256,t)]
        if b: parts.insert(0,(0,b*256,None))
        rows(b*256,256,parts)
    bm=branch_mask()
    def branch(b,_):
        st=pl.multiple_of(TRUNK+b*BRANCH,PIECE)
        rows(st,BRANCH,[(0,TRUNK,None),(st,BRANCH,bm)])
        return 0
    lax.fori_loop(0,4,branch,0)
    for i in range(n_p):
        dst=pl.ds(pl.multiple_of(order[i]*PIECE,PIECE),PIECE)
        att[dst,:]=of[i*PIECE:(i+1)*PIECE,:].astype(BF16)
    s=contract(q16[...],qkv[:,384:512],1,1)
    s=jnp.where(allowed_mask(qinfo,kinfo),s,NEGATIVE)
    top=jnp.max(s,axis=1,keepdims=True)
    e=jnp.exp(s-top)
    tot=jnp.sum(e,axis=1,keepdims=True)
    o=contract(e.astype(BF16),qkv[:,384:512],1,0)*(1.0/tot)
    of16[...]=o
    att16[...]=pltpu.roll(o,64,1).astype(BF16)
    lse16[...]=jnp.broadcast_to(top+jnp.log(tot),o.shape)

def allowed_mask(qinfo,kinfo):
    ks=kinfo[0:1,:]; kp=kinfo[1:2,:]
    return ((ks==qinfo[:,0:1])|(ks==qinfo[:,1:2])|(ks==qinfo[:,2:3]))&(kp<=qinfo[:,3:4])

def attention_forward(order,qkv,q16,qinfo,kinfo):
    n=qkv.shape[0]; r=q16.shape[0]
    sd=jax.ShapeDtypeStruct
    V=pl.BlockSpec(memory_space=pltpu.VMEM)
    return pl.pallas_call(fwd_kernel,
        in_specs=[pl.BlockSpec(memory_space=pltpu.SMEM)]+[V]*4,
        out_specs=[V]*7,
        out_shape=[sd((n,128),BF16),sd((r,128),BF16),sd((n,384),BF16),sd((n,128),F32),sd((n,128),F32),sd((r,128),F32),sd((r,128),F32)],
        compiler_params=pltpu.CompilerParams(vmem_limit_bytes=60<<20),
        cost_estimate=pl.CostEstimate(flops=20_000_000_000,bytes_accessed=8_000_000,transcendentals=7_000_000),
        name="tree_attention_forward",
    )(order,qkv,q16,qinfo,kinfo)

def bwd_kernel(order, canon, of, lse, datt, kv16, q16, of16, lse16, datt16, qinfo, kinfo, dqkv, dq16, dc, dacc):
    n_p=canon.shape[0]//PIECE
    for i in range(n_p):
        src=pl.ds(pl.multiple_of(order[i]*PIECE,PIECE),PIECE)
        dc[i*PIECE:(i+1)*PIECE,:]=datt[src,:]
    def rows(start,size,parts):
        r=pl.ds(start,size)
        qh=split_heads(canon[r,0:128])
        d=dc[r,:]
        dh=split_heads(d)
        prod=d.astype(F32)*of[r,:]
        delta=jnp.concatenate([jnp.sum(prod[:,0:64],axis=1,keepdims=True),jnp.sum(prod[:,64:128],axis=1,keepdims=True)],axis=0)
        l=jnp.concatenate([lse[r,0:1],lse[r,64:65]],axis=0)
        dq=0.
        for ks,kn,mask,first in parts:
            kk=canon[pl.ds(ks,kn),128:256]
            s=contract(qh,kk,1,1)
            if mask is not None:
                s=jnp.where(jnp.concatenate([mask,mask],axis=0),s,NEGATIVE)
            p=jnp.exp(s-l)
            dp=contract(dh,canon[pl.ds(ks,kn),256:384],1,1)
            ds=(p*(dp-delta)).astype(BF16)
            dv=contract(p.astype(BF16),dh,0,0)
            dk=contract(ds,qh,0,0)
            dq=dq+contract(ds,kk,1,0)
            if first:
                dacc[pl.ds(ks,kn),128:256]=dk
                dacc[pl.ds(ks,kn),256:384]=dv
            else:
                dacc[pl.ds(ks,kn),128:256]+=dk
                dacc[pl.ds(ks,kn),256:384]+=dv
        dacc[r,0:128]=join_heads(dq)
    t=tri(256)
    for b in range(4):
        parts=[(b*256,256,t,True)]
        if b: parts.insert(0,(0,b*256,None,False))
        rows(b*256,256,parts)
    bm=branch_mask()
    def branch(b,_):
        st=pl.multiple_of(TRUNK+b*BRANCH,PIECE)
        rows(st,BRANCH,[(0,TRUNK,None,False),(st,BRANCH,bm,True)])
        return 0
    lax.fori_loop(0,4,branch,0)
    for i in range(n_p):
        dst=pl.ds(pl.multiple_of(order[i]*PIECE,PIECE),PIECE)
        x=dacc[i*PIECE:(i+1)*PIECE,:]
        dqkv[dst,0:128]=(x[:,0:128]*0.125).astype(BF16)
        dqkv[dst,128:384]=x[:,128:384].astype(BF16)
    k16=kv16[:,384:512]
    s=contract(q16[...],k16,1,1)
    s=jnp.where(allowed_mask(qinfo,kinfo),s,NEGATIVE)
    p=jnp.exp(s-lse16[:,0:1])
    dp=contract(datt16[...],k16,1,1)
    delta=jnp.sum(datt16[...].astype(F32)*of16[...],axis=1,keepdims=True)
    ds=(p*(dp-delta)).astype(BF16)
    dqkv[:,384:512]=(contract(ds,q16[...],0,0)+contract(p.astype(BF16),datt16[...],0,0)).astype(BF16)
    lane=lax.broadcasted_iota(jnp.int32,(1,128),1)>=64
    dq=pltpu.roll(contract(ds,k16,1,0)*0.125,64,1)
    dq16[...]=jnp.where(lane,dq,0.0).astype(BF16)

def attention_backward(order,canon,of,lse,datt,qkv,q16,of16,lse16,datt16,qinfo,kinfo):
    n=canon.shape[0]; r=q16.shape[0]
    sd=jax.ShapeDtypeStruct
    V=pl.BlockSpec(memory_space=pltpu.VMEM)
    return pl.pallas_call(bwd_kernel,
        in_specs=[pl.BlockSpec(memory_space=pltpu.SMEM)]+[V]*11,
        out_specs=[V]*2,
        out_shape=[sd((n,512),BF16),sd((r,128),BF16)],
        scratch_shapes=[pltpu.VMEM((n,128),BF16),pltpu.VMEM((n,384),F32)],
        compiler_params=pltpu.CompilerParams(vmem_limit_bytes=60<<20),
        cost_estimate=pl.CostEstimate(flops=50_000_000_000,bytes_accessed=15_000_000,transcendentals=7_000_000),
        name="tree_attention_backward",
    )(order,canon,of,lse,datt,qkv,q16,of16,lse16,datt16,qinfo,kinfo)


def parent_lookup(identities, shifted_table):
    labels = jnp.arange(shifted_table.shape[0], dtype=jnp.int32)
    matches = identities[:, None] == labels[None, :]
    return jnp.sum(jnp.where(matches, shifted_table[None, :], 0), axis=1) - 1


def tree_order(segments, places, parent):
    own = segments.reshape(-1, PIECE)[:, 0]
    start = places.reshape(-1, PIECE)[:, 0]
    table = parent + 1
    first_up = parent_lookup(own, table)
    second_up = parent_lookup(first_up, table)
    is_branch = (first_up >= 0) & (second_up < 0)
    is_leaf = second_up >= 0
    branch = jnp.where(is_leaf, first_up, own)
    rank = jnp.sum((is_branch[None, :] & (own[None, :] < branch[:, None])).astype(jnp.int32), axis=1)
    twin = is_leaf[None, :] & (first_up[None, :] == first_up[:, None]) & (own[None, :] < own[:, None])
    leaf = 1 + jnp.sum(twin.astype(jnp.int32), axis=1)
    target = jnp.where(
        first_up < 0, start // PIECE, TRUNK // PIECE + 3 * rank + jnp.where(is_leaf, leaf, 0)
    )
    pieces = jnp.arange(own.shape[0], dtype=jnp.int32)
    order = jnp.sum(jnp.where(target[None, :] == pieces[:, None], pieces[None, :], 0), axis=1)
    return order, first_up, second_up


def local(
    tokens,
    cotangent,
    segment_of,
    position_of,
    parent,
    ln1_gain,
    ln1_bias,
    w_qkv,
    b_query,
    b_value,
    w_out,
    b_out,
    ln2_gain,
    ln2_bias,
    w_fc,
    b_fc,
    w_proj,
    b_proj,
):
    rows = tokens.shape[0]
    half = w_qkv.shape[0]
    shard = lax.axis_index("shard")
    tensor, context, me = place()
    members = 2 * lax.axis_size("tensor")
    tree_rows = members * rows
    low = shard == 0

    held = (ln1_gain, ln1_bias, b_query, b_value, b_out, ln2_gain, ln2_bias, b_proj)
    spare = -half % PIECE
    flat = jnp.concatenate([part for value in held for part in (value, jnp.zeros((spare,), BF16))])
    vectors = flat.reshape(len(held), half + spare)[:, :half].astype(F32)
    zeros = jnp.zeros_like(vectors)
    half_vectors = jnp.concatenate(
        [jnp.where(low, vectors, zeros), jnp.where(low, zeros, vectors)], axis=1
    )
    proj_mine = w_proj.T
    normed_all, mixed, query_last, vectors, weight, fc_other = project(tokens, w_qkv, half_vectors, w_fc)
    proj_give, cotangent_give, mixed = lax.optimization_barrier((proj_mine, cotangent, mixed))
    proj_other = swap(proj_give, "shard", 0)
    cotangent_far = swap(cotangent_give, "tensor", 1)

    tree_start = lax.div(context, 2) * tree_rows
    segments = lax.dynamic_slice_in_dim(segment_of, tree_start, tree_rows)
    places = lax.dynamic_slice_in_dim(position_of, tree_start, tree_rows)
    order, first_up, second_up = tree_order(segments, places, parent)
    key_info = jnp.stack([segments, places])
    query_info = jnp.stack(
        [segments, jnp.repeat(first_up, PIECE), jnp.repeat(second_up, PIECE), places], axis=1
    )
    query_info = lax.dynamic_slice_in_dim(query_info, me * rows, rows, 0)

    attended_pair, attended_last, sorted_qkv, exact, level, exact_last, level_last = attention_forward(
        order, mixed, query_last, query_info, key_info
    )
    residual, fed_give, d_middle, d_pair, d_last, joint_keep, joint_give, fc_keep, fc_give, proj_sum, sums = feed_forward(
        attended_pair,
        attended_last,
        tokens,
        cotangent,
        cotangent_far,
        w_out,
        w_fc,
        fc_other,
        proj_mine,
        proj_other,
        vectors,
        b_fc.astype(F32)[None, :],
    )

    fc_got = swap(fc_give, "shard", 0)
    joint_other = swap(joint_give, "tensor", 1)
    fed_other = swap(fed_give, "tensor", 1)
    proj_sum = lax.psum(proj_sum, "context")

    d_mixed, d_query_last = attention_backward(
        order, sorted_qkv, exact, level, d_pair, mixed, query_last, exact_last, level_last, d_last,
        query_info, key_info,
    )
    fc_got, joint_other, fed_other, d_mixed = lax.optimization_barrier(
        (fc_got, joint_other, fed_other, d_mixed)
    )
    fc_sum = (fc_keep.astype(F32) + fc_got.astype(F32)).astype(BF16)
    fc_sum = lax.psum(
        fc_sum, "context", axis_index_groups=[list(range(lax.axis_size("context")))[::-1]]
    )
    output, d_inputs, pairs, joint_all, sums = finish(
        d_mixed,
        d_query_last,
        normed_all,
        weight,
        tokens,
        d_middle,
        vectors,
        joint_keep,
        joint_other,
        sums,
        residual,
        fed_other,
    )
    proj_sum, fc_sum, sums = lax.optimization_barrier((proj_sum, fc_sum, sums))
    own_mixer, own_out, own_fc = write_gradients(pairs, joint_all, fc_sum)
    own_proj = proj_sum.T.astype(F32)
    mine = lax.dynamic_slice_in_dim(sums[:8], shard * half, half, 1)
    own_bias_fc = lax.dynamic_slice_in_dim(sums, 8 + tensor, 1, 0)[0]
    return (
        output,
        d_inputs,
        mine[0],
        mine[1],
        own_mixer,
        mine[2],
        mine[3],
        own_out,
        mine[4],
        mine[5],
        mine[6],
        own_fc,
        own_bias_fc,
        own_proj,
        mine[7],
    )


def solution(mesh):
    return jax.shard_map(
        local,
        mesh=mesh,
        in_specs=(
            P(("shard", "context", "tensor"), None),
            P(("shard", "context", "tensor"), None),
            P("shard"),
            P("shard"),
            P(),
            P("shard"),
            P("shard"),
            P("shard", None),
            P("shard"),
            P("shard"),
            P("shard", None),
            P("shard"),
            P("shard"),
            P("shard"),
            P("shard", "tensor"),
            P("tensor"),
            P("tensor", "shard"),
            P("shard"),
        ),
        out_specs=(
            P(("shard", "context", "tensor"), None),
            P(("shard", "context", "tensor"), None),
            P("shard"),
            P("shard"),
            P("shard", None),
            P("shard"),
            P("shard"),
            P("shard", None),
            P("shard"),
            P("shard"),
            P("shard"),
            P("shard", "tensor"),
            P("tensor"),
            P("tensor", "shard"),
            P("shard"),
        ),
        check_vma=False,
    )
```

```python
import functools

import jax
import jax.numpy as jnp
from jax import lax
from jax.experimental import pallas as pl
from jax.experimental.pallas import tpu as pltpu
from jax.sharding import PartitionSpec as P

HEAD_DIM = 64
PAIR = 2 * HEAD_DIM
PIECE = 128
TRUNK = 8 * PIECE
BRANCH = 3 * PIECE
EPSILON = 1e-05
NEGATIVE = -1e30
F32 = jnp.float32
BF16 = jnp.bfloat16
VMEM = pl.BlockSpec(memory_space=pltpu.VMEM)
SMEM = pl.BlockSpec(memory_space=pltpu.SMEM)
ANY = pl.BlockSpec(memory_space=pl.ANY)
MESH = pl.DeviceIdType.MESH


def contract(left, right, left_dim, right_dim):
    return lax.dot_general(
        left, right, (((left_dim,), (right_dim,)), ((), ())), preferred_element_type=F32
    )


def flip(value, bit):
    low = 1 << bit
    return value + low - 2 * low * lax.rem(lax.div(value, low), 2)


def place():
    tensor, context = lax.axis_index("tensor"), lax.axis_index("context")
    return tensor, context, lax.rem(context, 2) * lax.axis_size("tensor") + tensor


def member(mask):
    tensor, context, _ = place()
    size = lax.axis_size("tensor")
    bits = size.bit_length() - 1
    for bit in range(bits):
        if mask >> bit & 1:
            tensor = flip(tensor, bit)
    if mask >> bits & 1:
        context = flip(context, 0)
    return {"context": context, "tensor": tensor}, lax.rem(context, 2) * size + tensor


def swap(value, axis, bit):
    size = lax.axis_size(axis)
    return lax.ppermute(value, axis, [(i, i ^ 1 << bit) for i in range(size)])


class Wires:
    def __init__(self, send, recv):
        self.send, self.recv, self.used = send, recv, 0

    def start(self, source, target, device):
        assert self.used < self.send.shape[0]
        copy = pltpu.make_async_remote_copy(
            src_ref=source,
            dst_ref=target,
            send_sem=self.send.at[self.used],
            recv_sem=self.recv.at[self.used],
            device_id=device,
            device_id_type=MESH,
        )
        self.used += 1
        copy.start()
        return copy


def by_rows(rows, step, body, first=0):
    def run(i, carry):
        body(pl.ds(pl.multiple_of(first + i * step, step), step))
        return carry

    lax.fori_loop(0, rows // step, run, 0)


def norm_backward(values, grad, gain):
    average = jnp.mean(values, axis=1, keepdims=True)
    centered = values - average
    inverse = lax.rsqrt(jnp.mean(centered * centered, axis=1, keepdims=True) + EPSILON)
    normal = centered * inverse
    scaled = grad * gain
    result = inverse * (
        scaled
        - jnp.mean(scaled, axis=1, keepdims=True)
        - normal * jnp.mean(scaled * normal, axis=1, keepdims=True)
    )
    return result, jnp.sum(grad * normal, axis=0, keepdims=True), jnp.sum(grad, axis=0, keepdims=True)


def norm_forward(values, gain, shift):
    average = jnp.mean(values, axis=1, keepdims=True)
    centered = values - average
    spread = jnp.mean(centered * centered, axis=1, keepdims=True)
    return centered * lax.rsqrt(spread + EPSILON) * gain + shift


def project_kernel(
    tokens, w_all, half_vectors, w_fc, normed_out, mixed_out, query_last, vectors, weight, fc_other, normed, mixed, everyone, w_qkv, seen, local_sem, out_sem, send, recv
):
    tensor, context, me = place()
    shard = lax.axis_index("shard")
    members = 2 * lax.axis_size("tensor")
    rows, width = tokens.shape
    half = width // 2
    cut = rows // 2
    shared = width - HEAD_DIM
    across = {"shard": 1 - shard}
    wires = Wires(send, recv)
    turn = members // 2

    load = pltpu.make_async_copy(w_all, w_qkv, local_sem.at[1])
    load.start()
    barrier = pltpu.get_barrier_semaphore()
    peers = [member(mask)[0] for mask in (1, 2, turn)] + [across]
    rest = [m for m in range(4, members) if m & 1 == 0 and m not in (turn, turn + 2)]
    for peer in peers:
        pl.semaphore_signal(barrier, inc=1, device_id=peer, device_id_type=MESH)
    pl.semaphore_wait(barrier, len(peers))
    assert not rest

    def slot(owner, first=0, size=rows):
        index = member(owner)[1] * rows + first
        return everyone.at[pl.ds(pl.multiple_of(index, 16), size)]

    def hand(source, target):
        return wires.start(source, source, member(target)[0])

    own = pltpu.make_async_copy(tokens, slot(0), local_sem.at[0])
    own.start()
    far = {m: wires.start(tokens, slot(0), member(m)[0]) for m in (2, turn)}
    vector_wire = wires.start(half_vectors, seen, across)
    close = {0: wires.start(tokens, slot(0), member(1)[0])}
    lane = lax.broadcasted_iota(jnp.int32, (1, PAIR), 1) < HEAD_DIM

    def choose(i, carry):
        r = pl.ds(pl.multiple_of(i * 32, 32), 32)
        to = pl.ds(pl.multiple_of(shard * half + i * 32, 32), 32)

        def window(start, size=PAIR):
            return w_qkv[r, pl.ds(pl.multiple_of(start, PAIR), size)]

        def turned(value):
            return pltpu.roll(value.astype(F32), HEAD_DIM, 1)

        weight[to, 0:PAIR] = window(me * PAIR)
        left, right = window(shared + me * PAIR), window(shared + (me + 1) * PAIR)
        weight[to, PAIR : 2 * PAIR] = jnp.where(lane, turned(left), turned(right)).astype(BF16)
        weight[to, 2 * PAIR : 3 * PAIR] = window(2 * width + me * PAIR)
        value = w_qkv[r, 2 * width + shared :]
        value = jnp.concatenate([value, value], axis=1)
        key = turned(w_qkv[r, 2 * width - PAIR : 2 * width])
        weight[to, 3 * PAIR : 4 * PAIR] = jnp.where(lane, key, value.astype(F32)).astype(BF16)
        query = w_qkv[r, shared : shared + PAIR]
        weight[to, 4 * PAIR :] = jnp.where(lane, query, jnp.zeros_like(query))
        return carry

    load.wait()
    lax.fori_loop(0, half // 32, choose, 0)
    chosen = weight.at[pl.ds(pl.multiple_of(shard * half, half), half)]
    weight_wire = wires.start(chosen, chosen, across)
    fc_wire = wires.start(w_fc.at[0 : half // 2], fc_other, across)

    vector_wire.wait_recv()
    vectors[...] = half_vectors[...] + seen[...]
    gain, shift = vectors[0:1, :], vectors[1:2, :]
    scale = HEAD_DIM ** (-0.5)
    pair_lanes = pl.ds(pl.multiple_of(me * PAIR, PAIR), PAIR)
    bias_query, bias_value = vectors[2:3, pair_lanes], vectors[3:4, pair_lanes]
    value_tail = vectors[3:4, shared:]
    bias_last = jnp.where(lane, 0.0, jnp.concatenate([value_tail, value_tail], axis=1))
    query_tail = vectors[2:3, shared:]
    query_tail = jnp.where(lane, jnp.concatenate([query_tail, query_tail], axis=1), 0.0)

    stored = []

    def put(source, target, owner, first):
        r = pl.ds(pl.multiple_of(member(owner)[1] * rows, rows), rows)
        stored.append(pltpu.make_async_copy(source.at[r], target.at[r], out_sem.at[first + owner]))
        stored[-1].start()

    def normalise(owner, first=0, size=rows):
        index = member(owner)[1] * rows + first

        def run(i, carry):
            r = pl.ds(pl.multiple_of(index + i * 32, 32), 32)
            normed[r, :] = norm_forward(everyone[r, :].astype(F32), gain, shift).astype(BF16)
            return carry

        lax.fori_loop(0, size // 32, run, 0)
        put(normed, normed_out, owner, 0)

    def multiply(owner, first=0, size=rows):
        r = pl.ds(pl.multiple_of(member(owner)[1] * rows + first, 32), size)
        result = jnp.dot(normed[r, :], weight[:, 0 : 4 * PAIR], preferred_element_type=F32)
        mixed[r, 0:PAIR] = ((result[:, 0:PAIR] + bias_query) * scale).astype(BF16)
        mixed[r, PAIR : 2 * PAIR] = result[:, PAIR : 2 * PAIR].astype(BF16)
        mixed[r, 2 * PAIR : 3 * PAIR] = (result[:, 2 * PAIR : 3 * PAIR] + bias_value).astype(BF16)
        mixed[r, 3 * PAIR :] = (result[:, 3 * PAIR :] + bias_last).astype(BF16)
        put(mixed, mixed_out, owner, members)

    own.wait()
    normalise(0)
    close[0].wait_recv()
    normalise(1)
    pieces = {}
    for m, other, first in ((2, turn, 0), (turn, 2, cut)):
        far[m].wait_recv()
        close[m] = hand(slot(m), 1)
        pieces[other] = hand(slot(m, first, cut), other)
    weight_wire.wait_recv()
    multiply(0)
    last = jnp.dot(
        normed[pl.ds(pl.multiple_of(me * rows, 32), rows), :], weight[:, 4 * PAIR :], preferred_element_type=F32
    )
    query_last[...] = ((last + query_tail) * scale).astype(BF16)
    multiply(1)
    for m in (2, turn):
        normalise(m)
        multiply(m)
    for m in (2, turn):
        close[m].wait_recv()
        normalise(m ^ 1)
        multiply(m ^ 1)
    opposite = 2 ^ turn
    passed = []
    for m, first in ((turn, 0), (2, cut)):
        pieces[m].wait_recv()
        passed.append(hand(slot(opposite, first, cut), 1))
    normalise(opposite)
    multiply(opposite)
    for wire in passed:
        wire.wait_recv()
    normalise(opposite ^ 1)
    multiply(opposite ^ 1)
    fc_wire.wait_recv()
    for copy in stored:
        copy.wait()
    for wire in list(far.values()) + list(close.values()) + list(pieces.values()) + passed + [vector_wire, weight_wire, fc_wire]:
        wire.wait_send()


def project(tokens, w_qkv, half_vectors, w_fc):
    rows, width = tokens.shape
    tree = 2 * lax.axis_size("tensor") * rows
    shape = jax.ShapeDtypeStruct
    return pl.pallas_call(
        project_kernel,
        in_specs=[VMEM, ANY, VMEM, ANY],
        out_specs=[ANY] * 2 + [VMEM] * 3 + [ANY],
        out_shape=[
            shape((tree, width), BF16),
            shape((tree, 4 * PAIR), BF16),
            shape((rows, PAIR), BF16),
            shape(half_vectors.shape, F32),
            shape((width, 5 * PAIR), BF16),
            shape((w_fc.shape[0] // 2, w_fc.shape[1]), BF16),
        ],
        scratch_shapes=[
            pltpu.VMEM((tree, width), BF16),
            pltpu.VMEM((tree, 4 * PAIR), BF16),
            pltpu.VMEM((tree, width), BF16),
            pltpu.VMEM(w_qkv.shape, BF16),
            pltpu.VMEM(half_vectors.shape, F32),
            pltpu.SemaphoreType.DMA((2,)),
            pltpu.SemaphoreType.DMA((2 * (tree // rows),)),
            pltpu.SemaphoreType.DMA((16,)),
            pltpu.SemaphoreType.DMA((16,)),
        ],
        compiler_params=pltpu.CompilerParams(
            collective_id=0, has_side_effects=True, vmem_limit_bytes=60 << 20
        ),
        name="project",
    )(tokens, w_qkv, half_vectors, w_fc)


def feed_forward_kernel(
    pair,
    last,
    tokens_all,
    cotangent,
    cotangent_far,
    out_mine,
    fc_mine,
    fc_other,
    proj_mine,
    proj_other,
    vectors,
    bias_fc,
    residual,
    fed_give,
    d_middle_out,
    d_pair,
    d_last,
    joint_keep,
    joint_give,
    fc_keep_out,
    fc_give_out,
    proj_sum,
    sums,
    w_out,
    w_fc,
    w_proj,
    attended,
    middle,
    normed,
    hidden,
    d_before,
    d_hidden,
    part,
    near,
    passing,
    far,
    d_attn,
    d_attended,
    grads,
    proj_keep,
    proj_give,
    proj_got,
    joint,
    joint_near,
    tokens,
    d_middle,
    fc_keep,
    fc_give,
    local_sem,
    send,
    recv,
):
    tensor, context, me = place()
    shard = lax.axis_index("shard")
    near_bit = lax.rem(tensor, 2)
    members = 2 * lax.axis_size("tensor")
    rows, width = tokens.shape
    half = width // 2
    shared = width - HEAD_DIM
    group = range(1, members)
    wires = Wires(send, recv)
    bias_out, gain, shift, bias_proj = (vectors[i : i + 1, :] for i in (4, 5, 6, 7))
    across = {"shard": 1 - shard}

    barrier = pltpu.get_barrier_semaphore()
    peers = [member(mask)[0] for mask in group] + [across]
    for peer in peers:
        pl.semaphore_signal(barrier, inc=1, device_id=peer, device_id_type=MESH)
    pl.semaphore_wait(barrier, len(peers))

    def slab(ref, index, size):
        return ref.at[pl.ds(pl.multiple_of(index * size, size), size)]

    def beside(ref, index):
        return ref.at[:, pl.ds(pl.multiple_of(index * PAIR, PAIR), PAIR)]

    moved = []
    for mask in group:
        device, index = member(mask)
        moved.append(wires.start(slab(pair, index, rows), beside(attended, me), device))
    quarter = half // 2
    out_wire = wires.start(
        slab(out_mine, near_bit, quarter), slab(w_out, 2 * shard + near_bit, quarter), across
    )
    local = [
        pltpu.make_async_copy(source, target, local_sem.at[i])
        for i, (source, target) in enumerate(
            (
                (slab(pair, me, rows), beside(attended, me)),
                (out_mine, slab(w_out, shard, half)),
                (fc_mine, slab(w_fc, shard, half)),
                (fc_other, slab(w_fc, 2 * (1 - shard), quarter)),
                (proj_mine, slab(w_proj, shard, half)),
                (proj_other, slab(w_proj, 1 - shard, half)),
                (tokens_all, tokens),
                (cotangent, slab(grads, 0, rows)),
                (cotangent_far, slab(grads, 2, rows)),
            )
        )
    ]
    pulled_wires = [
        wires.start(source, slab(grads, index, rows), member(1)[0])
        for index, source in ((1, cotangent), (3, cotangent_far))
    ]
    for copy in local:
        copy.start()
    attended[:, shared:] = last[:, 0:HEAD_DIM]
    out_wire.wait_recv()
    out_part = slab(w_out, 2 * (1 - shard) + near_bit, quarter)
    out_near = wires.start(out_part, out_part, member(1)[0])
    fc_wire = wires.start(
        fc_mine.at[quarter:half], slab(w_fc, 2 * shard + 1, quarter), across
    )
    for copy in local:
        copy.wait()
    for wire in moved + [out_near]:
        wire.wait_recv()

    start = 0
    while start < width:
        stop = min(start + 2 * PAIR, width)
        middle[:, start:stop] = (
            tokens[:, start:stop].astype(F32)
            + jnp.dot(attended[...], w_out[:, start:stop], preferred_element_type=F32)
            + bias_out[:, start:stop]
        )
        start = stop

    def second_norm(r):
        normed[r, :] = norm_forward(middle[r, :], gain, shift).astype(BF16)

    cut = rows // 2

    def piece(mask, i):
        return slice(mask * rows + i * cut, mask * rows + (i + 1) * cut)

    cross = []
    for i in range(2):
        by_rows(cut, 32, second_norm, i * cut)
        cross.append(wires.start(normed.at[piece(0, i)], normed.at[piece(2, i)], member(2)[0]))

    def block(ref, mask):
        return ref.at[mask * rows : (mask + 1) * rows, :]

    close = wires.start(block(normed, 0), block(normed, 1), member(1)[0])
    for wire in pulled_wires:
        wire.wait_recv()
    for mask in range(4):
        block(d_hidden, mask)[...] = jnp.dot(
            block(grads, mask)[...], w_proj[...], preferred_element_type=F32
        )

    def feed(r):
        start = 0
        while start < width:
            stop = min(start + 2 * PAIR, width)
            c = slice(start, stop)
            before = jnp.dot(normed[r, :], w_fc[:, c], preferred_element_type=F32) + bias_fc[0:1, c]
            cumulative = 0.5 + 0.5 * lax.erf(before * (0.5**0.5))
            hidden[r, c] = (before * cumulative).astype(BF16)
            slope = cumulative + before * jnp.exp(-0.5 * before * before) * ((2 * jnp.pi) ** -0.5)
            d_before[r, c] = (d_hidden[r, c] * slope).astype(BF16)
            start = stop

    def back(r):
        return contract(d_before[r, :], w_fc[...], 1, 1)

    def ahead(mask):
        return contract(hidden[mask * rows : (mask + 1) * rows, :], w_proj[...], 1, 1)

    fc_wire.wait_recv()
    feed(slice(0, rows))
    close.wait_recv()
    feed(slice(rows, 2 * rows))
    part[0] = back(slice(rows, 2 * rows)).astype(BF16)
    to_near = wires.start(part.at[0], near.at[0], member(1)[0])
    relay, to_pass, to_far = [], [], []
    for i in range(2):
        h = slice(i * cut, (i + 1) * cut)
        cross[i].wait_recv()
        relay.append(wires.start(normed.at[piece(2, i)], normed.at[piece(3, i)], member(1)[0]))
        feed(piece(2, i))
        relay[i].wait_recv()
        feed(piece(3, i))
        part[1, h] = back(piece(3, i)).astype(BF16)
        to_pass.append(wires.start(part.at[1, h], near.at[1, h], member(1)[0]))
        mine = back(piece(2, i))
        to_pass[i].wait_recv()
        passing[h] = (mine + near[1, h].astype(F32)).astype(BF16)
        to_far.append(wires.start(passing.at[h], far.at[h], member(2)[0]))

    other_part = pl.ds(pl.multiple_of(2 * rows + (1 - shard) * half, 8), half)
    own_part = pl.ds(pl.multiple_of(2 * rows + shard * half, 8), half)
    proj_wires = []
    start = 0
    while start < width:
        stop = min(start + 2 * PAIR, width)
        c = slice(start, stop)
        d_hidden_part = d_hidden.at[2 * rows : 2 * rows + width, 0 : stop - start]
        d_hidden_part[...] = contract(grads[...], hidden[:, c], 0, 0)
        proj_give[:, c] = d_hidden[other_part, 0 : stop - start].astype(BF16)
        proj_wires.append(wires.start(proj_give.at[:, c], proj_got.at[:, c], across))
        proj_keep[:, c] = d_hidden[own_part, 0 : stop - start]
        start = stop
    start = 0
    while start < width:
        stop = min(start + 2 * PAIR, width)
        c = slice(start, stop)
        d_hidden_part = d_hidden.at[2 * rows : 2 * rows + width, 0 : stop - start]
        d_hidden_part[...] = contract(normed[...], d_before[:, c], 0, 0)
        fc_give[:, c] = d_hidden[other_part, 0 : stop - start].astype(BF16)
        fc_keep[:, c] = d_hidden[own_part, 0 : stop - start].astype(BF16)
        start = stop
    stored = []

    def put(source, target):
        stored.append(pltpu.make_async_copy(source, target, local_sem.at[9 + len(stored)]))
        stored[-1].start()

    put(fc_keep, fc_keep_out)
    put(fc_give, fc_give_out)
    d_hidden[0:rows, :] = back(slice(0, rows))
    to_near.wait_recv()
    for wire in to_far:
        wire.wait_recv()

    sums[...] = jnp.zeros_like(sums)

    def second_back(r):
        grad = d_hidden[r, :] + near[0, r, :].astype(F32) + far[r, :].astype(F32)
        result, by_gain, by_shift = norm_backward(middle[r, :], grad, gain)
        pulled = grads[r, :].astype(F32)
        result = result + pulled
        d_middle[r, :] = result
        low = result.astype(BF16)
        d_attn[r, 0:width] = low
        d_attn[r, width:] = jnp.zeros((r.size, d_attn.shape[1] - width), BF16)
        sums[4:5, :] += jnp.sum(low.astype(F32), axis=0, keepdims=True)
        sums[5:6, :] += by_gain
        sums[6:7, :] += by_shift
        sums[7:8, :] += jnp.sum(pulled, axis=0, keepdims=True)

    by_rows(rows, 64, second_back)
    put(d_middle, d_middle_out)
    start = 0
    while start < width:
        stop = min(start + 2 * PAIR, width)
        d_attended[:, start:stop] = contract(d_attn[:, 0:width], w_out[start:stop, :], 1, 1).astype(BF16)
        start = stop
    returned = []
    for mask in group:
        device, index = member(mask)
        returned.append(wires.start(beside(d_attended, index), slab(d_pair, me, rows), device))
    own_copy = pltpu.make_async_copy(beside(d_attended, me), slab(d_pair, me, rows), local_sem.at[0])
    own_copy.start()
    lane = lax.broadcasted_iota(jnp.int32, (1, PAIR), 1) >= HEAD_DIM
    tail = jnp.concatenate([d_attended[:, shared:]] * 2, axis=1)
    d_last[...] = jnp.where(lane, tail, jnp.zeros_like(tail))
    joint[:, shared : shared + PAIR] = jnp.zeros((width, PAIR), BF16)
    start = 0
    while start < d_attn.shape[1]:
        stop = min(start + 2 * PAIR, d_attn.shape[1])
        to = start if start < shared else start + PAIR
        joint[:, to : to + stop - start] = contract(attended[...], d_attn[:, start:stop], 0, 0).astype(BF16)
        start = stop
    side = joint.shape[1] // 2
    kept = pl.ds(pl.multiple_of(near_bit * side, side), side)
    given = pl.ds(pl.multiple_of((1 - near_bit) * side, side), side)
    joint_wire = wires.start(joint.at[:, given], joint_near, member(1)[0])
    part[2] = ahead(3).astype(BF16)
    to_pass_out = wires.start(part.at[2], near.at[3], member(1)[0])
    part[3] = ahead(1).astype(BF16)
    to_near_out = wires.start(part.at[3], near.at[2], member(1)[0])
    d_hidden[2 * rows : 3 * rows, :] = ahead(2)
    d_hidden[rows : 2 * rows, :] = ahead(0)
    bias = jnp.zeros((1, width), F32)

    def add_bias(i, total):
        r = pl.ds(pl.multiple_of(i * 64, 64), 64)
        return total + jnp.sum(d_before[r, :].astype(F32), axis=0, keepdims=True)

    bias = lax.fori_loop(0, 4 * rows // 64, add_bias, bias)
    for i in range(lax.axis_size("tensor")):
        sums[8 + i : 9 + i, :] = jnp.where(tensor == i, bias, 0.0)
    to_near_out.wait_recv()
    to_pass_out.wait_recv()

    def finish_output(r):
        third = pl.ds(pl.multiple_of(2 * rows + r.start, 64), r.size)
        again = pl.ds(pl.multiple_of(rows + r.start, 64), r.size)
        fed_give[r, :] = (d_hidden[third, :] + near[3, r, :].astype(F32)).astype(BF16)
        residual[r, :] = middle[r, :] + d_hidden[again, :] + near[2, r, :].astype(F32) + bias_proj

    by_rows(rows, 64, finish_output)
    joint_wire.wait_recv()
    second = lax.rem(lax.div(tensor, 2), 2)

    def add_joint(target, which):
        for i in range(2):

            def run(r):
                source = pl.ds(pl.multiple_of((2 * i + which) * quarter - i * quarter + r.start, 16), r.size)
                total = joint[source, kept].astype(F32) + joint_near[source, :].astype(F32)
                target[r, :] = total.astype(BF16)

            by_rows(quarter, 16, run, i * quarter)

    add_joint(joint_keep, second)
    add_joint(joint_give, 1 - second)
    for wire in proj_wires:
        wire.wait_recv()

    def add_proj(r):
        proj_sum[r, :] = (proj_keep[r, :] + proj_got[r, :].astype(F32)).astype(BF16)

    by_rows(half, 32, add_proj)
    own_copy.wait()
    for copy in stored:
        copy.wait()
    for wire in returned:
        wire.wait_recv()
    for wire in (
        moved + returned + [out_wire, out_near, fc_wire] + pulled_wires + proj_wires
        + cross + relay + to_pass + to_far + [joint_wire, close, to_near, to_near_out, to_pass_out]
    ):
        wire.wait_send()


def feed_forward(pair, last, tokens, cotangent, cotangent_far, out_mine, fc_mine, fc_other, proj_mine, proj_other, vectors, bias_fc):
    rows, width = tokens.shape
    members = 2 * lax.axis_size("tensor")
    hidden = fc_mine.shape[1]
    tall = 4 * rows
    shape = jax.ShapeDtypeStruct
    return pl.pallas_call(
        feed_forward_kernel,
        in_specs=[ANY, VMEM] + [ANY] * 8 + [VMEM] * 2,
        out_specs=[VMEM] * 2 + [ANY] * 2 + [VMEM] * 3 + [ANY] * 2 + [VMEM] * 2,
        out_shape=[
            shape((rows, width), F32),
            shape((rows, width), BF16),
            shape((rows, width), F32),
            shape((members * rows, PAIR), BF16),
            shape((rows, PAIR), BF16),
            shape((width // 2, 5 * PAIR), BF16),
            shape((width // 2, 5 * PAIR), BF16),
            shape((width // 2, hidden), BF16),
            shape((width // 2, hidden), BF16),
            shape((width // 2, hidden), BF16),
            shape((16, width), F32),
        ],
        scratch_shapes=[
            pltpu.VMEM((width, width), BF16),
            pltpu.VMEM((width, hidden), BF16),
            pltpu.VMEM((width, hidden), BF16),
            pltpu.VMEM((rows, width), BF16),
            pltpu.VMEM((rows, width), F32),
            pltpu.VMEM((tall, width), BF16),
            pltpu.VMEM((tall, hidden), BF16),
            pltpu.VMEM((tall, hidden), BF16),
            pltpu.VMEM((2 * rows + max(2 * rows, width), hidden), F32),
            pltpu.VMEM((4, rows, width), BF16),
            pltpu.VMEM((4, rows, width), BF16),
            pltpu.VMEM((rows, width), BF16),
            pltpu.VMEM((rows, width), BF16),
            pltpu.VMEM((rows, 9 * PAIR), BF16),
            pltpu.VMEM((rows, width), BF16),
            pltpu.VMEM((tall, width), BF16),
            pltpu.VMEM((width // 2, hidden), F32),
            pltpu.VMEM((width // 2, hidden), BF16),
            pltpu.VMEM((width // 2, hidden), BF16),
            pltpu.VMEM((width, 10 * PAIR), BF16),
            pltpu.VMEM((width, 5 * PAIR), BF16),
            pltpu.VMEM((rows, width), BF16),
            pltpu.VMEM((rows, width), F32),
            pltpu.VMEM((width // 2, hidden), BF16),
            pltpu.VMEM((width // 2, hidden), BF16),
            pltpu.SemaphoreType.DMA((12,)),
            pltpu.SemaphoreType.DMA((2 * members + 24,)),
            pltpu.SemaphoreType.DMA((2 * members + 24,)),
        ],
        compiler_params=pltpu.CompilerParams(
            collective_id=3, has_side_effects=True, vmem_limit_bytes=62 << 20
        ),
        name="feed_forward",
    )(pair, last, tokens, cotangent, cotangent_far, out_mine, fc_mine, fc_other, proj_mine, proj_other, vectors, bias_fc)


def finish_kernel(
    d_mixed_all,
    d_query_last,
    normed_all,
    weight_all,
    tokens_all,
    d_middle_all,
    gain,
    joint_keep_all,
    joint_other_all,
    vectors,
    residual_all,
    fed_other_all,
    output,
    d_tokens,
    pairs,
    joint_all,
    sums,
    near_give,
    near_got,
    row_sum,
    second_got,
    turn_last,
    last_low,
    pair_t,
    pair,
    pair_give,
    pair_got,
    pair_low,
    pair_seen,
    tail,
    tail_near,
    tail_sum,
    tail_give,
    tail_got,
    joint_give,
    joint_got,
    half_low,
    half_seen,
    pair_sum,
    half_sum,
    vec,
    vec_give,
    vec_got,
    d_mixed,
    normed,
    weight,
    tokens,
    d_middle,
    joint_keep,
    joint_other,
    residual,
    fed_other,
    load_sem,
    send,
    recv,
):
    tensor, context, me = place()
    shard = lax.axis_index("shard")
    near = lax.rem(tensor, 2)
    second = lax.rem(lax.div(tensor, 2), 2)
    contexts = lax.axis_size("context")
    members = 2 * lax.axis_size("tensor")
    turn = members // 2
    rows, width = tokens.shape
    half = width // 2
    quarter = half // 2
    side = joint_keep.shape[1]
    shared = width - HEAD_DIM
    block = 4 * PAIR
    across = {"shard": 1 - shard}
    higher = [
        {"context": flip(context, bit)} for bit in range(1, contexts.bit_length() - 1)
    ]
    group = range(1, members)
    wires = Wires(send, recv)

    loads = [
        pltpu.make_async_copy(source, target, load_sem.at[i])
        for i, (source, target) in enumerate(
            (
                (d_mixed_all, d_mixed),
                (normed_all, normed),
                (weight_all, weight),
                (tokens_all, tokens),
                (d_middle_all, d_middle),
                (joint_keep_all, joint_keep),
                (joint_other_all, joint_other),
                (residual_all, residual),
                (fed_other_all, fed_other),
            )
        )
    ]
    for copy in loads:
        copy.start()
    barrier = pltpu.get_barrier_semaphore()
    peers = [member(mask)[0] for mask in group] + [across] + higher
    for peer in peers:
        pl.semaphore_signal(barrier, inc=1, device_id=peer, device_id_type=MESH)
    pl.semaphore_wait(barrier, len(peers))
    for copy in loads:
        copy.wait()

    def part(ref, index, size):
        return ref.at[pl.ds(pl.multiple_of(index * size, size), size)]

    def term(mask):
        r = pl.ds(pl.multiple_of(member(mask)[1] * rows, rows), rows)
        return contract(d_mixed[r, :], weight[:, 0:block], 1, 1)

    steps = d_mixed.shape[0] // (2 * rows)
    pair_t[...] = jnp.zeros_like(pair_t)

    def accumulate(i, carry):
        r = pl.ds(pl.multiple_of(i * 2 * rows, 2 * rows), 2 * rows)
        pair_t[...] += contract(d_mixed[r, :], normed[r, :], 0, 0)
        return carry

    lax.fori_loop(0, steps, accumulate, 0)
    pair[...] = pair_t[...].T
    other = pl.ds(pl.multiple_of((1 - shard) * half, half), half)
    own = pl.ds(pl.multiple_of(shard * half, half), half)
    pair_give[...] = pair[other, 0 : 3 * PAIR].astype(BF16)
    pair_wire = wires.start(pair_give, pair_got, across)
    mine = pl.ds(pl.multiple_of(me * rows, rows), rows)
    tail[:, 0:PAIR] = pair[:, 3 * PAIR :].astype(BF16)
    tail[:, PAIR:] = contract(d_query_last[...], normed[mine, :], 0, 0).T.astype(BF16)
    tail_near_wire = wires.start(tail, tail_near, member(1)[0])

    order = [6, 2, 4, 0]
    near_wires = {}
    for i, mask in enumerate(order):
        near_give[i] = term(mask ^ 1).astype(BF16)
        near_wires[mask] = wires.start(near_give.at[i], near_got.at[i], member(1)[0])

    tail_near_wire.wait_recv()

    def add_tail_near(r):
        tail_sum[r, :] = tail[r, :].astype(F32) + tail_near[r, :].astype(F32)

    by_rows(width, 64, add_tail_near)
    to_second, to_turn = member(2)[0], member(turn)[0]
    for i in range(2):
        source = pl.ds(pl.multiple_of(i * half + (1 - second) * quarter, 16), quarter)
        tail_give[i * quarter : (i + 1) * quarter, :] = tail_sum[source, :].astype(BF16)
    tail_wire = wires.start(tail_give, tail_got, to_second)

    second_wires = []
    for i, mask in enumerate(order):
        total = term(mask)
        if mask == 0:
            query = pltpu.roll(d_query_last[...].astype(F32), HEAD_DIM, 1).astype(BF16)
            total = total + contract(query, weight[:, block:], 1, 1)
        near_wires[mask].wait_recv()
        total = total + near_got[i].astype(F32)
        if i >= 2:
            row_sum[i - 2] = total
        if mask & 2:
            near_got[i] = total.astype(BF16)
            second_wires.append(wires.start(near_got.at[i], second_got.at[i], to_second))

    pair_wire.wait_recv()
    pair_own = pair[own, 0 : 3 * PAIR] + pair_got[...].astype(F32)
    pair_wires = []
    for i, device in enumerate(higher):
        pair_low[i] = pair_own.astype(BF16)
        wire = wires.start(pair_low.at[i], pair_seen.at[i], device)
        pair_wires.append(wire)
        if i < len(higher) - 1:
            wire.wait_recv()
            pair_own = pair_own + pair_seen[i].astype(F32)
    pair_sum[...] = pair_own

    tail_wire.wait_recv()
    wide = joint_keep.shape[1] - 2 * PAIR

    def joint_term(which):
        r = pl.ds(pl.multiple_of(which * quarter, quarter), quarter)
        s = pl.ds(pl.multiple_of(which * half + second * quarter, quarter), quarter)
        total = joint_keep[r, :].astype(F32) + joint_other[r, :].astype(F32)
        last = jnp.where(near == 1, tail_sum[s, :] + tail_got[r, :].astype(F32), 0.0)
        return jnp.concatenate([total[:, :wide], total[:, wide:] + last], axis=1)

    joint_give[...] = joint_term(1 - shard).astype(BF16)
    joint_wire = wires.start(joint_give, joint_got, across)

    vec[...] = vectors[...]

    def add_columns(i, total):
        r = pl.ds(pl.multiple_of(i * 64, 64), 64)
        return total + jnp.sum(d_mixed[r, :].astype(F32), axis=0, keepdims=True)

    columns = lax.fori_loop(0, d_mixed.shape[0] // 64, add_columns, jnp.zeros((1, block), F32))
    pair_lanes = pl.ds(pl.multiple_of(me * PAIR, PAIR), PAIR)
    vec[2:3, pair_lanes] = columns[:, 0:PAIR]
    vec[3:4, pair_lanes] = columns[:, 2 * PAIR : 3 * PAIR]
    query = jnp.sum(d_query_last[...].astype(F32), axis=0, keepdims=True)
    vec[2:3, shared:] = pltpu.roll(query, HEAD_DIM, 1)[:, :HEAD_DIM]
    vec[3:4, shared:] = pltpu.roll(columns[:, 3 * PAIR :], HEAD_DIM, 1)[:, :HEAD_DIM]


    def add_fed(r):
        output[r, :] = (residual[r, :] + fed_other[r, :].astype(F32)).astype(BF16)

    by_rows(rows, 64, add_fed)

    joint_wire.wait_recv()
    half_sum[...] = joint_term(shard) + joint_got[...].astype(F32)
    hops = [to_turn] + higher
    joint_wires = []

    def joint_hop(i):
        if i:
            joint_wires[-1].wait_recv()
            half_sum[...] += half_seen[i - 1].astype(F32)
        if i < len(hops):
            half_low[i] = half_sum[...].astype(BF16)
            joint_wires.append(wires.start(half_low.at[i], half_seen.at[i], hops[i]))

    joint_hop(0)

    second_wires[0].wait_recv()
    last_low[...] = (row_sum[0] + second_got[0].astype(F32)).astype(BF16)
    turn_wire = wires.start(last_low, turn_last, to_turn)

    for i in range(1, len(hops)):
        joint_hop(i)

    if pair_wires:
        pair_wires[-1].wait_recv()
        pair_sum[...] += pair_seen[len(higher) - 1].astype(F32)

    def slot(owner, start=0, size=half):
        return pairs.at[pl.ds(pl.multiple_of(member(owner)[1] * half + start, 16), size)]

    def hand(source, target):
        return wires.start(source, source, member(target)[0])

    pairs[pl.ds(pl.multiple_of(me * half, half), half), :] = pair_sum[...].astype(BF16)
    far = {mask: hand(slot(0), mask) for mask in (turn, 2)}
    close = {0: hand(slot(0), 1)}

    second_wires[1].wait_recv()
    turn_wire.wait_recv()

    def first_norm(r):
        grad = row_sum[1, r, :] + second_got[1, r, :].astype(F32) + turn_last[r, :].astype(F32)
        result, by_gain, by_shift = norm_backward(tokens[r, :].astype(F32), grad, gain[0:1, :])
        d_tokens[r, :] = result + d_middle[r, :]
        vec[0:1, :] += by_gain
        vec[1:2, :] += by_shift

    by_rows(rows, 64, first_norm)
    vec_wires = []
    opposite = 2 ^ turn

    def vec_send(devices):
        for device in devices:
            i = len(vec_wires)
            vec_give[i] = vec[...]
            vec_wires.append(wires.start(vec_give.at[i], vec_got.at[i], device))

    def vec_add(count):
        for i in range(len(vec_wires) - count, len(vec_wires)):
            vec_wires[i].wait_recv()
            vec[...] += vec_got[i]

    vec_send([member(1)[0]])

    far[turn].wait_recv()
    far[opposite] = hand(slot(turn), 2)
    close[turn] = hand(slot(turn), 1)
    far[2].wait_recv()
    close[2] = hand(slot(2), 1)
    vec_add(1)
    vec_send([member(mask)[0] for mask in (2, turn, opposite)])

    joint_hop(len(hops))
    keep = pl.ds(pl.multiple_of(second * quarter, quarter), quarter)
    kept = pl.ds(pl.multiple_of(near * side, side), side)
    joint_all[keep, kept] = half_sum[...].astype(BF16)
    joint_mine = joint_all.at[keep, kept]
    back = wires.start(joint_mine, joint_mine, to_second)
    vec_add(3)
    vec_send([across])
    far[opposite].wait_recv()
    close[opposite] = hand(slot(opposite), 1)
    vec_add(1)
    if higher:
        vec_send(higher[:1])
    back.wait_recv()
    joint_side = joint_all.at[:, kept]
    back_near = wires.start(joint_side, joint_side, member(1)[0])
    if higher:
        vec_add(1)
    for device in higher[1:]:
        vec_send([device])
        vec_add(1)
    sums[...] = vec[...]
    for wire in close.values():
        wire.wait_recv()
    back_near.wait_recv()

    for wire in (
        [pair_wire, tail_near_wire, tail_wire, joint_wire, back, back_near]
        + list(near_wires.values()) + second_wires + [turn_wire] + pair_wires + list(far.values())
        + list(close.values()) + joint_wires + vec_wires
    ):
        wire.wait_send()


def finish(d_mixed, d_query_last, normed, weight, tokens, d_middle, gain, joint_keep, joint_other, vectors, residual, fed_other):
    rows, width = tokens.shape
    half = width // 2
    members = 2 * lax.axis_size("tensor")
    higher = lax.axis_size("context").bit_length() - 2
    side = joint_keep.shape[1]
    tall = vectors.shape[0]
    scratch = [
        pltpu.VMEM((4, rows, width), BF16),
        pltpu.VMEM((4, rows, width), BF16),
        pltpu.VMEM((2, rows, width), F32),
        pltpu.VMEM((2, rows, width), BF16),
        pltpu.VMEM((rows, width), BF16),
        pltpu.VMEM((rows, width), BF16),
        pltpu.VMEM((4 * PAIR, width), F32),
        pltpu.VMEM((width, 4 * PAIR), F32),
        pltpu.VMEM((half, 3 * PAIR), BF16),
        pltpu.VMEM((half, 3 * PAIR), BF16),
        pltpu.VMEM((max(higher, 1), half, 3 * PAIR), BF16),
        pltpu.VMEM((max(higher, 1), half, 3 * PAIR), BF16),
        pltpu.VMEM((width, 2 * PAIR), BF16),
        pltpu.VMEM((width, 2 * PAIR), BF16),
        pltpu.VMEM((width, 2 * PAIR), F32),
        pltpu.VMEM((half, 2 * PAIR), BF16),
        pltpu.VMEM((half, 2 * PAIR), BF16),
        pltpu.VMEM((half // 2, side), BF16),
        pltpu.VMEM((half // 2, side), BF16),
        pltpu.VMEM((higher + 1, half // 2, side), BF16),
        pltpu.VMEM((higher + 1, half // 2, side), BF16),
        pltpu.VMEM((half, 3 * PAIR), F32),
        pltpu.VMEM((half // 2, side), F32),
        pltpu.VMEM((tall, width), F32),
        pltpu.VMEM((higher + 5, tall, width), F32),
        pltpu.VMEM((higher + 5, tall, width), F32),
        pltpu.VMEM(d_mixed.shape, d_mixed.dtype),
        pltpu.VMEM(normed.shape, normed.dtype),
        pltpu.VMEM(weight.shape, weight.dtype),
        pltpu.VMEM(tokens.shape, tokens.dtype),
        pltpu.VMEM(d_middle.shape, d_middle.dtype),
        pltpu.VMEM(joint_keep.shape, joint_keep.dtype),
        pltpu.VMEM(joint_other.shape, joint_other.dtype),
        pltpu.VMEM(residual.shape, residual.dtype),
        pltpu.VMEM(fed_other.shape, fed_other.dtype),
        pltpu.SemaphoreType.DMA((9,)),
        pltpu.SemaphoreType.DMA((3 * members + 3 * higher + 20,)),
        pltpu.SemaphoreType.DMA((3 * members + 3 * higher + 20,)),
    ]
    return pl.pallas_call(
        finish_kernel,
        in_specs=[ANY, VMEM] + [ANY] * 4 + [VMEM] + [ANY] * 2 + [VMEM] + [ANY] * 2,
        out_specs=[VMEM] * 5,
        out_shape=[
            jax.ShapeDtypeStruct((rows, width), BF16),
            jax.ShapeDtypeStruct((rows, width), F32),
            jax.ShapeDtypeStruct((members * half, 3 * PAIR), BF16),
            jax.ShapeDtypeStruct((half, 2 * side), BF16),
            jax.ShapeDtypeStruct((tall, width), F32),
        ],
        scratch_shapes=scratch,
        compiler_params=pltpu.CompilerParams(
            collective_id=6, has_side_effects=True, vmem_limit_bytes=63 << 20
        ),
        name="finish",
    )(d_mixed, d_query_last, normed, weight, tokens, d_middle, gain, joint_keep, joint_other, vectors, residual, fed_other)


def write_kernel(pairs, joint, fc, own_mixer, own_out, own_fc):
    members = pairs.shape[0]
    width = own_out.shape[1]
    shared = width - HEAD_DIM
    lane = lax.broadcasted_iota(jnp.int32, (1, PAIR), 1) < HEAD_DIM

    def write(r):
        own_out[r, 0:shared] = joint[r, 0:shared].astype(F32)
        eighth = joint[r, shared : shared + PAIR].astype(F32)
        ninth = joint[r, shared + PAIR :].astype(F32)
        own_out[r, shared:] = ninth[:, :HEAD_DIM]
        own_fc[r, :] = fc[r, :].astype(F32)
        keys = []
        for k in range(members):
            value = pairs[k, r, :].astype(F32)
            own_mixer[r, k * PAIR : (k + 1) * PAIR] = value[:, 0:PAIR]
            own_mixer[r, 2 * width + k * PAIR : 2 * width + (k + 1) * PAIR] = value[:, 2 * PAIR :]
            keys.append(value[:, PAIR : 2 * PAIR])
        keys = jnp.concatenate(keys + [jnp.where(lane, eighth, ninth)], axis=1)
        own_mixer[r, shared : 2 * width] = pltpu.roll(keys, HEAD_DIM, 1)
        own_mixer[r, 2 * width + shared :] = pltpu.roll(eighth, HEAD_DIM, 1)[:, :HEAD_DIM]

    by_rows(fc.shape[0], 16, write)


def write_gradients(pairs, joint, fc):
    half, width = fc.shape
    members = pairs.shape[0] // half
    step = half // 2

    def block(*shape):
        return pl.BlockSpec(shape, lambda i: (0,) * (len(shape) - 2) + (i, 0))

    return pl.pallas_call(
        write_kernel,
        grid=(half // step,),
        in_specs=[block(members, step, 3 * PAIR), block(step, joint.shape[1]), block(step, width)],
        out_specs=[block(step, 3 * width), block(step, width), block(step, width)],
        out_shape=[
            jax.ShapeDtypeStruct((half, 3 * width), F32),
            jax.ShapeDtypeStruct((half, width), F32),
            jax.ShapeDtypeStruct((half, width), F32),
        ],
        compiler_params=pltpu.CompilerParams(vmem_limit_bytes=60 << 20),
        name="write_gradients",
    )(pairs.reshape(members, half, 3 * PAIR), joint, fc)


def tri(n):
    r=lax.broadcasted_iota(jnp.int32,(n,n),0); c=lax.broadcasted_iota(jnp.int32,(n,n),1)
    return c<=r

def branch_mask():
    r=lax.broadcasted_iota(jnp.int32,(BRANCH,BRANCH),0); c=lax.broadcasted_iota(jnp.int32,(BRANCH,BRANCH),1)
    return (c<=r)&((c<PIECE)|(c//PIECE==r//PIECE))

def split_heads(x):
    lane=lax.broadcasted_iota(jnp.int32,(1,2*64),1)<64
    z=jnp.zeros_like(x)
    return jnp.concatenate([jnp.where(lane,x,z),jnp.where(lane,z,x)],axis=0)

def join_heads(x):
    n=x.shape[0]//2
    lane=lax.broadcasted_iota(jnp.int32,(1,2*64),1)<64
    return jnp.where(lane,x[:n],x[n:])

def fwd_kernel(order, qkv, q16, qinfo, kinfo, att, att16, canon, of, lse, of16, lse16):
    n_p=qkv.shape[0]//PIECE
    for i in range(n_p):
        src=pl.ds(pl.multiple_of(order[i]*PIECE,PIECE),PIECE)
        canon[i*PIECE:(i+1)*PIECE,:]=qkv[src,0:384]
    def rows(start,size,parts):
        qh=split_heads(canon[pl.ds(start,size),0:128])
        ss=[]
        for ks,kn,mask in parts:
            s=contract(qh,canon[pl.ds(ks,kn),128:256],1,1)
            if mask is not None:
                m2=jnp.concatenate([mask,mask],axis=0)
                s=jnp.where(m2,s,NEGATIVE)
            ss.append(s)
        top=functools.reduce(jnp.maximum,[jnp.max(s,axis=1,keepdims=True) for s in ss])
        tot=0.; o=0.
        for (ks,kn,_),s in zip(parts,ss):
            e=jnp.exp(s-top)
            tot=tot+jnp.sum(e,axis=1,keepdims=True)
            o=o+contract(e.astype(BF16),canon[pl.ds(ks,kn),256:384],1,0)
        o=join_heads(o*(1.0/tot))
        of[pl.ds(start,size),:]=o
        l=top+jnp.log(tot)
        lse[pl.ds(start,size),:]=join_heads(jnp.broadcast_to(l,(2*size,128)))
    t=tri(256)
    for b in range(4):
        parts=[(b*256,256,t)]
        if b: parts.insert(0,(0,b*256,None))
        rows(b*256,256,parts)
    bm=branch_mask()
    def branch(b,_):
        st=pl.multiple_of(TRUNK+b*BRANCH,PIECE)
        rows(st,BRANCH,[(0,TRUNK,None),(st,BRANCH,bm)])
        return 0
    lax.fori_loop(0,4,branch,0)
    for i in range(n_p):
        dst=pl.ds(pl.multiple_of(order[i]*PIECE,PIECE),PIECE)
        att[dst,:]=of[i*PIECE:(i+1)*PIECE,:].astype(BF16)
    s=contract(q16[...],qkv[:,384:512],1,1)
    s=jnp.where(allowed_mask(qinfo,kinfo),s,NEGATIVE)
    top=jnp.max(s,axis=1,keepdims=True)
    e=jnp.exp(s-top)
    tot=jnp.sum(e,axis=1,keepdims=True)
    o=contract(e.astype(BF16),qkv[:,384:512],1,0)*(1.0/tot)
    of16[...]=o
    att16[...]=pltpu.roll(o,64,1).astype(BF16)
    lse16[...]=jnp.broadcast_to(top+jnp.log(tot),o.shape)

def allowed_mask(qinfo,kinfo):
    ks=kinfo[0:1,:]; kp=kinfo[1:2,:]
    return ((ks==qinfo[:,0:1])|(ks==qinfo[:,1:2])|(ks==qinfo[:,2:3]))&(kp<=qinfo[:,3:4])

def attention_forward(order,qkv,q16,qinfo,kinfo):
    n=qkv.shape[0]; r=q16.shape[0]
    sd=jax.ShapeDtypeStruct
    V=pl.BlockSpec(memory_space=pltpu.VMEM)
    return pl.pallas_call(fwd_kernel,
        in_specs=[pl.BlockSpec(memory_space=pltpu.SMEM)]+[V]*4,
        out_specs=[V]*7,
        out_shape=[sd((n,128),BF16),sd((r,128),BF16),sd((n,384),BF16),sd((n,128),F32),sd((n,128),F32),sd((r,128),F32),sd((r,128),F32)],
        compiler_params=pltpu.CompilerParams(vmem_limit_bytes=60<<20),
        cost_estimate=pl.CostEstimate(flops=20_000_000_000,bytes_accessed=8_000_000,transcendentals=7_000_000),
        name="tree_attention_forward",
    )(order,qkv,q16,qinfo,kinfo)

def bwd_kernel(order, canon, of, lse, datt, kv16, q16, of16, lse16, datt16, qinfo, kinfo, dqkv, dq16, dc, dacc):
    n_p=canon.shape[0]//PIECE
    for i in range(n_p):
        src=pl.ds(pl.multiple_of(order[i]*PIECE,PIECE),PIECE)
        dc[i*PIECE:(i+1)*PIECE,:]=datt[src,:]
    def rows(start,size,parts):
        r=pl.ds(start,size)
        qh=split_heads(canon[r,0:128])
        d=dc[r,:]
        dh=split_heads(d)
        prod=d.astype(F32)*of[r,:]
        delta=jnp.concatenate([jnp.sum(prod[:,0:64],axis=1,keepdims=True),jnp.sum(prod[:,64:128],axis=1,keepdims=True)],axis=0)
        l=jnp.concatenate([lse[r,0:1],lse[r,64:65]],axis=0)
        dq=0.
        for ks,kn,mask,first in parts:
            kk=canon[pl.ds(ks,kn),128:256]
            s=contract(qh,kk,1,1)
            if mask is not None:
                s=jnp.where(jnp.concatenate([mask,mask],axis=0),s,NEGATIVE)
            p=jnp.exp(s-l)
            dp=contract(dh,canon[pl.ds(ks,kn),256:384],1,1)
            ds=(p*(dp-delta)).astype(BF16)
            dv=contract(p.astype(BF16),dh,0,0)
            dk=contract(ds,qh,0,0)
            dq=dq+contract(ds,kk,1,0)
            if first:
                dacc[pl.ds(ks,kn),128:256]=dk
                dacc[pl.ds(ks,kn),256:384]=dv
            else:
                dacc[pl.ds(ks,kn),128:256]+=dk
                dacc[pl.ds(ks,kn),256:384]+=dv
        dacc[r,0:128]=join_heads(dq)
    t=tri(256)
    for b in range(4):
        parts=[(b*256,256,t,True)]
        if b: parts.insert(0,(0,b*256,None,False))
        rows(b*256,256,parts)
    bm=branch_mask()
    def branch(b,_):
        st=pl.multiple_of(TRUNK+b*BRANCH,PIECE)
        rows(st,BRANCH,[(0,TRUNK,None,False),(st,BRANCH,bm,True)])
        return 0
    lax.fori_loop(0,4,branch,0)
    for i in range(n_p):
        dst=pl.ds(pl.multiple_of(order[i]*PIECE,PIECE),PIECE)
        x=dacc[i*PIECE:(i+1)*PIECE,:]
        dqkv[dst,0:128]=(x[:,0:128]*0.125).astype(BF16)
        dqkv[dst,128:384]=x[:,128:384].astype(BF16)
    k16=kv16[:,384:512]
    s=contract(q16[...],k16,1,1)
    s=jnp.where(allowed_mask(qinfo,kinfo),s,NEGATIVE)
    p=jnp.exp(s-lse16[:,0:1])
    dp=contract(datt16[...],k16,1,1)
    delta=jnp.sum(datt16[...].astype(F32)*of16[...],axis=1,keepdims=True)
    ds=(p*(dp-delta)).astype(BF16)
    dqkv[:,384:512]=(contract(ds,q16[...],0,0)+contract(p.astype(BF16),datt16[...],0,0)).astype(BF16)
    lane=lax.broadcasted_iota(jnp.int32,(1,128),1)>=64
    dq=pltpu.roll(contract(ds,k16,1,0)*0.125,64,1)
    dq16[...]=jnp.where(lane,dq,0.0).astype(BF16)

def attention_backward(order,canon,of,lse,datt,qkv,q16,of16,lse16,datt16,qinfo,kinfo):
    n=canon.shape[0]; r=q16.shape[0]
    sd=jax.ShapeDtypeStruct
    V=pl.BlockSpec(memory_space=pltpu.VMEM)
    return pl.pallas_call(bwd_kernel,
        in_specs=[pl.BlockSpec(memory_space=pltpu.SMEM)]+[V]*11,
        out_specs=[V]*2,
        out_shape=[sd((n,512),BF16),sd((r,128),BF16)],
        scratch_shapes=[pltpu.VMEM((n,128),BF16),pltpu.VMEM((n,384),F32)],
        compiler_params=pltpu.CompilerParams(vmem_limit_bytes=60<<20),
        cost_estimate=pl.CostEstimate(flops=50_000_000_000,bytes_accessed=15_000_000,transcendentals=7_000_000),
        name="tree_attention_backward",
    )(order,canon,of,lse,datt,qkv,q16,of16,lse16,datt16,qinfo,kinfo)


def parent_lookup(identities, shifted_table):
    labels = jnp.arange(shifted_table.shape[0], dtype=jnp.int32)
    matches = identities[:, None] == labels[None, :]
    return jnp.sum(jnp.where(matches, shifted_table[None, :], 0), axis=1) - 1


def tree_order(segments, places, parent):
    own = segments.reshape(-1, PIECE)[:, 0]
    start = places.reshape(-1, PIECE)[:, 0]
    table = parent + 1
    first_up = parent_lookup(own, table)
    second_up = parent_lookup(first_up, table)
    is_branch = (first_up >= 0) & (second_up < 0)
    is_leaf = second_up >= 0
    branch = jnp.where(is_leaf, first_up, own)
    rank = jnp.sum((is_branch[None, :] & (own[None, :] < branch[:, None])).astype(jnp.int32), axis=1)
    twin = is_leaf[None, :] & (first_up[None, :] == first_up[:, None]) & (own[None, :] < own[:, None])
    leaf = 1 + jnp.sum(twin.astype(jnp.int32), axis=1)
    target = jnp.where(
        first_up < 0, start // PIECE, TRUNK // PIECE + 3 * rank + jnp.where(is_leaf, leaf, 0)
    )
    pieces = jnp.arange(own.shape[0], dtype=jnp.int32)
    order = jnp.sum(jnp.where(target[None, :] == pieces[:, None], pieces[None, :], 0), axis=1)
    return order, first_up, second_up


def local(
    tokens,
    cotangent,
    segment_of,
    position_of,
    parent,
    ln1_gain,
    ln1_bias,
    w_qkv,
    b_query,
    b_value,
    w_out,
    b_out,
    ln2_gain,
    ln2_bias,
    w_fc,
    b_fc,
    w_proj,
    b_proj,
):
    rows = tokens.shape[0]
    half = w_qkv.shape[0]
    shard = lax.axis_index("shard")
    tensor, context, me = place()
    members = 2 * lax.axis_size("tensor")
    tree_rows = members * rows
    low = shard == 0

    held = (ln1_gain, ln1_bias, b_query, b_value, b_out, ln2_gain, ln2_bias, b_proj)
    spare = -half % PIECE
    flat = jnp.concatenate([part for value in held for part in (value, jnp.zeros((spare,), BF16))])
    vectors = flat.reshape(len(held), half + spare)[:, :half].astype(F32)
    zeros = jnp.zeros_like(vectors)
    half_vectors = jnp.concatenate(
        [jnp.where(low, vectors, zeros), jnp.where(low, zeros, vectors)], axis=1
    )
    proj_mine = w_proj.T
    normed_all, mixed, query_last, vectors, weight, fc_other = project(tokens, w_qkv, half_vectors, w_fc)
    proj_give, cotangent_give, mixed = lax.optimization_barrier((proj_mine, cotangent, mixed))
    proj_other = swap(proj_give, "shard", 0)
    cotangent_far = swap(cotangent_give, "tensor", 1)

    tree_start = lax.div(context, 2) * tree_rows
    segments = lax.dynamic_slice_in_dim(segment_of, tree_start, tree_rows)
    places = lax.dynamic_slice_in_dim(position_of, tree_start, tree_rows)
    order, first_up, second_up = tree_order(segments, places, parent)
    key_info = jnp.stack([segments, places])
    query_info = jnp.stack(
        [segments, jnp.repeat(first_up, PIECE), jnp.repeat(second_up, PIECE), places], axis=1
    )
    query_info = lax.dynamic_slice_in_dim(query_info, me * rows, rows, 0)

    attended_pair, attended_last, sorted_qkv, exact, level, exact_last, level_last = attention_forward(
        order, mixed, query_last, query_info, key_info
    )
    residual, fed_give, d_middle, d_pair, d_last, joint_keep, joint_give, fc_keep, fc_give, proj_sum, sums = feed_forward(
        attended_pair,
        attended_last,
        tokens,
        cotangent,
        cotangent_far,
        w_out,
        w_fc,
        fc_other,
        proj_mine,
        proj_other,
        vectors,
        b_fc.astype(F32)[None, :],
    )

    fc_got = swap(fc_give, "shard", 0)
    joint_other = swap(joint_give, "tensor", 1)
    fed_other = swap(fed_give, "tensor", 1)
    proj_sum = lax.psum(proj_sum, "context")

    d_mixed, d_query_last = attention_backward(
        order, sorted_qkv, exact, level, d_pair, mixed, query_last, exact_last, level_last, d_last,
        query_info, key_info,
    )
    fc_got, joint_other, fed_other, d_mixed = lax.optimization_barrier(
        (fc_got, joint_other, fed_other, d_mixed)
    )
    fc_sum = (fc_keep.astype(F32) + fc_got.astype(F32)).astype(BF16)
    fc_sum = lax.psum(
        fc_sum, "context", axis_index_groups=[list(range(lax.axis_size("context")))[::-1]]
    )
    output, d_inputs, pairs, joint_all, sums = finish(
        d_mixed,
        d_query_last,
        normed_all,
        weight,
        tokens,
        d_middle,
        vectors,
        joint_keep,
        joint_other,
        sums,
        residual,
        fed_other,
    )
    proj_sum, fc_sum, sums = lax.optimization_barrier((proj_sum, fc_sum, sums))
    own_mixer, own_out, own_fc = write_gradients(pairs, joint_all, fc_sum)
    own_proj = proj_sum.T.astype(F32)
    mine = lax.dynamic_slice_in_dim(sums[:8], shard * half, half, 1)
    own_bias_fc = lax.dynamic_slice_in_dim(sums, 8 + tensor, 1, 0)[0]
    return (
        output,
        d_inputs,
        mine[0],
        mine[1],
        own_mixer,
        mine[2],
        mine[3],
        own_out,
        mine[4],
        mine[5],
        mine[6],
        own_fc,
        own_bias_fc,
        own_proj,
        mine[7],
    )


def solution(mesh):
    return jax.shard_map(
        local,
        mesh=mesh,
        in_specs=(
            P(("shard", "context", "tensor"), None),
            P(("shard", "context", "tensor"), None),
            P("shard"),
            P("shard"),
            P(),
            P("shard"),
            P("shard"),
            P("shard", None),
            P("shard"),
            P("shard"),
            P("shard", None),
            P("shard"),
            P("shard"),
            P("shard"),
            P("shard", "tensor"),
            P("tensor"),
            P("tensor", "shard"),
            P("shard"),
        ),
        out_specs=(
            P(("shard", "context", "tensor"), None),
            P(("shard", "context", "tensor"), None),
            P("shard"),
            P("shard"),
            P("shard", None),
            P("shard"),
            P("shard"),
            P("shard", None),
            P("shard"),
            P("shard"),
            P("shard"),
            P("shard", "tensor"),
            P("tensor"),
            P("tensor", "shard"),
            P("shard"),
        ),
        check_vma=False,
    )
```
